32 devices in a mesh: dp: 16 (over z, x, core), fsdp: 2 (over y).
Axes of the slice: x: 2, y: 2, z: 4, core: 2. Of those that a mesh axis runs over, the one named last changes fastest.
Arguments:
- picture_mean_embeddings: bfloat16 [640, 1152], P(('dp', 'fsdp')), may hold values from -0.1875 to 0.1875
- caption_tower_summary: bfloat16 [640, 1152], P(('dp', 'fsdp')), may hold values from -0.125 to 0.125
- caption_mapping_matrix: bfloat16 [1152, 1152], P('fsdp'), may hold values from -0.125 to 1
- picture_match_index: int32 [640], P('dp'), may hold values from 0 to 639, as said below
- sharpness_factor: float32 [1], replicated, may hold values from 40 to 56
- score_shift_term: float32 [1], replicated, may hold values from -11 to -10
Outputs:
- grad_image: float32 [640, 1152], P(('dp', 'fsdp'))
- grad_text: float32 [640, 1152], P(('dp', 'fsdp'))
- head_grad: float32 [1152, 1152], P('fsdp')
The draws below stay inside these ranges and needn't reach their ends.
Inputs may be any that keep to these rules, and one draw needn't show every extreme that they name: `picture_match_index`: every text is the pair of exactly one image.
All inputs are finite; a program needn't handle non-finite values.
Results may differ from the reference program's by a relative error of at most 0.0086.
Values may be sent and summed in bfloat16 or wider, within the bound.
No kernel may reach another device: no remote copies, remote signals or barrier semaphores. Data moves between devices by JAX's collectives and lax.ppermute only.
A program may use at most 64 MiB of HBM per device.

```python
import math
import jax
import jax.numpy as jnp
from jax import lax

D = 1152
E = 1152
ROWS = 20
B = 640
N_FSDP = 2


def pair_order(key):
    return jax.random.permutation(jax.random.fold_in(key, 71), B).astype(jnp.int32)


def text_base(key):
    values = 0.03 * jax.random.normal(jax.random.fold_in(key, 72), (B, D), jnp.float32)
    return jnp.clip(values, -0.125, 0.125)


def draw_picture_match_index(key, part):
    return pair_order(key)


def draw_caption_tower_summary(key, part):
    return text_base(key).astype(jnp.bfloat16)


def draw_picture_mean_embeddings(key, part):
    base = text_base(key)
    order = pair_order(key)
    key = jax.random.fold_in(key, 3)
    reach_key, noise_key = jax.random.split(key)
    reach = jnp.exp(jax.random.uniform(reach_key, (B, 1), jnp.float32, math.log(1.0), math.log(2.5)))
    noise = 0.03 * jax.random.normal(noise_key, (B, E), jnp.float32)
    paired = jnp.take(base, order, axis=0)
    image = reach * paired + noise
    return jnp.clip(image, -0.1875, 0.1875).astype(jnp.bfloat16)


def draw_caption_mapping_matrix(key, part):
    key = jax.random.fold_in(key, 5)
    noise = jnp.clip(0.03 * jax.random.normal(key, (D, E), jnp.float32), -0.125, 0.125)
    row_ids = lax.broadcasted_iota(jnp.int32, (D, E), 0)
    col_ids = lax.broadcasted_iota(jnp.int32, (D, E), 1)
    return jnp.where(row_ids == col_ids, 1.0, noise).astype(jnp.bfloat16)


def setup_inputs(seed: int = 0) -> dict:
    key_of = jax.random.split(jax.random.key(seed), 7)
    picture_mean_embeddings = draw_picture_mean_embeddings(jax.random.fold_in(key_of[6], 71), 0)
    caption_tower_summary = draw_caption_tower_summary(jax.random.fold_in(key_of[6], 71), 0)
    caption_mapping_matrix = draw_caption_mapping_matrix(jax.random.fold_in(key_of[6], 71), 0)
    picture_match_index = draw_picture_match_index(jax.random.fold_in(key_of[6], 71), 0)
    sharpness_factor = jnp.clip(jax.random.uniform(key_of[4], (1,), jnp.float32, 40.0, 56.0), 40.0, 56.0)
    score_shift_term = jnp.clip(jax.random.uniform(key_of[5], (1,), jnp.float32, -11.0, -10.0), -11.0, -10.0)
    return {"picture_mean_embeddings": picture_mean_embeddings, "caption_tower_summary": caption_tower_summary, "caption_mapping_matrix": caption_mapping_matrix, "picture_match_index": picture_match_index, "sharpness_factor": sharpness_factor, "score_shift_term": score_shift_term}


epsilon = 1e-06

def normalize(values):
    norms = jnp.sqrt(lax.optimization_barrier(jnp.sum(values * values, axis=1, keepdims=True)) + epsilon)
    return (values / norms, norms)

def unproject(grad_unit, unit, norms):
    return (grad_unit - unit * lax.optimization_barrier(jnp.sum(unit * grad_unit, axis=1, keepdims=True))) / norms

def reference(picture_mean_embeddings, caption_tower_summary, caption_mapping_matrix, picture_match_index, sharpness_factor, score_shift_term):
    unit_image, image_norm = normalize(picture_mean_embeddings.astype(jnp.float32))
    image_unit = unit_image.astype(jnp.bfloat16)
    projected = jnp.dot(caption_tower_summary, caption_mapping_matrix, preferred_element_type=jnp.float32)
    unit_text, text_norm = normalize(projected)
    text_unit = unit_text.astype(jnp.bfloat16)
    score_multiplier = sharpness_factor[0]
    offset = score_shift_term[0]
    total = image_unit.shape[0]
    block = ROWS * N_FSDP
    text_rows = jnp.arange(total, dtype=jnp.int32)

    def visit(carried, number):
        start = (number * block).astype(jnp.int32)
        image_block = lax.dynamic_slice_in_dim(image_unit, start, block, 0)
        pair_block = lax.dynamic_slice_in_dim(picture_match_index, start, block, 0)
        scores = lax.dot_general(image_block, text_unit, (((1,), (1,)), ((), ())), preferred_element_type=jnp.float32)
        logits = score_multiplier * scores + offset
        sign = jnp.where(pair_block[:, None] == text_rows[None, :], 1.0, -1.0).astype(jnp.float32)
        weights = (score_multiplier * -sign * jax.nn.sigmoid(-sign * logits)).astype(jnp.bfloat16)
        image_part = jnp.dot(weights, text_unit, preferred_element_type=jnp.float32)
        text_part = lax.dot_general(weights, image_block, (((0,), (0,)), ((), ())), preferred_element_type=jnp.float32)
        return (carried + text_part, image_part)
    start_sum = jnp.zeros((total, text_unit.shape[1]), jnp.float32)
    grad_zt, image_parts = lax.scan(visit, start_sum, jnp.arange(total // block, dtype=jnp.int32))
    grad_zi = image_parts.reshape(total, text_unit.shape[1])
    grad_image = unproject(grad_zi, unit_image, image_norm)
    grad_proj = unproject(grad_zt, unit_text, text_norm).astype(jnp.bfloat16)
    grad_text = lax.dot_general(grad_proj, caption_mapping_matrix, (((1,), (1,)), ((), ())), preferred_element_type=jnp.float32)
    head_grad = lax.dot_general(caption_tower_summary, grad_proj, (((0,), (0,)), ((), ())), preferred_element_type=jnp.float32)
    return (grad_image, grad_text, head_grad)
```

```python
import jax
import jax.numpy as jnp
from jax import lax
from jax.sharding import PartitionSpec as P

epsilon = 1e-06


def passed_along(block, axis, distance):
    devices = range(lax.axis_size(axis))
    route = [((i - distance) % len(devices), i) for i in devices]
    return lax.ppermute(block, axis, route)


def normalize(values):
    norms = jnp.sqrt(jnp.sum(values * values, axis=1, keepdims=True) + epsilon)
    return (values / norms, norms)


def unproject(grad_unit, unit, norms):
    return (grad_unit - unit * jnp.sum(unit * grad_unit, axis=1, keepdims=True)) / norms


def ring_plan(
    picture_mean_embeddings,
    caption_tower_summary,
    caption_mapping_matrix,
    picture_match_index,
    sharpness_factor,
    score_shift_term,
):
    rows = caption_tower_summary.shape[0]
    width = caption_mapping_matrix.shape[1]
    cycle_size = lax.axis_size("dp")
    column_count = lax.axis_size("fsdp")
    cycle_index = lax.axis_index("dp")
    column_index = lax.axis_index("fsdp")
    score_multiplier = sharpness_factor[0]
    offset = score_shift_term[0]
    feature_column_set = lax.all_to_all(
        caption_tower_summary, "fsdp", split_axis=1, concat_axis=0, tiled=True
    )
    projected = jnp.dot(
        caption_tower_summary,
        lax.all_gather(caption_mapping_matrix, "fsdp", axis=0, tiled=True),
        preferred_element_type=jnp.float32,
    )
    unit_text, text_norm = normalize(projected)
    text_unit = unit_text.astype(jnp.bfloat16)
    unit_image, image_norm = normalize(picture_mean_embeddings.astype(jnp.float32))
    image_unit = lax.all_gather(unit_image.astype(jnp.bfloat16), "fsdp", axis=0, tiled=True)
    group = image_unit.shape[0]

    def tile(block, text_rows):
        scores = lax.dot_general(
            image_unit, block, (((1,), (1,)), ((), ())), preferred_element_type=jnp.float32
        )
        logits = score_multiplier * scores + offset
        sign = jnp.where(picture_match_index[:, None] == text_rows[None, :], 1.0, -1.0).astype(
            jnp.float32
        )
        weights = (score_multiplier * -sign * jax.nn.sigmoid(-sign * logits)).astype(jnp.bfloat16)
        image_part = jnp.dot(weights, block, preferred_element_type=jnp.float32)
        text_part = lax.dot_general(
            weights, image_unit, (((0,), (0,)), ((), ())), preferred_element_type=jnp.float32
        )
        return (image_part, text_part)

    def rows_of(owner, count):
        return (owner * column_count + column_index) * rows + jnp.arange(count, dtype=jnp.int32)

    image_start = jnp.zeros((group, width), jnp.float32)

    def advance(count, state):
        block, carried, image_sum = state
        owner = (cycle_index - count) % cycle_size
        image_part, text_part = tile(block, rows_of(owner, rows))
        block = passed_along(block, "dp", 1)
        carried = passed_along(carried + text_part, "dp", 1)
        return (block, carried, image_sum + image_part)

    state = (text_unit, jnp.zeros((rows, width), jnp.float32), image_start)
    block, grad_zt, image_sum = lax.fori_loop(0, cycle_size, advance, state)
    grad_zi = lax.psum_scatter(image_sum, "fsdp", scatter_dimension=0, tiled=True)
    grad_image = unproject(grad_zi, unit_image, image_norm)
    grad_proj = unproject(grad_zt, unit_text, text_norm).astype(jnp.bfloat16)
    grad_group = lax.all_gather(grad_proj, "fsdp", axis=0, tiled=True)
    head_part = lax.dot_general(
        feature_column_set, grad_group, (((0,), (0,)), ((), ())), preferred_element_type=jnp.float32
    )
    head_grad = lax.psum(head_part, "dp")
    grad_text = lax.dot_general(
        grad_proj,
        lax.all_gather(caption_mapping_matrix, "fsdp", axis=0, tiled=True),
        (((1,), (1,)), ((), ())),
        preferred_element_type=jnp.float32,
    )
    return (grad_image, grad_text, head_grad)


def gathered_plan(
    picture_mean_embeddings,
    caption_tower_summary,
    caption_mapping_matrix,
    picture_match_index,
    sharpness_factor,
    score_shift_term,
):
    rows = caption_tower_summary.shape[0]
    depth = caption_mapping_matrix.shape[0]
    index = lax.axis_index("dp") * lax.axis_size("fsdp") + lax.axis_index("fsdp")
    multiplier = sharpness_factor[0]
    offset = score_shift_term[0]
    pairs = jnp.stack([picture_mean_embeddings, caption_tower_summary])
    pairs = lax.all_gather(pairs, ("dp", "fsdp"), axis=1, tiled=True)
    images, texts = pairs[0], pairs[1]
    matrix = lax.all_gather(caption_mapping_matrix, "fsdp", axis=0, tiled=True)
    match = lax.all_gather(picture_match_index, "dp", axis=0, tiled=True)
    total = images.shape[0]

    unit_image, image_norm = normalize(images.astype(jnp.float32))
    zi = unit_image.astype(jnp.bfloat16)
    projected = jnp.dot(texts, matrix, preferred_element_type=jnp.float32)
    unit_text, text_norm = normalize(projected)
    zt = unit_text.astype(jnp.bfloat16)
    scores = lax.dot_general(zi, zt, (((1,), (1,)), ((), ())), preferred_element_type=jnp.float32)
    logits = multiplier * scores + offset
    paired = match[:, None] == jnp.arange(total, dtype=jnp.int32)[None, :]
    sign = jnp.where(paired, 1.0, -1.0).astype(jnp.float32)
    weights = (multiplier * -sign * jax.nn.sigmoid(-sign * logits)).astype(jnp.bfloat16)
    grad_zt = lax.dot_general(
        weights, zi, (((0,), (0,)), ((), ())), preferred_element_type=jnp.float32
    )
    grad_proj = unproject(grad_zt, unit_text, text_norm).astype(jnp.bfloat16)

    def own(array):
        return lax.dynamic_slice_in_dim(array, index * rows, rows, 0)

    grad_zi = jnp.dot(own(weights), zt, preferred_element_type=jnp.float32)
    grad_image = unproject(grad_zi, own(unit_image), own(image_norm))
    grad_text = lax.dot_general(
        own(grad_proj), matrix, (((1,), (1,)), ((), ())), preferred_element_type=jnp.float32
    )
    columns = lax.dynamic_slice_in_dim(texts, lax.axis_index("fsdp") * depth, depth, 1)
    head_grad = lax.dot_general(
        columns, grad_proj, (((0,), (0,)), ((), ())), preferred_element_type=jnp.float32
    )
    return (grad_image, grad_text, head_grad)


GATHERED_ROWS = 1024


def solution(mesh):
    devices = mesh.shape["dp"] * mesh.shape["fsdp"]

    def per_device(*arguments):
        whole = arguments[0].shape[0] * devices
        plan = gathered_plan if whole <= GATHERED_ROWS else ring_plan
        return plan(*arguments)

    return jax.shard_map(
        per_device,
        mesh=mesh,
        in_specs=(
            P(("dp", "fsdp"), None),
            P(("dp", "fsdp"), None),
            P("fsdp", None),
            P("dp"),
            P(),
            P(),
        ),
        out_specs=(P(("dp", "fsdp"), None), P(("dp", "fsdp"), None), P("fsdp", None)),
        check_vma=False,
    )
```

```python
import jax
import jax.numpy as jnp
from jax import lax
from jax.sharding import PartitionSpec as P

epsilon = 1e-06


def passed_along(block, axis, distance):
    devices = range(lax.axis_size(axis))
    route = [((i - distance) % len(devices), i) for i in devices]
    return lax.ppermute(block, axis, route)


def normalize(values):
    norms = jnp.sqrt(jnp.sum(values * values, axis=1, keepdims=True) + epsilon)
    return (values / norms, norms)


def unproject(grad_unit, unit, norms):
    return (grad_unit - unit * jnp.sum(unit * grad_unit, axis=1, keepdims=True)) / norms


def ring_plan(
    picture_mean_embeddings,
    caption_tower_summary,
    caption_mapping_matrix,
    picture_match_index,
    sharpness_factor,
    score_shift_term,
):
    rows = caption_tower_summary.shape[0]
    width = caption_mapping_matrix.shape[1]
    cycle_size = lax.axis_size("dp")
    column_count = lax.axis_size("fsdp")
    cycle_index = lax.axis_index("dp")
    column_index = lax.axis_index("fsdp")
    score_multiplier = sharpness_factor[0]
    offset = score_shift_term[0]
    feature_column_set = lax.all_to_all(
        caption_tower_summary, "fsdp", split_axis=1, concat_axis=0, tiled=True
    )
    projected = jnp.dot(
        caption_tower_summary,
        lax.all_gather(caption_mapping_matrix, "fsdp", axis=0, tiled=True),
        preferred_element_type=jnp.float32,
    )
    unit_text, text_norm = normalize(projected)
    text_unit = unit_text.astype(jnp.bfloat16)
    unit_image, image_norm = normalize(picture_mean_embeddings.astype(jnp.float32))
    image_unit = lax.all_gather(unit_image.astype(jnp.bfloat16), "fsdp", axis=0, tiled=True)
    group = image_unit.shape[0]

    def tile(block, text_rows):
        scores = lax.dot_general(
            image_unit, block, (((1,), (1,)), ((), ())), preferred_element_type=jnp.float32
        )
        logits = score_multiplier * scores + offset
        sign = jnp.where(picture_match_index[:, None] == text_rows[None, :], 1.0, -1.0).astype(
            jnp.float32
        )
        weights = (score_multiplier * -sign * jax.nn.sigmoid(-sign * logits)).astype(jnp.bfloat16)
        image_part = jnp.dot(weights, block, preferred_element_type=jnp.float32)
        text_part = lax.dot_general(
            weights, image_unit, (((0,), (0,)), ((), ())), preferred_element_type=jnp.float32
        )
        return (image_part, text_part)

    def rows_of(owner, count):
        return (owner * column_count + column_index) * rows + jnp.arange(count, dtype=jnp.int32)

    image_start = jnp.zeros((group, width), jnp.float32)

    def advance(count, state):
        block, carried, image_sum = state
        owner = (cycle_index - count) % cycle_size
        image_part, text_part = tile(block, rows_of(owner, rows))
        block = passed_along(block, "dp", 1)
        carried = passed_along(carried + text_part, "dp", 1)
        return (block, carried, image_sum + image_part)

    state = (text_unit, jnp.zeros((rows, width), jnp.float32), image_start)
    block, grad_zt, image_sum = lax.fori_loop(0, cycle_size, advance, state)
    grad_zi = lax.psum_scatter(image_sum, "fsdp", scatter_dimension=0, tiled=True)
    grad_image = unproject(grad_zi, unit_image, image_norm)
    grad_proj = unproject(grad_zt, unit_text, text_norm).astype(jnp.bfloat16)
    grad_group = lax.all_gather(grad_proj, "fsdp", axis=0, tiled=True)
    head_part = lax.dot_general(
        feature_column_set, grad_group, (((0,), (0,)), ((), ())), preferred_element_type=jnp.float32
    )
    head_grad = lax.psum(head_part, "dp")
    grad_text = lax.dot_general(
        grad_proj,
        lax.all_gather(caption_mapping_matrix, "fsdp", axis=0, tiled=True),
        (((1,), (1,)), ((), ())),
        preferred_element_type=jnp.float32,
    )
    return (grad_image, grad_text, head_grad)


def across(block, bits):
    count = lax.axis_size("dp") * lax.axis_size("fsdp")
    return lax.ppermute(block, ("dp", "fsdp"), [(i, i ^ bits) for i in range(count)])


Y, CORE, X, Z1, Z2 = 1, 2, 4, 8, 16


def gathered_plan(
    picture_mean_embeddings,
    caption_tower_summary,
    caption_mapping_matrix,
    picture_match_index,
    sharpness_factor,
    score_shift_term,
):
    rows, width = caption_tower_summary.shape
    depth = caption_mapping_matrix.shape[0]
    half = depth // 2
    group = lax.axis_index("dp")
    side = lax.axis_index("fsdp")
    place = group * 2 + side
    core = group % 2
    multiplier = sharpness_factor[0]
    offset = score_shift_term[0]

    own = jnp.stack([picture_mean_embeddings, caption_tower_summary])[None]
    along_z = [own] + [across(own, bits) for bits in (Z1, Z2, Z1 | Z2)]
    quarter = lax.dynamic_slice_in_dim(caption_mapping_matrix, core * half, half, 0)
    quarter = across(quarter, Y)
    other_quarter = across(quarter, CORE)
    column = jnp.concatenate(along_z)
    beside = across(column, X)
    plane = jnp.concatenate([column, beside])
    behind = across(plane, Y)
    mine = jnp.concatenate([plane, behind])
    pairs = jnp.concatenate([mine, across(mine, CORE)])
    order = [bits for bits in (0, Z1, Z2, Z1 | Z2)]
    order += [bits | X for bits in order]
    order += [bits | Y for bits in order]
    order += [bits | CORE for bits in order]
    owners = jnp.array(order, jnp.int32) ^ place
    text_ids = (owners[:, None] * rows + jnp.arange(rows, dtype=jnp.int32)).reshape(-1)

    lower = jnp.where(core == 0, quarter, other_quarter)
    upper = jnp.where(core == 0, other_quarter, quarter)
    other = jnp.concatenate([lower, upper])
    match = lax.all_gather(picture_match_index, "dp", axis=0, tiled=True)
    match = match.reshape(-1, rows)[owners].reshape(-1)
    images = pairs[:, 0].reshape(-1, width)
    texts = pairs[:, 1].reshape(-1, width)

    unit_image, image_norm = normalize(images.astype(jnp.float32))
    zi = unit_image.astype(jnp.bfloat16)
    own_columns = lax.dynamic_slice_in_dim(texts, side * depth, depth, 1)
    other_columns = lax.dynamic_slice_in_dim(texts, (1 - side) * depth, depth, 1)
    projected = jnp.dot(own_columns, caption_mapping_matrix, preferred_element_type=jnp.float32)
    projected += jnp.dot(other_columns, other, preferred_element_type=jnp.float32)
    unit_text, text_norm = normalize(projected)
    zt = unit_text.astype(jnp.bfloat16)
    scores = lax.dot_general(zi, zt, (((1,), (1,)), ((), ())), preferred_element_type=jnp.float32)
    logits = multiplier * scores + offset
    paired = match[:, None] == text_ids[None, :]
    sign = jnp.where(paired, 1.0, -1.0).astype(jnp.float32)
    weights = (multiplier * -sign * jax.nn.sigmoid(-sign * logits)).astype(jnp.bfloat16)
    grad_zt = lax.dot_general(
        weights, zi, (((0,), (0,)), ((), ())), preferred_element_type=jnp.float32
    )
    grad_proj = unproject(grad_zt, unit_text, text_norm).astype(jnp.bfloat16)
    grad_zi = jnp.dot(weights[:rows], zt, preferred_element_type=jnp.float32)
    grad_image = unproject(grad_zi, unit_image[:rows], image_norm[:rows])
    contract = (((1,), (1,)), ((), ()))
    mine = lax.dot_general(
        grad_proj[:rows], caption_mapping_matrix, contract, preferred_element_type=jnp.float32
    )
    rest = lax.dot_general(grad_proj[:rows], other, contract, preferred_element_type=jnp.float32)
    left = jnp.where(side == 0, mine, rest)
    grad_text = jnp.concatenate([left, jnp.where(side == 0, rest, mine)], axis=1)
    head_grad = lax.dot_general(
        own_columns, grad_proj, (((0,), (0,)), ((), ())), preferred_element_type=jnp.float32
    )
    return (grad_image, grad_text, head_grad)


def solution(mesh):
    gathered = dict(mesh.shape) == {"dp": 16, "fsdp": 2}
    per_device = gathered_plan if gathered else ring_plan
    return jax.shard_map(
        per_device,
        mesh=mesh,
        in_specs=(
            P(("dp", "fsdp"), None),
            P(("dp", "fsdp"), None),
            P("fsdp", None),
            P("dp"),
            P(),
            P(),
        ),
        out_specs=(P(("dp", "fsdp"), None), P(("dp", "fsdp"), None), P("fsdp", None)),
        check_vma=False,
    )
```

```python
import jax
import jax.numpy as jnp
from jax import lax
from jax.experimental import pallas as pl
from jax.experimental.pallas import tpu as pltpu
from jax.sharding import PartitionSpec as P

epsilon = 1e-06


def passed_along(block, axis, distance):
    devices = range(lax.axis_size(axis))
    route = [((i - distance) % len(devices), i) for i in devices]
    return lax.ppermute(block, axis, route)


def normalize(values):
    norms = jnp.sqrt(jnp.sum(values * values, axis=1, keepdims=True) + epsilon)
    return (values / norms, norms)


def unproject(grad_unit, unit, norms):
    return (grad_unit - unit * jnp.sum(unit * grad_unit, axis=1, keepdims=True)) / norms


def ring_plan(
    picture_mean_embeddings,
    caption_tower_summary,
    caption_mapping_matrix,
    picture_match_index,
    sharpness_factor,
    score_shift_term,
):
    rows = caption_tower_summary.shape[0]
    width = caption_mapping_matrix.shape[1]
    cycle_size = lax.axis_size("dp")
    column_count = lax.axis_size("fsdp")
    cycle_index = lax.axis_index("dp")
    column_index = lax.axis_index("fsdp")
    score_multiplier = sharpness_factor[0]
    offset = score_shift_term[0]
    feature_column_set = lax.all_to_all(
        caption_tower_summary, "fsdp", split_axis=1, concat_axis=0, tiled=True
    )
    projected = jnp.dot(
        caption_tower_summary,
        lax.all_gather(caption_mapping_matrix, "fsdp", axis=0, tiled=True),
        preferred_element_type=jnp.float32,
    )
    unit_text, text_norm = normalize(projected)
    text_unit = unit_text.astype(jnp.bfloat16)
    unit_image, image_norm = normalize(picture_mean_embeddings.astype(jnp.float32))
    image_unit = lax.all_gather(unit_image.astype(jnp.bfloat16), "fsdp", axis=0, tiled=True)
    group = image_unit.shape[0]

    def tile(block, text_rows):
        scores = lax.dot_general(
            image_unit, block, (((1,), (1,)), ((), ())), preferred_element_type=jnp.float32
        )
        logits = score_multiplier * scores + offset
        sign = jnp.where(picture_match_index[:, None] == text_rows[None, :], 1.0, -1.0).astype(
            jnp.float32
        )
        weights = (score_multiplier * -sign * jax.nn.sigmoid(-sign * logits)).astype(jnp.bfloat16)
        image_part = jnp.dot(weights, block, preferred_element_type=jnp.float32)
        text_part = lax.dot_general(
            weights, image_unit, (((0,), (0,)), ((), ())), preferred_element_type=jnp.float32
        )
        return (image_part, text_part)

    def rows_of(owner, count):
        return (owner * column_count + column_index) * rows + jnp.arange(count, dtype=jnp.int32)

    image_start = jnp.zeros((group, width), jnp.float32)

    def advance(count, state):
        block, carried, image_sum = state
        owner = (cycle_index - count) % cycle_size
        image_part, text_part = tile(block, rows_of(owner, rows))
        block = passed_along(block, "dp", 1)
        carried = passed_along(carried + text_part, "dp", 1)
        return (block, carried, image_sum + image_part)

    state = (text_unit, jnp.zeros((rows, width), jnp.float32), image_start)
    block, grad_zt, image_sum = lax.fori_loop(0, cycle_size, advance, state)
    grad_zi = lax.psum_scatter(image_sum, "fsdp", scatter_dimension=0, tiled=True)
    grad_image = unproject(grad_zi, unit_image, image_norm)
    grad_proj = unproject(grad_zt, unit_text, text_norm).astype(jnp.bfloat16)
    grad_group = lax.all_gather(grad_proj, "fsdp", axis=0, tiled=True)
    head_part = lax.dot_general(
        feature_column_set, grad_group, (((0,), (0,)), ((), ())), preferred_element_type=jnp.float32
    )
    head_grad = lax.psum(head_part, "dp")
    grad_text = lax.dot_general(
        grad_proj,
        lax.all_gather(caption_mapping_matrix, "fsdp", axis=0, tiled=True),
        (((1,), (1,)), ((), ())),
        preferred_element_type=jnp.float32,
    )
    return (grad_image, grad_text, head_grad)


def across(block, bits):
    count = lax.axis_size("dp") * lax.axis_size("fsdp")
    return lax.ppermute(block, ("dp", "fsdp"), [(i, i ^ bits) for i in range(count)])


Y, CORE, X, Z1, Z2 = 1, 2, 4, 8, 16
NT = (((1,), (1,)), ((), ()))
TN = (((0,), (0,)), ((), ()))


def dot(a, b, dims=(((1,), (0,)), ((), ()))):
    return lax.dot_general(a, b, dims, preferred_element_type=jnp.float32)


def batch_kernel(
    scalars,
    image,
    text_column,
    text_row,
    match_column,
    match_row,
    matrix_own,
    matrix_near,
    matrix_far,
    *rest,
):
    pieces, rest = rest[:16], rest[16:]
    grad_image, grad_text, head_grad, zi, text, zt, unit, norm, proj, matrix, sems = rest
    rows = image.shape[0]
    total = zi.shape[0]
    depth, near = matrix_own.shape[0], matrix_near.shape[0]
    core = lax.rem(lax.axis_index("dp"), 2)
    side = lax.axis_index("fsdp")
    multiplier, offset = scalars[0], scalars[1]

    other = (1 - side) * depth
    places = (side * depth, other + core * near, other + (1 - core) * near)
    copies = []
    for k, (source, place) in enumerate(zip((matrix_own, matrix_near, matrix_far), places)):
        place = pl.multiple_of(place, 32)
        target = matrix.at[pl.ds(place, source.shape[0])]
        copies.append(pltpu.make_async_copy(source, target, sems.at[k]))
        copies[-1].start()

    for k in range(0, 16, 2):
        pair = 2 * pieces[k].shape[1]
        for kind, target in ((0, zi), (1, text)):
            both = [pieces[k + j][kind].astype(jnp.float32) for j in (0, 1)]
            target[pl.ds(k // 2 * pair, pair)] = jnp.concatenate(both).astype(jnp.bfloat16)
    for copy in copies:
        copy.wait()

    step = total // 4

    def project(k, carry):
        block = pl.ds(pl.multiple_of(k * step, 32), step)
        projected = dot(text[block], matrix[...])
        length = jnp.sqrt(jnp.sum(projected * projected, axis=1, keepdims=True) + epsilon)
        value = projected / length
        unit[block] = value
        norm[block] = length
        zt[block] = value.astype(jnp.bfloat16)
        return carry

    lax.fori_loop(0, 4, project, 0)

    def weigh(scores, paired):
        logits = multiplier * scores + offset
        sign = jnp.where(paired, 1.0, -1.0)
        return (multiplier * -sign * jax.nn.sigmoid(-sign * logits)).astype(jnp.bfloat16)

    def text_gradient(k, carry):
        block = pl.ds(pl.multiple_of(k * step, 32), step)
        scores = dot(zt[block], zi[...], NT)
        weights = weigh(scores, text_column[block] == match_row[...])
        grad = dot(weights, zi[...])
        proj[block] = unproject(grad, unit[block], norm[block]).astype(jnp.bfloat16)
        return carry

    lax.fori_loop(0, 4, text_gradient, 0)

    for s in (0, 1):

        @pl.when(side == s)
        def _():
            head_grad[...] = dot(text[:, s * depth : (s + 1) * depth], proj[...], TN)

    two = match_column.shape[0]
    scores = dot(zi[:two], zt[...], NT)
    weights = weigh(scores, match_column[...] == text_row[...])
    grad_zi = dot(weights, zt[...])[:rows]
    unit_image, image_norm = normalize(image[...].astype(jnp.float32))
    grad_image[...] = unproject(grad_zi, unit_image, image_norm)
    grad_text[...] = dot(proj[:two], matrix[...], NT)[:rows]


def gathered_plan(
    picture_mean_embeddings,
    caption_tower_summary,
    caption_mapping_matrix,
    picture_match_index,
    sharpness_factor,
    score_shift_term,
):
    rows, width = caption_tower_summary.shape
    depth = caption_mapping_matrix.shape[0]
    half = depth // 2
    group = lax.axis_index("dp")
    side = lax.axis_index("fsdp")
    place = group * 2 + side
    total = rows * 32

    unit_image, _ = normalize(picture_mean_embeddings.astype(jnp.float32))
    own = jnp.stack([unit_image.astype(jnp.bfloat16), caption_tower_summary])
    own = jnp.concatenate([own, across(own, Y)], axis=1)

    match = [picture_match_index] + [
        across(picture_match_index, bits) for bits in (Z1, Z2, Z1 | Z2)
    ]
    match = jnp.concatenate(match)
    match = jnp.concatenate([match, across(match, X)])
    match = jnp.concatenate([match, across(match, CORE)]).reshape(16, 2, rows)
    match = jnp.where(side == 0, match, match[:, ::-1]).reshape(total)
    order = [0, Z1, Z2, Z1 | Z2]
    order += [bits | X for bits in order]
    order += [bits | CORE for bits in order]
    owners = jnp.array([bits | y for bits in order for y in (0, Y)], jnp.int32) ^ place
    text_ids = (owners[:, None] * rows + jnp.arange(rows, dtype=jnp.int32)).reshape(total)

    quarter = lax.dynamic_slice_in_dim(caption_mapping_matrix, (group % 2) * half, half, 0)
    near = across(quarter, Y)
    far = across(near, CORE)
    pieces = [own] + [across(own, bits) for bits in (Z1, Z2, Z1 | Z2)]
    pieces += [across(piece, X) for piece in pieces]
    pieces += [across(piece, CORE) for piece in pieces]

    scalars = jnp.concatenate([sharpness_factor, score_shift_term])
    vmem = pl.BlockSpec(memory_space=pltpu.VMEM)
    anywhere = pl.BlockSpec(memory_space=pl.ANY)
    f32, bf16 = jnp.float32, jnp.bfloat16
    return pl.pallas_call(
        batch_kernel,
        out_shape=(
            jax.ShapeDtypeStruct((rows, width), f32),
            jax.ShapeDtypeStruct((rows, width), f32),
            jax.ShapeDtypeStruct((depth, width), f32),
        ),
        in_specs=[pl.BlockSpec(memory_space=pltpu.SMEM)]
        + [vmem] * 5
        + [anywhere] * 3
        + [vmem] * 16,
        out_specs=(vmem, vmem, vmem),
        scratch_shapes=[
            pltpu.VMEM((total, width), bf16),
            pltpu.VMEM((total, width), bf16),
            pltpu.VMEM((total, width), bf16),
            pltpu.VMEM((total, width), f32),
            pltpu.VMEM((total, 1), f32),
            pltpu.VMEM((total, width), bf16),
            pltpu.VMEM((2 * depth, width), bf16),
            pltpu.SemaphoreType.DMA((3,)),
        ],
        compiler_params=pltpu.CompilerParams(vmem_limit_bytes=48 * 2**20),
        name="batch_gradients",
    )(
        scalars,
        picture_mean_embeddings,
        text_ids[:, None],
        text_ids[None, :],
        match[: 2 * rows, None],
        match[None, :],
        caption_mapping_matrix,
        near,
        far,
        *pieces,
    )


def solution(mesh):
    gathered = dict(mesh.shape) == {"dp": 16, "fsdp": 2}
    per_device = gathered_plan if gathered else ring_plan
    return jax.shard_map(
        per_device,
        mesh=mesh,
        in_specs=(
            P(("dp", "fsdp"), None),
            P(("dp", "fsdp"), None),
            P("fsdp", None),
            P("dp"),
            P(),
            P(),
        ),
        out_specs=(P(("dp", "fsdp"), None), P(("dp", "fsdp"), None), P("fsdp", None)),
        check_vma=False,
    )
```

```python
import functools

import jax
import jax.numpy as jnp
from jax import lax
from jax.experimental import pallas as pl
from jax.experimental.pallas import tpu as pltpu
from jax.sharding import PartitionSpec as P

epsilon = 1e-06


def passed_along(block, axis, distance):
    devices = range(lax.axis_size(axis))
    route = [((i - distance) % len(devices), i) for i in devices]
    return lax.ppermute(block, axis, route)


def normalize(values):
    norms = jnp.sqrt(jnp.sum(values * values, axis=1, keepdims=True) + epsilon)
    return (values / norms, norms)


def unproject(grad_unit, unit, norms):
    return (grad_unit - unit * jnp.sum(unit * grad_unit, axis=1, keepdims=True)) / norms


def ring_plan(
    picture_mean_embeddings,
    caption_tower_summary,
    caption_mapping_matrix,
    picture_match_index,
    sharpness_factor,
    score_shift_term,
):
    rows = caption_tower_summary.shape[0]
    width = caption_mapping_matrix.shape[1]
    cycle_size = lax.axis_size("dp")
    column_count = lax.axis_size("fsdp")
    cycle_index = lax.axis_index("dp")
    column_index = lax.axis_index("fsdp")
    score_multiplier = sharpness_factor[0]
    offset = score_shift_term[0]
    feature_column_set = lax.all_to_all(
        caption_tower_summary, "fsdp", split_axis=1, concat_axis=0, tiled=True
    )
    projected = jnp.dot(
        caption_tower_summary,
        lax.all_gather(caption_mapping_matrix, "fsdp", axis=0, tiled=True),
        preferred_element_type=jnp.float32,
    )
    unit_text, text_norm = normalize(projected)
    text_unit = unit_text.astype(jnp.bfloat16)
    unit_image, image_norm = normalize(picture_mean_embeddings.astype(jnp.float32))
    image_unit = lax.all_gather(unit_image.astype(jnp.bfloat16), "fsdp", axis=0, tiled=True)
    group = image_unit.shape[0]

    def tile(block, text_rows):
        scores = lax.dot_general(
            image_unit, block, (((1,), (1,)), ((), ())), preferred_element_type=jnp.float32
        )
        logits = score_multiplier * scores + offset
        sign = jnp.where(picture_match_index[:, None] == text_rows[None, :], 1.0, -1.0).astype(
            jnp.float32
        )
        weights = (score_multiplier * -sign * jax.nn.sigmoid(-sign * logits)).astype(jnp.bfloat16)
        image_part = jnp.dot(weights, block, preferred_element_type=jnp.float32)
        text_part = lax.dot_general(
            weights, image_unit, (((0,), (0,)), ((), ())), preferred_element_type=jnp.float32
        )
        return (image_part, text_part)

    def rows_of(owner, count):
        return (owner * column_count + column_index) * rows + jnp.arange(count, dtype=jnp.int32)

    image_start = jnp.zeros((group, width), jnp.float32)

    def advance(count, state):
        block, carried, image_sum = state
        owner = (cycle_index - count) % cycle_size
        image_part, text_part = tile(block, rows_of(owner, rows))
        block = passed_along(block, "dp", 1)
        carried = passed_along(carried + text_part, "dp", 1)
        return (block, carried, image_sum + image_part)

    state = (text_unit, jnp.zeros((rows, width), jnp.float32), image_start)
    block, grad_zt, image_sum = lax.fori_loop(0, cycle_size, advance, state)
    grad_zi = lax.psum_scatter(image_sum, "fsdp", scatter_dimension=0, tiled=True)
    grad_image = unproject(grad_zi, unit_image, image_norm)
    grad_proj = unproject(grad_zt, unit_text, text_norm).astype(jnp.bfloat16)
    grad_group = lax.all_gather(grad_proj, "fsdp", axis=0, tiled=True)
    head_part = lax.dot_general(
        feature_column_set, grad_group, (((0,), (0,)), ((), ())), preferred_element_type=jnp.float32
    )
    head_grad = lax.psum(head_part, "dp")
    grad_text = lax.dot_general(
        grad_proj,
        lax.all_gather(caption_mapping_matrix, "fsdp", axis=0, tiled=True),
        (((1,), (1,)), ((), ())),
        preferred_element_type=jnp.float32,
    )
    return (grad_image, grad_text, head_grad)


def across(block, bits):
    count = lax.axis_size("dp") * lax.axis_size("fsdp")
    return lax.ppermute(block, ("dp", "fsdp"), [(i, i ^ bits) for i in range(count)])


Y, CORE, X, Z1, Z2 = 1, 2, 4, 8, 16
NT = (((1,), (1,)), ((), ()))
TN = (((0,), (0,)), ((), ()))


def dot(a, b, dims=(((1,), (0,)), ((), ()))):
    return lax.dot_general(a, b, dims, preferred_element_type=jnp.float32)


def cuts(size, step):
    return [slice(k, min(k + step, size)) for k in range(0, size, step)]


def batch_kernel(groups, scalars, image, text_ids, match_column, match_row, *rest):
    (matrix_own, matrix_near, matrix_far), rest = rest[:3], rest[3:]
    pieces = []
    for ref, count in zip(rest, groups):
        pieces += [ref.at[k] for k in range(count)] if count else [ref]
    rest = rest[len(groups) :]
    grad_image, grad_text, head_grad, rest = *rest[:3], rest[3:]
    zi, text, zt, projected, weights, grad, proj, turned, matrix, head, sems = rest
    rows = image.shape[0]
    total, width = zi.shape
    depth, near = matrix_own.shape[0], matrix_near.shape[0]
    core = lax.rem(lax.axis_index("dp"), 2)
    side = lax.axis_index("fsdp")
    multiplier, offset = scalars[0], scalars[1]
    columns = cuts(width, 256)

    other = (1 - side) * depth
    places = (side * depth, other + core * near, other + (1 - core) * near)
    copies = []
    for k, (source, place) in enumerate(zip((matrix_own, matrix_near, matrix_far), places)):
        place = pl.multiple_of(place, 32)
        target = matrix.at[pl.ds(place, source.shape[0])]
        copies.append(pltpu.make_async_copy(source, target, sems.at[k]))
        copies[-1].start()

    for kind, target in ((1, text), (0, zi)):
        for k in range(0, 16, 2):
            pair = 2 * pieces[k].shape[1]
            both = [pieces[k + j][kind].astype(jnp.float32) for j in (0, 1)]
            target[pl.ds(k // 2 * pair, pair)] = jnp.concatenate(both).astype(jnp.bfloat16)
    for s in (0, 1):

        @pl.when(side == s)
        def _():
            turned[...] = jnp.transpose(text[:, s * depth : (s + 1) * depth])

    for copy in copies:
        copy.wait()

    for cut in columns:
        projected[:, cut] = dot(text[...], matrix[:, cut])
    step = 128
    for block in cuts(total, step):
        value = projected[block]
        inverse = lax.rsqrt(jnp.sum(value * value, axis=1, keepdims=True) + epsilon)
        zt[block] = (value * inverse).astype(jnp.bfloat16)

    def weigh(scores, paired):
        logits = multiplier * scores + offset
        sign = jnp.where(paired, 1.0, -1.0)
        return (multiplier * -sign * jax.nn.sigmoid(-sign * logits)).astype(jnp.bfloat16)

    for cut in cuts(total, 256):
        scores = dot(zt[...], zi[cut], NT)
        weights[:, cut] = weigh(scores, text_ids[...] == match_row[:, cut])
    for cut in columns:
        grad[:, cut] = dot(weights[...], zi[:, cut])
    for block in cuts(total, step):
        value, slope = projected[block], grad[block]
        squares = jnp.sum(value * value, axis=1, keepdims=True) + epsilon
        inner = jnp.sum(value * slope, axis=1, keepdims=True)
        proj[block] = ((slope - value * (inner / squares)) * lax.rsqrt(squares)).astype(
            jnp.bfloat16
        )
    copies = []
    for k, cut in enumerate(columns):
        head[:, cut] = dot(turned[...], proj[:, cut])
        copies.append(pltpu.make_async_copy(head.at[:, cut], head_grad.at[:, cut], sems.at[k]))
        copies[-1].start()

    some = match_column.shape[0]
    scores = dot(zi[:some], zt[...], NT)
    text_row = jnp.transpose(text_ids[...].astype(jnp.float32)).astype(jnp.int32)
    own_weights = weigh(scores, match_column[...] == text_row)
    unit_image, image_norm = normalize(image[...].astype(jnp.float32))
    grad_image[...] = unproject(dot(own_weights, zt[...])[:rows], unit_image, image_norm)
    grad_text[...] = dot(proj[:some], matrix[...], NT)[:rows]
    for copy in copies:
        copy.wait()


def gathered_plan(
    picture_mean_embeddings,
    caption_tower_summary,
    caption_mapping_matrix,
    picture_match_index,
    sharpness_factor,
    score_shift_term,
):
    rows, width = caption_tower_summary.shape
    depth = caption_mapping_matrix.shape[0]
    half = depth // 2
    group = lax.axis_index("dp")
    side = lax.axis_index("fsdp")
    place = group * 2 + side
    total = rows * 32

    match = jnp.broadcast_to(picture_match_index, (16, 2 * rows))
    match = lax.all_to_all(match, "dp", split_axis=0, concat_axis=0, tiled=True)

    unit_image, _ = normalize(picture_mean_embeddings.astype(jnp.float32))
    own = jnp.stack([unit_image.astype(jnp.bfloat16), caption_tower_summary])
    beside = across(own, Y)
    own, beside, match = lax.optimization_barrier((own, beside, match))
    own = jnp.concatenate([own, beside], axis=1)
    along_z = (0, Z1, Z2, Z1 | Z2)
    p0, p1, p2, p3 = [own] + [across(own, bits) for bits in along_z[1:]]
    x0, x1, x2, x3 = [across(piece, X) for piece in (p0, p1, p2, p3)]
    matrix, _ = lax.optimization_barrier((caption_mapping_matrix, beside))
    quarter = lax.dynamic_slice_in_dim(matrix, (group % 2) * half, half, 0)
    near = across(quarter, Y)
    far = across(near, CORE)
    first = across(jnp.stack([p0, x0]), CORE)
    second = across(jnp.stack([p1, x1]), CORE)
    third = across(jnp.stack([p2, p3, x2]), CORE)
    last = across(x3, CORE)
    pieces = [p0, x0, p1, x1, p2, p3, x2, x3, first, second, third, last]
    groups = [0] * 8 + [2, 2, 3, 0]
    order = [0, X, Z1, X | Z1, Z2, Z1 | Z2, X | Z2, X | Z1 | Z2]
    order += [bits | CORE for bits in order]

    owners = jnp.array([bits | y for bits in order for y in (0, Y)], jnp.int32) ^ place
    text_ids = (owners[:, None] * rows + jnp.arange(rows, dtype=jnp.int32)).reshape(total)
    match = match.reshape(32, rows)[owners].reshape(total)

    scalars = jnp.concatenate([sharpness_factor, score_shift_term])
    vmem = pl.BlockSpec(memory_space=pltpu.VMEM)
    anywhere = pl.BlockSpec(memory_space=pl.ANY)
    f32, bf16 = jnp.float32, jnp.bfloat16
    return pl.pallas_call(
        functools.partial(batch_kernel, groups),
        out_shape=(
            jax.ShapeDtypeStruct((rows, width), f32),
            jax.ShapeDtypeStruct((rows, width), f32),
            jax.ShapeDtypeStruct((depth, width), f32),
        ),
        in_specs=[pl.BlockSpec(memory_space=pltpu.SMEM)]
        + [vmem] * 4
        + [anywhere] * 3
        + [vmem] * len(pieces),
        out_specs=(vmem, vmem, anywhere),
        scratch_shapes=[
            pltpu.VMEM((total, width), bf16),
            pltpu.VMEM((total, width), bf16),
            pltpu.VMEM((total, width), bf16),
            pltpu.VMEM((total, width), f32),
            pltpu.VMEM((total, total), bf16),
            pltpu.VMEM((total, width), f32),
            pltpu.VMEM((total, width), bf16),
            pltpu.VMEM((depth, total), bf16),
            pltpu.VMEM((2 * depth, width), bf16),
            pltpu.VMEM((depth, width), f32),
            pltpu.SemaphoreType.DMA((8,)),
        ],
        compiler_params=pltpu.CompilerParams(vmem_limit_bytes=40 * 2**20),
        name="batch_gradients",
    )(
        scalars,
        picture_mean_embeddings,
        text_ids[:, None],
        match[:48, None],
        match[None, :],
        caption_mapping_matrix,
        near,
        far,
        *pieces,
    )


def solution(mesh):
    gathered = dict(mesh.shape) == {"dp": 16, "fsdp": 2}
    per_device = gathered_plan if gathered else ring_plan
    return jax.shard_map(
        per_device,
        mesh=mesh,
        in_specs=(
            P(("dp", "fsdp"), None),
            P(("dp", "fsdp"), None),
            P("fsdp", None),
            P("dp"),
            P(),
            P(),
        ),
        out_specs=(P(("dp", "fsdp"), None), P(("dp", "fsdp"), None), P("fsdp", None)),
        check_vma=False,
    )
```

```python
import functools

import jax
import jax.numpy as jnp
from jax import lax
from jax.experimental import pallas as pl
from jax.experimental.pallas import tpu as pltpu
from jax.sharding import PartitionSpec as P

epsilon = 1e-06


def passed_along(block, axis, distance):
    devices = range(lax.axis_size(axis))
    route = [((i - distance) % len(devices), i) for i in devices]
    return lax.ppermute(block, axis, route)


def normalize(values):
    norms = jnp.sqrt(jnp.sum(values * values, axis=1, keepdims=True) + epsilon)
    return (values / norms, norms)


def unproject(grad_unit, unit, norms):
    return (grad_unit - unit * jnp.sum(unit * grad_unit, axis=1, keepdims=True)) / norms


def ring_plan(
    picture_mean_embeddings,
    caption_tower_summary,
    caption_mapping_matrix,
    picture_match_index,
    sharpness_factor,
    score_shift_term,
):
    rows = caption_tower_summary.shape[0]
    width = caption_mapping_matrix.shape[1]
    cycle_size = lax.axis_size("dp")
    column_count = lax.axis_size("fsdp")
    cycle_index = lax.axis_index("dp")
    column_index = lax.axis_index("fsdp")
    score_multiplier = sharpness_factor[0]
    offset = score_shift_term[0]
    feature_column_set = lax.all_to_all(
        caption_tower_summary, "fsdp", split_axis=1, concat_axis=0, tiled=True
    )
    projected = jnp.dot(
        caption_tower_summary,
        lax.all_gather(caption_mapping_matrix, "fsdp", axis=0, tiled=True),
        preferred_element_type=jnp.float32,
    )
    unit_text, text_norm = normalize(projected)
    text_unit = unit_text.astype(jnp.bfloat16)
    unit_image, image_norm = normalize(picture_mean_embeddings.astype(jnp.float32))
    image_unit = lax.all_gather(unit_image.astype(jnp.bfloat16), "fsdp", axis=0, tiled=True)
    group = image_unit.shape[0]

    def tile(block, text_rows):
        scores = lax.dot_general(
            image_unit, block, (((1,), (1,)), ((), ())), preferred_element_type=jnp.float32
        )
        logits = score_multiplier * scores + offset
        sign = jnp.where(picture_match_index[:, None] == text_rows[None, :], 1.0, -1.0).astype(
            jnp.float32
        )
        weights = (score_multiplier * -sign * jax.nn.sigmoid(-sign * logits)).astype(jnp.bfloat16)
        image_part = jnp.dot(weights, block, preferred_element_type=jnp.float32)
        text_part = lax.dot_general(
            weights, image_unit, (((0,), (0,)), ((), ())), preferred_element_type=jnp.float32
        )
        return (image_part, text_part)

    def rows_of(owner, count):
        return (owner * column_count + column_index) * rows + jnp.arange(count, dtype=jnp.int32)

    image_start = jnp.zeros((group, width), jnp.float32)

    def advance(count, state):
        block, carried, image_sum = state
        owner = (cycle_index - count) % cycle_size
        image_part, text_part = tile(block, rows_of(owner, rows))
        block = passed_along(block, "dp", 1)
        carried = passed_along(carried + text_part, "dp", 1)
        return (block, carried, image_sum + image_part)

    state = (text_unit, jnp.zeros((rows, width), jnp.float32), image_start)
    block, grad_zt, image_sum = lax.fori_loop(0, cycle_size, advance, state)
    grad_zi = lax.psum_scatter(image_sum, "fsdp", scatter_dimension=0, tiled=True)
    grad_image = unproject(grad_zi, unit_image, image_norm)
    grad_proj = unproject(grad_zt, unit_text, text_norm).astype(jnp.bfloat16)
    grad_group = lax.all_gather(grad_proj, "fsdp", axis=0, tiled=True)
    head_part = lax.dot_general(
        feature_column_set, grad_group, (((0,), (0,)), ((), ())), preferred_element_type=jnp.float32
    )
    head_grad = lax.psum(head_part, "dp")
    grad_text = lax.dot_general(
        grad_proj,
        lax.all_gather(caption_mapping_matrix, "fsdp", axis=0, tiled=True),
        (((1,), (1,)), ((), ())),
        preferred_element_type=jnp.float32,
    )
    return (grad_image, grad_text, head_grad)


def across(block, bits):
    count = lax.axis_size("dp") * lax.axis_size("fsdp")
    return lax.ppermute(block, ("dp", "fsdp"), [(i, i ^ bits) for i in range(count)])


Y, CORE, X, Z1, Z2 = 1, 2, 4, 8, 16
IMAGE_ORDER = (Y, X, Z2, Z1, CORE)
TEXT_ORDER = (Y, Z2, Z1, X, CORE)
NT = (((1,), (1,)), ((), ()))
TN = (((0,), (0,)), ((), ()))


def dot(a, b, dims=(((1,), (0,)), ((), ()))):
    return lax.dot_general(a, b, dims, preferred_element_type=jnp.float32)


def cuts(size, step):
    return [slice(k, min(k + step, size)) for k in range(0, size, step)]


def batch_kernel(sharpness, shift, image, match, *rest):
    (matrix_own, matrix_near, matrix_far), images, texts, rest = (
        rest[:3],
        rest[3:7],
        rest[7:11],
        rest[11:],
    )
    (grad_image, grad_text, head_grad), rest = rest[:3], rest[3:]
    zi, text, zt, projected, weights, grad, turned, matrix, sems = rest
    proj, head = text, grad
    rows = image.shape[0]
    total, width = zi.shape
    depth, near = matrix_own.shape[0], matrix_near.shape[0]
    group, side = lax.axis_index("dp"), lax.axis_index("fsdp")
    core = lax.rem(group, 2)
    place = group * 2 + side
    multiplier, offset = sharpness[0], shift[0]
    columns = cuts(width, 256)

    other = (1 - side) * depth
    places = (side * depth, other + core * near, other + (1 - core) * near)
    copies = []
    for k, (source, start) in enumerate(zip((matrix_own, matrix_near, matrix_far), places)):
        start = pl.multiple_of(start, 32)
        target = matrix.at[pl.ds(start, source.shape[0])]
        copies.append(pltpu.make_async_copy(source, target, sems.at[k]))
        copies[-1].start()

    for sources, target in ((texts, text), (images, zi)):
        count = total // len(sources)
        for k, source in enumerate(sources):
            target[pl.ds(k * count, count)] = source[...]
    for s in (0, 1):

        @pl.when(side == s)
        def _():
            turned[...] = jnp.transpose(text[:, s * depth : (s + 1) * depth])

    for copy in copies:
        copy.wait()

    for cut in columns:
        projected[:, cut] = dot(text[...], matrix[:, cut])
    step = 128
    for block in cuts(total, step):
        value = projected[block]
        inverse = lax.rsqrt(jnp.sum(value * value, axis=1, keepdims=True) + epsilon)
        zt[block] = (value * inverse).astype(jnp.bfloat16)

    def text_ids(shape, axis):
        row = lax.broadcasted_iota(jnp.int32, shape, axis)
        block = sum((row >= k * rows).astype(jnp.int32) for k in range(1, total // rows))
        owner = jnp.zeros_like(row)
        for k, bits in enumerate(TEXT_ORDER):
            owner += ((block >> k) & 1) * bits
        return (owner ^ place) * rows + row - block * rows

    def weigh(scores, paired):
        logits = multiplier * scores + offset
        sign = jnp.where(paired, 1.0, -1.0)
        return (multiplier * -sign * jax.nn.sigmoid(-sign * logits)).astype(jnp.bfloat16)

    ids = text_ids((total, 1), 0)
    for cut in cuts(total, 256):
        scores = dot(zt[...], zi[cut], NT)
        weights[:, cut] = weigh(scores, ids == match[:, cut])
    for cut in columns:
        grad[:, cut] = dot(weights[...], zi[:, cut])
    for block in cuts(total, step):
        value, slope = projected[block], grad[block]
        squares = jnp.sum(value * value, axis=1, keepdims=True) + epsilon
        inner = jnp.sum(value * slope, axis=1, keepdims=True)
        proj[block] = ((slope - value * (inner / squares)) * lax.rsqrt(squares)).astype(
            jnp.bfloat16
        )
    copies = []
    for k, cut in enumerate(columns):
        head[:depth, cut] = dot(turned[...], proj[:, cut])
        copies.append(
            pltpu.make_async_copy(head.at[:depth, cut], head_grad.at[:, cut], sems.at[k])
        )
        copies[-1].start()

    some = 48
    scores = dot(zi[:some], zt[...], NT)
    own_match = jnp.transpose(match[:, :128].astype(jnp.float32)).astype(jnp.int32)[:some]
    own_weights = weigh(scores, own_match == text_ids((1, total), 1))
    unit_image, image_norm = normalize(image[...].astype(jnp.float32))
    grad_image[...] = unproject(dot(own_weights, zt[...])[:rows], unit_image, image_norm)
    grad_text[...] = dot(proj[:some], matrix[...], NT)[:rows]
    for copy in copies:
        copy.wait()


def gathered_plan(
    picture_mean_embeddings,
    caption_tower_summary,
    caption_mapping_matrix,
    picture_match_index,
    sharpness_factor,
    score_shift_term,
):
    rows, width = caption_tower_summary.shape
    depth = caption_mapping_matrix.shape[0]
    half = depth // 2
    core = lax.axis_index("dp") % 2
    side = lax.axis_index("fsdp")
    total = rows * 32

    match = jnp.where(side == 0, picture_match_index, jnp.roll(picture_match_index, rows))
    for bits in IMAGE_ORDER[1:]:
        match = jnp.concatenate([match, across(match, bits)])

    unit_image, _ = normalize(picture_mean_embeddings.astype(jnp.float32))
    images = unit_image.astype(jnp.bfloat16)
    texts = caption_tower_summary
    beside = across(jnp.stack([images, texts]), Y)
    images = jnp.concatenate([images, beside[0]])
    texts = jnp.concatenate([texts, beside[1]])
    matrix, _ = lax.optimization_barrier((caption_mapping_matrix, beside))
    quarter = lax.dynamic_slice_in_dim(matrix, core * half, half, 0)
    near = across(quarter, Y)
    far = across(near, CORE)
    gathered = []
    for block, order in ((images, IMAGE_ORDER), (texts, TEXT_ORDER)):
        for bits in order[1:3]:
            block = jnp.concatenate([block, across(block, bits)])
        late = across(block, order[3])
        gathered += [block, late, across(block, order[4]), across(late, order[4])]

    smem = pl.BlockSpec(memory_space=pltpu.SMEM)
    vmem = pl.BlockSpec(memory_space=pltpu.VMEM)
    anywhere = pl.BlockSpec(memory_space=pl.ANY)
    f32, bf16 = jnp.float32, jnp.bfloat16
    return pl.pallas_call(
        batch_kernel,
        out_shape=(
            jax.ShapeDtypeStruct((rows, width), f32),
            jax.ShapeDtypeStruct((rows, width), f32),
            jax.ShapeDtypeStruct((depth, width), f32),
        ),
        in_specs=[smem] * 2 + [vmem] * 2 + [anywhere] * 3 + [vmem] * 8,
        out_specs=(vmem, vmem, anywhere),
        scratch_shapes=[
            pltpu.VMEM((total, width), bf16),
            pltpu.VMEM((total, width), bf16),
            pltpu.VMEM((total, width), bf16),
            pltpu.VMEM((total, width), f32),
            pltpu.VMEM((total, total), bf16),
            pltpu.VMEM((total, width), f32),
            pltpu.VMEM((depth, total), bf16),
            pltpu.VMEM((2 * depth, width), bf16),
            pltpu.SemaphoreType.DMA((8,)),
        ],
        compiler_params=pltpu.CompilerParams(vmem_limit_bytes=24 * 2**20),
        name="batch_gradients",
    )(
        sharpness_factor,
        score_shift_term,
        picture_mean_embeddings,
        match[None, :],
        caption_mapping_matrix,
        near,
        far,
        *gathered,
    )


def solution(mesh):
    gathered = dict(mesh.shape) == {"dp": 16, "fsdp": 2}
    per_device = gathered_plan if gathered else ring_plan
    return jax.shard_map(
        per_device,
        mesh=mesh,
        in_specs=(
            P(("dp", "fsdp"), None),
            P(("dp", "fsdp"), None),
            P("fsdp", None),
            P("dp"),
            P(),
            P(),
        ),
        out_specs=(P(("dp", "fsdp"), None), P(("dp", "fsdp"), None), P("fsdp", None)),
        check_vma=False,
    )
```

```python
import functools

import jax
import jax.numpy as jnp
from jax import lax
from jax.experimental import pallas as pl
from jax.experimental.pallas import tpu as pltpu
from jax.sharding import PartitionSpec as P

epsilon = 1e-06


def passed_along(block, axis, distance):
    devices = range(lax.axis_size(axis))
    route = [((i - distance) % len(devices), i) for i in devices]
    return lax.ppermute(block, axis, route)


def normalize(values):
    norms = jnp.sqrt(jnp.sum(values * values, axis=1, keepdims=True) + epsilon)
    return (values / norms, norms)


def unproject(grad_unit, unit, norms):
    return (grad_unit - unit * jnp.sum(unit * grad_unit, axis=1, keepdims=True)) / norms


def ring_plan(
    picture_mean_embeddings,
    caption_tower_summary,
    caption_mapping_matrix,
    picture_match_index,
    sharpness_factor,
    score_shift_term,
):
    rows = caption_tower_summary.shape[0]
    width = caption_mapping_matrix.shape[1]
    cycle_size = lax.axis_size("dp")
    column_count = lax.axis_size("fsdp")
    cycle_index = lax.axis_index("dp")
    column_index = lax.axis_index("fsdp")
    score_multiplier = sharpness_factor[0]
    offset = score_shift_term[0]
    feature_column_set = lax.all_to_all(
        caption_tower_summary, "fsdp", split_axis=1, concat_axis=0, tiled=True
    )
    projected = jnp.dot(
        caption_tower_summary,
        lax.all_gather(caption_mapping_matrix, "fsdp", axis=0, tiled=True),
        preferred_element_type=jnp.float32,
    )
    unit_text, text_norm = normalize(projected)
    text_unit = unit_text.astype(jnp.bfloat16)
    unit_image, image_norm = normalize(picture_mean_embeddings.astype(jnp.float32))
    image_unit = lax.all_gather(unit_image.astype(jnp.bfloat16), "fsdp", axis=0, tiled=True)
    group = image_unit.shape[0]

    def tile(block, text_rows):
        scores = lax.dot_general(
            image_unit, block, (((1,), (1,)), ((), ())), preferred_element_type=jnp.float32
        )
        logits = score_multiplier * scores + offset
        sign = jnp.where(picture_match_index[:, None] == text_rows[None, :], 1.0, -1.0).astype(
            jnp.float32
        )
        weights = (score_multiplier * -sign * jax.nn.sigmoid(-sign * logits)).astype(jnp.bfloat16)
        image_part = jnp.dot(weights, block, preferred_element_type=jnp.float32)
        text_part = lax.dot_general(
            weights, image_unit, (((0,), (0,)), ((), ())), preferred_element_type=jnp.float32
        )
        return (image_part, text_part)

    def rows_of(owner, count):
        return (owner * column_count + column_index) * rows + jnp.arange(count, dtype=jnp.int32)

    image_start = jnp.zeros((group, width), jnp.float32)

    def advance(count, state):
        block, carried, image_sum = state
        owner = (cycle_index - count) % cycle_size
        image_part, text_part = tile(block, rows_of(owner, rows))
        block = passed_along(block, "dp", 1)
        carried = passed_along(carried + text_part, "dp", 1)
        return (block, carried, image_sum + image_part)

    state = (text_unit, jnp.zeros((rows, width), jnp.float32), image_start)
    block, grad_zt, image_sum = lax.fori_loop(0, cycle_size, advance, state)
    grad_zi = lax.psum_scatter(image_sum, "fsdp", scatter_dimension=0, tiled=True)
    grad_image = unproject(grad_zi, unit_image, image_norm)
    grad_proj = unproject(grad_zt, unit_text, text_norm).astype(jnp.bfloat16)
    grad_group = lax.all_gather(grad_proj, "fsdp", axis=0, tiled=True)
    head_part = lax.dot_general(
        feature_column_set, grad_group, (((0,), (0,)), ((), ())), preferred_element_type=jnp.float32
    )
    head_grad = lax.psum(head_part, "dp")
    grad_text = lax.dot_general(
        grad_proj,
        lax.all_gather(caption_mapping_matrix, "fsdp", axis=0, tiled=True),
        (((1,), (1,)), ((), ())),
        preferred_element_type=jnp.float32,
    )
    return (grad_image, grad_text, head_grad)


def across(block, bits):
    count = lax.axis_size("dp") * lax.axis_size("fsdp")
    return lax.ppermute(block, ("dp", "fsdp"), [(i, i ^ bits) for i in range(count)])


Y, CORE, X, Z1, Z2 = 1, 2, 4, 8, 16
IMAGE_ORDER = (Y, X, Z2, Z1, CORE)
TEXT_ORDER = (Y, Z2, Z1, X, CORE)
NT = (((1,), (1,)), ((), ()))
TN = (((0,), (0,)), ((), ()))


def dot(a, b, dims=(((1,), (0,)), ((), ()))):
    return lax.dot_general(a, b, dims, preferred_element_type=jnp.float32)


def cuts(size, step):
    return [slice(k, min(k + step, size)) for k in range(0, size, step)]


def text_ids(shape, axis, rows, place):
    row = lax.broadcasted_iota(jnp.int32, shape, axis)
    block = sum((row >= k * rows).astype(jnp.int32) for k in range(1, shape[axis] // rows))
    owner = jnp.zeros_like(row)
    for k, bits in enumerate(TEXT_ORDER):
        owner += ((block >> k) & 1) * bits
    return (owner ^ place) * rows + row - block * rows


def weigh(scores, paired, sharpness, shift):
    logits = sharpness[0] * scores + shift[0]
    sign = jnp.where(paired, 1.0, -1.0)
    return (sharpness[0] * -sign * jax.nn.sigmoid(-sign * logits)).astype(jnp.bfloat16)


def text_kernel(sharpness, shift, image, images, match, *rest):
    (matrix_own, matrix_near, matrix_far), texts, rest = rest[:3], rest[3:7], rest[7:]
    zt, projected, turned, matrix, grad_image, text, sems = rest
    rows = image.shape[0]
    total, width = text.shape
    depth, near = matrix_own.shape[0], matrix_near.shape[0]
    group, side = lax.axis_index("dp"), lax.axis_index("fsdp")
    core = lax.rem(group, 2)

    other = (1 - side) * depth
    places = (side * depth, other + core * near, other + (1 - core) * near)
    copies = []
    for k, (source, start) in enumerate(zip((matrix_own, matrix_near, matrix_far), places)):
        start = pl.multiple_of(start, 32)
        target = matrix.at[pl.ds(start, source.shape[0])]
        copies.append(pltpu.make_async_copy(source, target, sems.at[k]))
        copies[-1].start()
    count = total // len(texts)
    for k, source in enumerate(texts):
        text[pl.ds(k * count, count)] = source[...]
    for s in (0, 1):

        @pl.when(side == s)
        def _():
            turned[...] = jnp.transpose(text[:, s * depth : (s + 1) * depth])

    for copy in copies:
        copy.wait()

    for cut in cuts(width, 256):
        projected[:, cut] = dot(text[...], matrix[:, cut])
    for block in cuts(total, 128):
        value = projected[block]
        inverse = lax.rsqrt(jnp.sum(value * value, axis=1, keepdims=True) + epsilon)
        zt[block] = (value * inverse).astype(jnp.bfloat16)

    scores = dot(images[...], zt[...], NT)
    ids = text_ids((1, total), 1, rows, group * 2 + side)
    weights = weigh(scores, match[...] == ids, sharpness, shift)
    unit_image, image_norm = normalize(image[...].astype(jnp.float32))
    grad_image[...] = unproject(dot(weights, zt[...])[:rows], unit_image, image_norm)


def pair_kernel(rows, sharpness, shift, match, zt, projected, turned, matrix, *rest):
    images, rest = rest[:4], rest[4:]
    grad_text, head_grad, zi, weights, grad, proj, head, sems = rest
    total, width = zi.shape
    place = lax.axis_index("dp") * 2 + lax.axis_index("fsdp")
    count = total // len(images)
    for k, source in enumerate(images):
        zi[pl.ds(k * count, count)] = source[...]

    ids = text_ids((total, 1), 0, rows, place)
    for cut in cuts(total, 256):
        scores = dot(zt[...], zi[cut], NT)
        weights[:, cut] = weigh(scores, ids == match[:, cut], sharpness, shift)
    for cut in cuts(width, 256):
        grad[:, cut] = dot(weights[...], zi[:, cut])
    for block in cuts(total, 128):
        value, slope = projected[block], grad[block]
        squares = jnp.sum(value * value, axis=1, keepdims=True) + epsilon
        inner = jnp.sum(value * slope, axis=1, keepdims=True)
        proj[block] = ((slope - value * (inner / squares)) * lax.rsqrt(squares)).astype(
            jnp.bfloat16
        )
    copies = []
    for k, cut in enumerate(cuts(width, 256)):
        head[:, cut] = dot(turned[...], proj[:, cut])
        copies.append(pltpu.make_async_copy(head.at[:, cut], head_grad.at[:, cut], sems.at[k]))
        copies[-1].start()
    grad_text[...] = dot(proj[:48], matrix[...], NT)[:rows]
    for copy in copies:
        copy.wait()


def gathered_plan(
    picture_mean_embeddings,
    caption_tower_summary,
    caption_mapping_matrix,
    picture_match_index,
    sharpness_factor,
    score_shift_term,
):
    rows, width = caption_tower_summary.shape
    depth = caption_mapping_matrix.shape[0]
    half = depth // 2
    core = lax.axis_index("dp") % 2
    side = lax.axis_index("fsdp")
    total = rows * 32
    smem = pl.BlockSpec(memory_space=pltpu.SMEM)
    vmem = pl.BlockSpec(memory_space=pltpu.VMEM)
    anywhere = pl.BlockSpec(memory_space=pl.ANY)
    f32, bf16 = jnp.float32, jnp.bfloat16

    def doubled(block, bits):
        return jnp.concatenate([block, across(block, bits)])

    texts = doubled(caption_tower_summary, TEXT_ORDER[0])
    quarter = lax.dynamic_slice_in_dim(caption_mapping_matrix, core * half, half, 0)
    quarter, _ = lax.optimization_barrier((quarter, texts))
    near = across(quarter, Y)
    far = across(near, CORE)
    for bits in TEXT_ORDER[1:3]:
        texts = doubled(texts, bits)
    late = across(texts, TEXT_ORDER[3])
    texts = [texts, late, across(texts, CORE), across(late, CORE)]

    unit_image, _ = normalize(picture_mean_embeddings.astype(f32))
    own_images = doubled(unit_image.astype(bf16), IMAGE_ORDER[0])
    own_match = jnp.where(side == 0, picture_match_index, jnp.roll(picture_match_index, rows))
    images, match = own_images, own_match
    for bits in IMAGE_ORDER[1:3]:
        match = doubled(match, bits)
        images, match = lax.optimization_barrier((images, match))
        images = doubled(images, bits)
    match = doubled(match, IMAGE_ORDER[3])
    images, match = lax.optimization_barrier((images, match))
    late = across(images, IMAGE_ORDER[3])
    match = doubled(match, CORE)
    images = [images, late, across(images, CORE), across(late, CORE)]

    zt, projected, turned, matrix, grad_image = pl.pallas_call(
        text_kernel,
        out_shape=(
            jax.ShapeDtypeStruct((total, width), bf16),
            jax.ShapeDtypeStruct((total, width), f32),
            jax.ShapeDtypeStruct((depth, total), bf16),
            jax.ShapeDtypeStruct((2 * depth, width), bf16),
            jax.ShapeDtypeStruct((rows, width), f32),
        ),
        in_specs=[smem] * 2 + [vmem] * 3 + [anywhere] * 3 + [vmem] * 4,
        out_specs=(vmem,) * 5,
        scratch_shapes=[pltpu.VMEM((total, width), bf16), pltpu.SemaphoreType.DMA((3,))],
        compiler_params=pltpu.CompilerParams(vmem_limit_bytes=24 * 2**20),
        name="texts",
    )(
        sharpness_factor,
        score_shift_term,
        picture_mean_embeddings,
        own_images,
        own_match[:, None],
        caption_mapping_matrix,
        near,
        far,
        *texts,
    )
    grad_text, head_grad = pl.pallas_call(
        functools.partial(pair_kernel, rows),
        out_shape=(
            jax.ShapeDtypeStruct((rows, width), f32),
            jax.ShapeDtypeStruct((depth, width), f32),
        ),
        in_specs=[smem] * 2 + [vmem] * 9,
        out_specs=(vmem, anywhere),
        scratch_shapes=[
            pltpu.VMEM((total, width), bf16),
            pltpu.VMEM((total, total), bf16),
            pltpu.VMEM((total, width), f32),
            pltpu.VMEM((total, width), bf16),
            pltpu.VMEM((depth, width), f32),
            pltpu.SemaphoreType.DMA((8,)),
        ],
        compiler_params=pltpu.CompilerParams(vmem_limit_bytes=24 * 2**20),
        name="pairs",
    )(
        sharpness_factor,
        score_shift_term,
        match[None, :],
        zt,
        projected,
        turned,
        matrix,
        *images,
    )
    return (grad_image, grad_text, head_grad)


def solution(mesh):
    gathered = dict(mesh.shape) == {"dp": 16, "fsdp": 2}
    per_device = gathered_plan if gathered else ring_plan
    return jax.shard_map(
        per_device,
        mesh=mesh,
        in_specs=(
            P(("dp", "fsdp"), None),
            P(("dp", "fsdp"), None),
            P("fsdp", None),
            P("dp"),
            P(),
            P(),
        ),
        out_specs=(P(("dp", "fsdp"), None), P(("dp", "fsdp"), None), P("fsdp", None)),
        check_vma=False,
    )
```

```python
import functools

import jax
import jax.numpy as jnp
from jax import lax
from jax.experimental import pallas as pl
from jax.experimental.pallas import tpu as pltpu
from jax.sharding import PartitionSpec as P

epsilon = 1e-06


def passed_along(block, axis, distance):
    devices = range(lax.axis_size(axis))
    route = [((i - distance) % len(devices), i) for i in devices]
    return lax.ppermute(block, axis, route)


def normalize(values):
    norms = jnp.sqrt(jnp.sum(values * values, axis=1, keepdims=True) + epsilon)
    return (values / norms, norms)


def unproject(grad_unit, unit, norms):
    return (grad_unit - unit * jnp.sum(unit * grad_unit, axis=1, keepdims=True)) / norms


def ring_plan(
    picture_mean_embeddings,
    caption_tower_summary,
    caption_mapping_matrix,
    picture_match_index,
    sharpness_factor,
    score_shift_term,
):
    rows = caption_tower_summary.shape[0]
    width = caption_mapping_matrix.shape[1]
    cycle_size = lax.axis_size("dp")
    column_count = lax.axis_size("fsdp")
    cycle_index = lax.axis_index("dp")
    column_index = lax.axis_index("fsdp")
    score_multiplier = sharpness_factor[0]
    offset = score_shift_term[0]
    feature_column_set = lax.all_to_all(
        caption_tower_summary, "fsdp", split_axis=1, concat_axis=0, tiled=True
    )
    projected = jnp.dot(
        caption_tower_summary,
        lax.all_gather(caption_mapping_matrix, "fsdp", axis=0, tiled=True),
        preferred_element_type=jnp.float32,
    )
    unit_text, text_norm = normalize(projected)
    text_unit = unit_text.astype(jnp.bfloat16)
    unit_image, image_norm = normalize(picture_mean_embeddings.astype(jnp.float32))
    image_unit = lax.all_gather(unit_image.astype(jnp.bfloat16), "fsdp", axis=0, tiled=True)
    group = image_unit.shape[0]

    def tile(block, text_rows):
        scores = lax.dot_general(
            image_unit, block, (((1,), (1,)), ((), ())), preferred_element_type=jnp.float32
        )
        logits = score_multiplier * scores + offset
        sign = jnp.where(picture_match_index[:, None] == text_rows[None, :], 1.0, -1.0).astype(
            jnp.float32
        )
        weights = (score_multiplier * -sign * jax.nn.sigmoid(-sign * logits)).astype(jnp.bfloat16)
        image_part = jnp.dot(weights, block, preferred_element_type=jnp.float32)
        text_part = lax.dot_general(
            weights, image_unit, (((0,), (0,)), ((), ())), preferred_element_type=jnp.float32
        )
        return (image_part, text_part)

    def rows_of(owner, count):
        return (owner * column_count + column_index) * rows + jnp.arange(count, dtype=jnp.int32)

    image_start = jnp.zeros((group, width), jnp.float32)

    def advance(count, state):
        block, carried, image_sum = state
        owner = (cycle_index - count) % cycle_size
        image_part, text_part = tile(block, rows_of(owner, rows))
        block = passed_along(block, "dp", 1)
        carried = passed_along(carried + text_part, "dp", 1)
        return (block, carried, image_sum + image_part)

    state = (text_unit, jnp.zeros((rows, width), jnp.float32), image_start)
    block, grad_zt, image_sum = lax.fori_loop(0, cycle_size, advance, state)
    grad_zi = lax.psum_scatter(image_sum, "fsdp", scatter_dimension=0, tiled=True)
    grad_image = unproject(grad_zi, unit_image, image_norm)
    grad_proj = unproject(grad_zt, unit_text, text_norm).astype(jnp.bfloat16)
    grad_group = lax.all_gather(grad_proj, "fsdp", axis=0, tiled=True)
    head_part = lax.dot_general(
        feature_column_set, grad_group, (((0,), (0,)), ((), ())), preferred_element_type=jnp.float32
    )
    head_grad = lax.psum(head_part, "dp")
    grad_text = lax.dot_general(
        grad_proj,
        lax.all_gather(caption_mapping_matrix, "fsdp", axis=0, tiled=True),
        (((1,), (1,)), ((), ())),
        preferred_element_type=jnp.float32,
    )
    return (grad_image, grad_text, head_grad)


def across(block, bits):
    count = lax.axis_size("dp") * lax.axis_size("fsdp")
    return lax.ppermute(block, ("dp", "fsdp"), [(i, i ^ bits) for i in range(count)])


Y, CORE, X, Z1, Z2 = 1, 2, 4, 8, 16
IMAGE_ORDER = (Y, X, Z2, Z1, CORE)
TEXT_ORDER = (Y, Z2, Z1, CORE, X)
NT = (((1,), (1,)), ((), ()))
TN = (((0,), (0,)), ((), ()))


def dot(a, b, dims=(((1,), (0,)), ((), ()))):
    return lax.dot_general(a, b, dims, preferred_element_type=jnp.float32)


def cuts(size, step):
    return [slice(k, min(k + step, size)) for k in range(0, size, step)]


def text_ids(shape, axis, rows, place):
    row = lax.broadcasted_iota(jnp.int32, shape, axis)
    block = sum((row >= k * rows).astype(jnp.int32) for k in range(1, shape[axis] // rows))
    owner = jnp.zeros_like(row)
    for k, bits in enumerate(TEXT_ORDER):
        owner += ((block >> k) & 1) * bits
    return (owner ^ place) * rows + row - block * rows


def weigh(scores, paired, sharpness, shift):
    logits = sharpness[0] * scores + shift[0]
    sign = jnp.where(paired, 1.0, -1.0)
    return (sharpness[0] * -sign * jax.nn.sigmoid(-sign * logits)).astype(jnp.bfloat16)


def project(text, matrix, projected, zt):
    for cut in cuts(matrix.shape[1], 256):
        projected[:, cut] = dot(text[...], matrix[:, cut])
    for block in cuts(text.shape[0], 160):
        value = projected[block]
        inverse = lax.rsqrt(jnp.sum(value * value, axis=1, keepdims=True) + epsilon)
        zt[block] = (value * inverse).astype(jnp.bfloat16)


def early_kernel(matrix_own, matrix_near, matrix_far, *rest):
    texts, rest = rest[:2], rest[2:]
    zt, projected, turned, matrix, text, sems = rest
    depth, near = matrix_own.shape[0], matrix_near.shape[0]
    core, side = lax.rem(lax.axis_index("dp"), 2), lax.axis_index("fsdp")

    other = (1 - side) * depth
    places = (side * depth, other + core * near, other + (1 - core) * near)
    copies = []
    for k, (source, start) in enumerate(zip((matrix_own, matrix_near, matrix_far), places)):
        start = pl.multiple_of(start, 32)
        target = matrix.at[pl.ds(start, source.shape[0])]
        copies.append(pltpu.make_async_copy(source, target, sems.at[k]))
        copies[-1].start()
    count = texts[0].shape[0]
    for k, source in enumerate(texts):
        text[pl.ds(k * count, count)] = source[...]
    for s in (0, 1):

        @pl.when(side == s)
        def _():
            turned[...] = jnp.transpose(text[: turned.shape[1], s * depth : (s + 1) * depth])

    for copy in copies:
        copy.wait()
    project(text, matrix, projected, zt)


def batch_kernel(sharpness, shift, image, match, zt_early, projected_early, *rest):
    (turned_early, matrix), texts, images, rest = rest[:2], rest[2:6], rest[6:10], rest[10:]
    (grad_image, grad_text, head_grad), rest = rest[:3], rest[3:]
    zi, text, zt, projected, weights, grad, turned, proj, sems = rest
    rows = image.shape[0]
    total, width = zi.shape
    half = total // 2
    depth = head_grad.shape[0]
    group, side = lax.axis_index("dp"), lax.axis_index("fsdp")

    count = total // 4
    for sources, target in ((texts, text), (images, zi)):
        for k, source in enumerate(sources):
            target[pl.ds(k * count, count)] = source[...]
    late = pl.ds(half, half)
    project(text.at[late], matrix, projected.at[late], zt.at[late])
    zt[:half] = zt_early[...]
    first = turned_early.shape[1]
    turned[:, :first] = turned_early[...]
    for s in (0, 1):

        @pl.when(side == s)
        def _():
            turned[:, first:] = jnp.transpose(text[first:, s * depth : (s + 1) * depth])

    ids = text_ids((total, 1), 0, rows, group * 2 + side)
    for cut in cuts(total, 256):
        scores = dot(zt[...], zi[cut], NT)
        weights[:, cut] = weigh(scores, ids == match[:, cut], sharpness, shift)
    for cut in cuts(width, 256):
        grad[:, cut] = dot(weights[...], zi[:, cut])
    for block in cuts(total, 160):
        value = projected_early[block] if block.stop <= half else projected[block]
        slope = grad[block]
        squares = jnp.sum(value * value, axis=1, keepdims=True) + epsilon
        inner = jnp.sum(value * slope, axis=1, keepdims=True)
        proj[block] = ((slope - value * (inner / squares)) * lax.rsqrt(squares)).astype(
            jnp.bfloat16
        )
    copies = []
    head = grad
    for k, cut in enumerate(cuts(width, 256)):
        head[:depth, cut] = dot(turned[...], proj[:, cut])
        copies.append(
            pltpu.make_async_copy(head.at[:depth, cut], head_grad.at[:, cut], sems.at[k])
        )
        copies[-1].start()
    grad_text[...] = dot(proj[:48], matrix[...], NT)[:rows]
    grad_zi = dot(weights[:, :128], zt[...], TN)[:rows]
    unit_image, image_norm = normalize(image[...].astype(jnp.float32))
    grad_image[...] = unproject(grad_zi, unit_image, image_norm)
    for copy in copies:
        copy.wait()


def gathered_plan(
    picture_mean_embeddings,
    caption_tower_summary,
    caption_mapping_matrix,
    picture_match_index,
    sharpness_factor,
    score_shift_term,
):
    rows, width = caption_tower_summary.shape
    depth = caption_mapping_matrix.shape[0]
    half = depth // 2
    core = lax.axis_index("dp") % 2
    place = lax.axis_index("dp") * 2 + lax.axis_index("fsdp")
    total = rows * 32
    smem = pl.BlockSpec(memory_space=pltpu.SMEM)
    vmem = pl.BlockSpec(memory_space=pltpu.VMEM)
    anywhere = pl.BlockSpec(memory_space=pl.ANY)
    f32, bf16 = jnp.float32, jnp.bfloat16

    def doubled(block, bits):
        return jnp.concatenate([block, across(block, bits)])

    unit_image, _ = normalize(picture_mean_embeddings.astype(f32))
    own = jnp.stack([unit_image.astype(bf16), caption_tower_summary])
    match = jnp.broadcast_to(picture_match_index, (16, 2 * rows))
    own, match = lax.optimization_barrier((own, match))
    beside = across(own, Y)
    match = lax.all_to_all(match, "dp", split_axis=0, concat_axis=0, tiled=True)
    images = jnp.concatenate([own[0], beside[0]])
    texts = jnp.concatenate([own[1], beside[1]])

    quarter = lax.dynamic_slice_in_dim(caption_mapping_matrix, core * half, half, 0)
    quarter, _ = lax.optimization_barrier((quarter, beside))
    near = across(quarter, Y)
    far = across(near, CORE)
    for bits in TEXT_ORDER[1:3]:
        texts = doubled(texts, bits)
    texts = [texts, across(texts, CORE), across(texts, TEXT_ORDER[4])]

    images = doubled(images, IMAGE_ORDER[1])
    owners = jnp.zeros((32,), jnp.int32)
    for k, bits in enumerate(IMAGE_ORDER):
        owners += ((jnp.arange(32, dtype=jnp.int32) >> k) & 1) * bits
    match = match.reshape(32, rows)[owners ^ place].reshape(1, total)
    images, match = lax.optimization_barrier((images, match))
    images = doubled(images, IMAGE_ORDER[2])
    images = [images, across(images, IMAGE_ORDER[3]), across(images, CORE)]

    params = pltpu.CompilerParams(vmem_limit_bytes=24 * 2**20)
    zt, projected, turned, matrix = pl.pallas_call(
        early_kernel,
        out_shape=(
            jax.ShapeDtypeStruct((total // 2, width), bf16),
            jax.ShapeDtypeStruct((total // 2, width), f32),
            jax.ShapeDtypeStruct((depth, 256), bf16),
            jax.ShapeDtypeStruct((2 * depth, width), bf16),
        ),
        in_specs=[anywhere] * 3 + [vmem] * 2,
        out_specs=(vmem,) * 4,
        scratch_shapes=[pltpu.VMEM((total // 2, width), bf16), pltpu.SemaphoreType.DMA((3,))],
        compiler_params=params,
        name="early_texts",
    )(caption_mapping_matrix, near, far, *texts[:2])
    texts[2], images[1], zt = lax.optimization_barrier((texts[2], images[1], zt))
    texts.append(across(texts[2], CORE))
    images.append(across(images[1], CORE))
    return pl.pallas_call(
        batch_kernel,
        out_shape=(
            jax.ShapeDtypeStruct((rows, width), f32),
            jax.ShapeDtypeStruct((rows, width), f32),
            jax.ShapeDtypeStruct((depth, width), f32),
        ),
        in_specs=[smem] * 2 + [vmem] * 14,
        out_specs=(vmem, vmem, anywhere),
        scratch_shapes=[
            pltpu.VMEM((total, width), bf16),
            pltpu.VMEM((total, width), bf16),
            pltpu.VMEM((total, width), bf16),
            pltpu.VMEM((total, width), f32),
            pltpu.VMEM((total, total), bf16),
            pltpu.VMEM((total, width), f32),
            pltpu.VMEM((depth, total), bf16),
            pltpu.VMEM((total, width), bf16),
            pltpu.SemaphoreType.DMA((8,)),
        ],
        compiler_params=params,
        name="batch",
    )(
        sharpness_factor,
        score_shift_term,
        picture_mean_embeddings,
        match,
        zt,
        projected,
        turned,
        matrix,
        *texts,
        *images,
    )


def solution(mesh):
    gathered = dict(mesh.shape) == {"dp": 16, "fsdp": 2}
    per_device = gathered_plan if gathered else ring_plan
    return jax.shard_map(
        per_device,
        mesh=mesh,
        in_specs=(
            P(("dp", "fsdp"), None),
            P(("dp", "fsdp"), None),
            P("fsdp", None),
            P("dp"),
            P(),
            P(),
        ),
        out_specs=(P(("dp", "fsdp"), None), P(("dp", "fsdp"), None), P("fsdp", None)),
        check_vma=False,
    )
```

```python
import functools

import jax
import jax.numpy as jnp
from jax import lax
from jax.experimental import pallas as pl
from jax.experimental.pallas import tpu as pltpu
from jax.sharding import PartitionSpec as P

epsilon = 1e-06


def passed_along(block, axis, distance):
    devices = range(lax.axis_size(axis))
    route = [((i - distance) % len(devices), i) for i in devices]
    return lax.ppermute(block, axis, route)


def normalize(values):
    norms = jnp.sqrt(jnp.sum(values * values, axis=1, keepdims=True) + epsilon)
    return (values / norms, norms)


def unproject(grad_unit, unit, norms):
    return (grad_unit - unit * jnp.sum(unit * grad_unit, axis=1, keepdims=True)) / norms


def ring_plan(
    picture_mean_embeddings,
    caption_tower_summary,
    caption_mapping_matrix,
    picture_match_index,
    sharpness_factor,
    score_shift_term,
):
    rows = caption_tower_summary.shape[0]
    width = caption_mapping_matrix.shape[1]
    cycle_size = lax.axis_size("dp")
    column_count = lax.axis_size("fsdp")
    cycle_index = lax.axis_index("dp")
    column_index = lax.axis_index("fsdp")
    score_multiplier = sharpness_factor[0]
    offset = score_shift_term[0]
    feature_column_set = lax.all_to_all(
        caption_tower_summary, "fsdp", split_axis=1, concat_axis=0, tiled=True
    )
    projected = jnp.dot(
        caption_tower_summary,
        lax.all_gather(caption_mapping_matrix, "fsdp", axis=0, tiled=True),
        preferred_element_type=jnp.float32,
    )
    unit_text, text_norm = normalize(projected)
    text_unit = unit_text.astype(jnp.bfloat16)
    unit_image, image_norm = normalize(picture_mean_embeddings.astype(jnp.float32))
    image_unit = lax.all_gather(unit_image.astype(jnp.bfloat16), "fsdp", axis=0, tiled=True)
    group = image_unit.shape[0]

    def tile(block, text_rows):
        scores = lax.dot_general(
            image_unit, block, (((1,), (1,)), ((), ())), preferred_element_type=jnp.float32
        )
        logits = score_multiplier * scores + offset
        sign = jnp.where(picture_match_index[:, None] == text_rows[None, :], 1.0, -1.0).astype(
            jnp.float32
        )
        weights = (score_multiplier * -sign * jax.nn.sigmoid(-sign * logits)).astype(jnp.bfloat16)
        image_part = jnp.dot(weights, block, preferred_element_type=jnp.float32)
        text_part = lax.dot_general(
            weights, image_unit, (((0,), (0,)), ((), ())), preferred_element_type=jnp.float32
        )
        return (image_part, text_part)

    def rows_of(owner, count):
        return (owner * column_count + column_index) * rows + jnp.arange(count, dtype=jnp.int32)

    image_start = jnp.zeros((group, width), jnp.float32)

    def advance(count, state):
        block, carried, image_sum = state
        owner = (cycle_index - count) % cycle_size
        image_part, text_part = tile(block, rows_of(owner, rows))
        block = passed_along(block, "dp", 1)
        carried = passed_along(carried + text_part, "dp", 1)
        return (block, carried, image_sum + image_part)

    state = (text_unit, jnp.zeros((rows, width), jnp.float32), image_start)
    block, grad_zt, image_sum = lax.fori_loop(0, cycle_size, advance, state)
    grad_zi = lax.psum_scatter(image_sum, "fsdp", scatter_dimension=0, tiled=True)
    grad_image = unproject(grad_zi, unit_image, image_norm)
    grad_proj = unproject(grad_zt, unit_text, text_norm).astype(jnp.bfloat16)
    grad_group = lax.all_gather(grad_proj, "fsdp", axis=0, tiled=True)
    head_part = lax.dot_general(
        feature_column_set, grad_group, (((0,), (0,)), ((), ())), preferred_element_type=jnp.float32
    )
    head_grad = lax.psum(head_part, "dp")
    grad_text = lax.dot_general(
        grad_proj,
        lax.all_gather(caption_mapping_matrix, "fsdp", axis=0, tiled=True),
        (((1,), (1,)), ((), ())),
        preferred_element_type=jnp.float32,
    )
    return (grad_image, grad_text, head_grad)


def across(block, bits):
    count = lax.axis_size("dp") * lax.axis_size("fsdp")
    return lax.ppermute(block, ("dp", "fsdp"), [(i, i ^ bits) for i in range(count)])


Y, CORE, X, Z1, Z2 = 1, 2, 4, 8, 16
IMAGE_ORDER = (Y, X, Z2, Z1, CORE)
TEXT_ORDER = (Y, Z2, Z1, CORE, X)
NT = (((1,), (1,)), ((), ()))
TN = (((0,), (0,)), ((), ()))


def dot(a, b, dims=(((1,), (0,)), ((), ()))):
    return lax.dot_general(a, b, dims, preferred_element_type=jnp.float32)


def cuts(size, step):
    return [slice(k, min(k + step, size)) for k in range(0, size, step)]


def text_ids(shape, axis, rows, place):
    row = lax.broadcasted_iota(jnp.int32, shape, axis)
    block = sum((row >= k * rows).astype(jnp.int32) for k in range(1, shape[axis] // rows))
    owner = jnp.zeros_like(row)
    for k, bits in enumerate(TEXT_ORDER):
        owner += ((block >> k) & 1) * bits
    return (owner ^ place) * rows + row - block * rows


def weigh(scores, paired, sharpness, shift):
    logits = sharpness[0] * scores + shift[0]
    sign = jnp.where(paired, 1.0, -1.0)
    return (sharpness[0] * -sign * jax.nn.sigmoid(-sign * logits)).astype(jnp.bfloat16)


def own_kernel(image, text, own):
    unit_image, _ = normalize(image[...].astype(jnp.float32))
    own[0] = unit_image.astype(jnp.bfloat16)
    own[1] = text[...]


def project(text, matrix, projected, zt):
    for cut in cuts(matrix.shape[1], 256):
        projected[:, cut] = dot(text[...], matrix[:, cut])
    for block in cuts(text.shape[0], 160):
        value = projected[block]
        inverse = lax.rsqrt(jnp.sum(value * value, axis=1, keepdims=True) + epsilon)
        zt[block] = (value * inverse).astype(jnp.bfloat16)


def early_kernel(matrix_own, matrix_near, matrix_far, *rest):
    texts, rest = rest[:2], rest[2:]
    zt, projected, turned, matrix, text, sems = rest
    depth, near = matrix_own.shape[0], matrix_near.shape[0]
    core, side = lax.rem(lax.axis_index("dp"), 2), lax.axis_index("fsdp")

    other = (1 - side) * depth
    places = (side * depth, other + core * near, other + (1 - core) * near)
    copies = []
    for k, (source, start) in enumerate(zip((matrix_own, matrix_near, matrix_far), places)):
        start = pl.multiple_of(start, 32)
        target = matrix.at[pl.ds(start, source.shape[0])]
        copies.append(pltpu.make_async_copy(source, target, sems.at[k]))
        copies[-1].start()
    count = texts[0].shape[0]
    for k, source in enumerate(texts):
        text[pl.ds(k * count, count)] = source[...]
    for s in (0, 1):

        @pl.when(side == s)
        def _():
            turned[...] = jnp.transpose(text[: turned.shape[1], s * depth : (s + 1) * depth])

    for copy in copies:
        copy.wait()
    project(text, matrix, projected, zt)


def batch_kernel(sharpness, shift, image, match, zt_early, projected_early, *rest):
    (turned_early, matrix), texts, images, rest = rest[:2], rest[2:6], rest[6:10], rest[10:]
    (grad_image, grad_text, head_grad), rest = rest[:3], rest[3:]
    zi, text, zt, projected, weights, grad, turned, proj, sems = rest
    rows = image.shape[0]
    total, width = zi.shape
    half = total // 2
    depth = head_grad.shape[0]
    group, side = lax.axis_index("dp"), lax.axis_index("fsdp")

    count = total // 4
    for sources, target in ((texts, text), (images, zi)):
        for k, source in enumerate(sources):
            target[pl.ds(k * count, count)] = source[...]
    late = pl.ds(half, half)
    project(text.at[late], matrix, projected.at[late], zt.at[late])
    zt[:half] = zt_early[...]
    first = turned_early.shape[1]
    turned[:, :first] = turned_early[...]
    for s in (0, 1):

        @pl.when(side == s)
        def _():
            turned[:, first:] = jnp.transpose(text[first:, s * depth : (s + 1) * depth])

    ids = text_ids((total, 1), 0, rows, group * 2 + side)
    for cut in cuts(total, 256):
        scores = dot(zt[...], zi[cut], NT)
        weights[:, cut] = weigh(scores, ids == match[:, cut], sharpness, shift)
    for cut in cuts(width, 256):
        grad[:, cut] = dot(weights[...], zi[:, cut])
    for block in cuts(total, 160):
        value = projected_early[block] if block.stop <= half else projected[block]
        slope = grad[block]
        squares = jnp.sum(value * value, axis=1, keepdims=True) + epsilon
        inner = jnp.sum(value * slope, axis=1, keepdims=True)
        proj[block] = ((slope - value * (inner / squares)) * lax.rsqrt(squares)).astype(
            jnp.bfloat16
        )
    copies = []
    head = grad
    for k, cut in enumerate(cuts(width, 256)):
        head[:depth, cut] = dot(turned[...], proj[:, cut])
        copies.append(
            pltpu.make_async_copy(head.at[:depth, cut], head_grad.at[:, cut], sems.at[k])
        )
        copies[-1].start()
    grad_text[...] = dot(proj[:48], matrix[...], NT)[:rows]
    grad_zi = dot(weights[:, :128], zt[...], TN)[:rows]
    unit_image, image_norm = normalize(image[...].astype(jnp.float32))
    grad_image[...] = unproject(grad_zi, unit_image, image_norm)
    for copy in copies:
        copy.wait()


def gathered_plan(
    picture_mean_embeddings,
    caption_tower_summary,
    caption_mapping_matrix,
    picture_match_index,
    sharpness_factor,
    score_shift_term,
):
    rows, width = caption_tower_summary.shape
    depth = caption_mapping_matrix.shape[0]
    half = depth // 2
    core = lax.axis_index("dp") % 2
    place = lax.axis_index("dp") * 2 + lax.axis_index("fsdp")
    total = rows * 32
    smem = pl.BlockSpec(memory_space=pltpu.SMEM)
    vmem = pl.BlockSpec(memory_space=pltpu.VMEM)
    anywhere = pl.BlockSpec(memory_space=pl.ANY)
    f32, bf16 = jnp.float32, jnp.bfloat16

    def doubled(block, bits):
        return jnp.concatenate([block, across(block, bits)])

    own = pl.pallas_call(
        own_kernel,
        out_shape=jax.ShapeDtypeStruct((2, rows, width), bf16),
        name="own_block",
    )(picture_mean_embeddings, caption_tower_summary)
    beside = across(own, Y)
    images = jnp.concatenate([own[0], beside[0]])
    texts = jnp.concatenate([own[1], beside[1]])

    quarter = lax.dynamic_slice_in_dim(caption_mapping_matrix, core * half, half, 0)
    quarter, _ = lax.optimization_barrier((quarter, beside))
    near = across(quarter, Y)
    for bits in TEXT_ORDER[1:3]:
        texts = doubled(texts, bits)
    texts = [texts, across(texts, CORE), across(texts, TEXT_ORDER[4])]

    images = doubled(images, IMAGE_ORDER[1])
    owners = jnp.zeros((32,), jnp.int32)
    for k, bits in enumerate(IMAGE_ORDER):
        owners += ((jnp.arange(32, dtype=jnp.int32) >> k) & 1) * bits
    images, match = lax.optimization_barrier((images, picture_match_index))
    match = jnp.broadcast_to(match, (16, 2 * rows))
    match = lax.all_to_all(match, "dp", split_axis=0, concat_axis=0, tiled=True)
    near, match = lax.optimization_barrier((near, match))
    far = across(near, CORE)
    match = match.reshape(32, rows)[owners ^ place].reshape(1, total)
    images = doubled(images, IMAGE_ORDER[2])
    images = [images, across(images, IMAGE_ORDER[3]), across(images, CORE)]

    params = pltpu.CompilerParams(vmem_limit_bytes=24 * 2**20)
    zt, projected, turned, matrix = pl.pallas_call(
        early_kernel,
        out_shape=(
            jax.ShapeDtypeStruct((total // 2, width), bf16),
            jax.ShapeDtypeStruct((total // 2, width), f32),
            jax.ShapeDtypeStruct((depth, 256), bf16),
            jax.ShapeDtypeStruct((2 * depth, width), bf16),
        ),
        in_specs=[anywhere] * 3 + [vmem] * 2,
        out_specs=(vmem,) * 4,
        scratch_shapes=[pltpu.VMEM((total // 2, width), bf16), pltpu.SemaphoreType.DMA((3,))],
        compiler_params=params,
        name="early_texts",
    )(caption_mapping_matrix, near, far, *texts[:2])
    texts[2], images[1], zt = lax.optimization_barrier((texts[2], images[1], zt))
    texts.append(across(texts[2], CORE))
    images.append(across(images[1], CORE))
    return pl.pallas_call(
        batch_kernel,
        out_shape=(
            jax.ShapeDtypeStruct((rows, width), f32),
            jax.ShapeDtypeStruct((rows, width), f32),
            jax.ShapeDtypeStruct((depth, width), f32),
        ),
        in_specs=[smem] * 2 + [vmem] * 14,
        out_specs=(vmem, vmem, anywhere),
        scratch_shapes=[
            pltpu.VMEM((total, width), bf16),
            pltpu.VMEM((total, width), bf16),
            pltpu.VMEM((total, width), bf16),
            pltpu.VMEM((total, width), f32),
            pltpu.VMEM((total, total), bf16),
            pltpu.VMEM((total, width), f32),
            pltpu.VMEM((depth, total), bf16),
            pltpu.VMEM((total, width), bf16),
            pltpu.SemaphoreType.DMA((8,)),
        ],
        compiler_params=params,
        name="batch",
    )(
        sharpness_factor,
        score_shift_term,
        picture_mean_embeddings,
        match,
        zt,
        projected,
        turned,
        matrix,
        *texts,
        *images,
    )


def solution(mesh):
    gathered = dict(mesh.shape) == {"dp": 16, "fsdp": 2}
    per_device = gathered_plan if gathered else ring_plan
    return jax.shard_map(
        per_device,
        mesh=mesh,
        in_specs=(
            P(("dp", "fsdp"), None),
            P(("dp", "fsdp"), None),
            P("fsdp", None),
            P("dp"),
            P(),
            P(),
        ),
        out_specs=(P(("dp", "fsdp"), None), P(("dp", "fsdp"), None), P("fsdp", None)),
        check_vma=False,
    )
```

```python
import functools

import jax
import jax.numpy as jnp
from jax import lax
from jax.experimental import pallas as pl
from jax.experimental.pallas import tpu as pltpu
from jax.sharding import PartitionSpec as P

epsilon = 1e-06


def passed_along(block, axis, distance):
    devices = range(lax.axis_size(axis))
    route = [((i - distance) % len(devices), i) for i in devices]
    return lax.ppermute(block, axis, route)


def normalize(values):
    norms = jnp.sqrt(jnp.sum(values * values, axis=1, keepdims=True) + epsilon)
    return (values / norms, norms)


def unproject(grad_unit, unit, norms):
    return (grad_unit - unit * jnp.sum(unit * grad_unit, axis=1, keepdims=True)) / norms


def ring_plan(
    picture_mean_embeddings,
    caption_tower_summary,
    caption_mapping_matrix,
    picture_match_index,
    sharpness_factor,
    score_shift_term,
):
    rows = caption_tower_summary.shape[0]
    width = caption_mapping_matrix.shape[1]
    cycle_size = lax.axis_size("dp")
    column_count = lax.axis_size("fsdp")
    cycle_index = lax.axis_index("dp")
    column_index = lax.axis_index("fsdp")
    score_multiplier = sharpness_factor[0]
    offset = score_shift_term[0]
    feature_column_set = lax.all_to_all(
        caption_tower_summary, "fsdp", split_axis=1, concat_axis=0, tiled=True
    )
    projected = jnp.dot(
        caption_tower_summary,
        lax.all_gather(caption_mapping_matrix, "fsdp", axis=0, tiled=True),
        preferred_element_type=jnp.float32,
    )
    unit_text, text_norm = normalize(projected)
    text_unit = unit_text.astype(jnp.bfloat16)
    unit_image, image_norm = normalize(picture_mean_embeddings.astype(jnp.float32))
    image_unit = lax.all_gather(unit_image.astype(jnp.bfloat16), "fsdp", axis=0, tiled=True)
    group = image_unit.shape[0]

    def tile(block, text_rows):
        scores = lax.dot_general(
            image_unit, block, (((1,), (1,)), ((), ())), preferred_element_type=jnp.float32
        )
        logits = score_multiplier * scores + offset
        sign = jnp.where(picture_match_index[:, None] == text_rows[None, :], 1.0, -1.0).astype(
            jnp.float32
        )
        weights = (score_multiplier * -sign * jax.nn.sigmoid(-sign * logits)).astype(jnp.bfloat16)
        image_part = jnp.dot(weights, block, preferred_element_type=jnp.float32)
        text_part = lax.dot_general(
            weights, image_unit, (((0,), (0,)), ((), ())), preferred_element_type=jnp.float32
        )
        return (image_part, text_part)

    def rows_of(owner, count):
        return (owner * column_count + column_index) * rows + jnp.arange(count, dtype=jnp.int32)

    image_start = jnp.zeros((group, width), jnp.float32)

    def advance(count, state):
        block, carried, image_sum = state
        owner = (cycle_index - count) % cycle_size
        image_part, text_part = tile(block, rows_of(owner, rows))
        block = passed_along(block, "dp", 1)
        carried = passed_along(carried + text_part, "dp", 1)
        return (block, carried, image_sum + image_part)

    state = (text_unit, jnp.zeros((rows, width), jnp.float32), image_start)
    block, grad_zt, image_sum = lax.fori_loop(0, cycle_size, advance, state)
    grad_zi = lax.psum_scatter(image_sum, "fsdp", scatter_dimension=0, tiled=True)
    grad_image = unproject(grad_zi, unit_image, image_norm)
    grad_proj = unproject(grad_zt, unit_text, text_norm).astype(jnp.bfloat16)
    grad_group = lax.all_gather(grad_proj, "fsdp", axis=0, tiled=True)
    head_part = lax.dot_general(
        feature_column_set, grad_group, (((0,), (0,)), ((), ())), preferred_element_type=jnp.float32
    )
    head_grad = lax.psum(head_part, "dp")
    grad_text = lax.dot_general(
        grad_proj,
        lax.all_gather(caption_mapping_matrix, "fsdp", axis=0, tiled=True),
        (((1,), (1,)), ((), ())),
        preferred_element_type=jnp.float32,
    )
    return (grad_image, grad_text, head_grad)


def across(block, bits):
    count = lax.axis_size("dp") * lax.axis_size("fsdp")
    return lax.ppermute(block, ("dp", "fsdp"), [(i, i ^ bits) for i in range(count)])


Y, CORE, X, Z1, Z2 = 1, 2, 4, 8, 16
IMAGE_ORDER = (Y, X, Z2, Z1, CORE)
TEXT_ORDER = (Y, Z2, Z1, CORE, X)
NT = (((1,), (1,)), ((), ()))
TN = (((0,), (0,)), ((), ()))


def dot(a, b, dims=(((1,), (0,)), ((), ()))):
    return lax.dot_general(a, b, dims, preferred_element_type=jnp.float32)


def cuts(size, step):
    return [slice(k, min(k + step, size)) for k in range(0, size, step)]


def owners(order, shape, axis, rows, place):
    row = lax.broadcasted_iota(jnp.int32, shape, axis)
    block = sum((row >= k * rows).astype(jnp.int32) for k in range(1, shape[axis] // rows))
    owner = jnp.zeros_like(row)
    for k, bits in enumerate(order):
        owner += ((block >> k) & 1) * bits
    return owner ^ place, row - block * rows


def weigh(scores, paired, sharpness, shift):
    logits = sharpness[0] * scores + shift[0]
    sign = jnp.where(paired, 1.0, -1.0)
    return (sharpness[0] * -sign * jax.nn.sigmoid(-sign * logits)).astype(jnp.bfloat16)


def own_kernel(image, text, own, images):
    unit_image, _ = normalize(image[...].astype(jnp.float32))
    images[...] = unit_image.astype(jnp.bfloat16)
    own[0] = images[...]
    own[1] = text[...]


def index_kernel(rows, found, match):
    groups, count = found.shape
    place = lax.axis_index("dp") * 2 + lax.axis_index("fsdp")
    total = match.shape[1]
    owner, row = owners(IMAGE_ORDER, (1, total), 1, rows, place)
    column = (owner & 1) * rows + row
    chosen = lax.broadcasted_iota(jnp.int32, (count, total), 0) == column
    chosen = chosen.astype(jnp.float32).astype(jnp.bfloat16)
    spread = 0
    for part, scale in ((found[...] >> 5, 32.0), (found[...] & 31, 1.0)):
        spread += scale * dot(part.astype(jnp.float32).astype(jnp.bfloat16), chosen)
    mine = lax.broadcasted_iota(jnp.int32, (groups, total), 0) == owner >> 1
    match[...] = jnp.sum(jnp.where(mine, spread, 0.0), axis=0, keepdims=True).astype(jnp.int32)


def project(text, matrix, projected, zt):
    for cut in cuts(matrix.shape[1], 256):
        projected[:, cut] = dot(text[...], matrix[:, cut])
    for block in cuts(text.shape[0], 160):
        value = projected[block]
        inverse = lax.rsqrt(jnp.sum(value * value, axis=1, keepdims=True) + epsilon)
        zt[block] = (value * inverse).astype(jnp.bfloat16)


def early_kernel(matrix_own, matrix_near, matrix_far, *rest):
    texts, rest = rest[:2], rest[2:]
    zt, projected, turned, matrix, text, sems = rest
    depth, near = matrix_own.shape[0], matrix_near.shape[0]
    core, side = lax.rem(lax.axis_index("dp"), 2), lax.axis_index("fsdp")

    other = (1 - side) * depth
    places = (side * depth, other + core * near, other + (1 - core) * near)
    copies = []
    for k, (source, start) in enumerate(zip((matrix_own, matrix_near, matrix_far), places)):
        start = pl.multiple_of(start, 32)
        target = matrix.at[pl.ds(start, source.shape[0])]
        copies.append(pltpu.make_async_copy(source, target, sems.at[k]))
        copies[-1].start()
    count = texts[0].shape[0]
    for k, source in enumerate(texts):
        text[pl.ds(k * count, count)] = source[...]
    for s in (0, 1):

        @pl.when(side == s)
        def _():
            turned[...] = jnp.transpose(text[: turned.shape[1], s * depth : (s + 1) * depth])

    for copy in copies:
        copy.wait()
    project(text, matrix, projected, zt)


def batch_kernel(sharpness, shift, image, match, zt_early, projected_early, *rest):
    (turned_early, matrix), texts, images, rest = rest[:2], rest[2:6], rest[6:10], rest[10:]
    (grad_image, grad_text, head_grad), rest = rest[:3], rest[3:]
    zi, text, zt, projected, weights, grad, turned, proj, sems = rest
    rows = image.shape[0]
    total, width = zi.shape
    half = total // 2
    depth = head_grad.shape[0]
    group, side = lax.axis_index("dp"), lax.axis_index("fsdp")

    count = total // 4
    for sources, target in ((texts, text), (images, zi)):
        for k, source in enumerate(sources):
            target[pl.ds(k * count, count)] = source[...]
    late = pl.ds(half, half)
    project(text.at[late], matrix, projected.at[late], zt.at[late])
    zt[:half] = zt_early[...]
    first = turned_early.shape[1]
    turned[:, :first] = turned_early[...]
    for s in (0, 1):

        @pl.when(side == s)
        def _():
            turned[:, first:] = jnp.transpose(text[first:, s * depth : (s + 1) * depth])

    owner, row = owners(TEXT_ORDER, (total, 1), 0, rows, group * 2 + side)
    ids = owner * rows + row
    for cut in cuts(total, 256):
        scores = dot(zt[...], zi[cut], NT)
        weights[:, cut] = weigh(scores, ids == match[:, cut], sharpness, shift)
    for cut in cuts(width, 256):
        grad[:, cut] = dot(weights[...], zi[:, cut])
    for block in cuts(total, 160):
        value = projected_early[block] if block.stop <= half else projected[block]
        slope = grad[block]
        squares = jnp.sum(value * value, axis=1, keepdims=True) + epsilon
        inner = jnp.sum(value * slope, axis=1, keepdims=True)
        proj[block] = ((slope - value * (inner / squares)) * lax.rsqrt(squares)).astype(
            jnp.bfloat16
        )
    copies = []
    head = grad
    for k, cut in enumerate(cuts(width, 256)):
        head[:depth, cut] = dot(turned[...], proj[:, cut])
        copies.append(
            pltpu.make_async_copy(head.at[:depth, cut], head_grad.at[:, cut], sems.at[k])
        )
        copies[-1].start()
    grad_text[...] = dot(proj[:48], matrix[...], NT)[:rows]
    grad_zi = dot(weights[:, :128], zt[...], TN)[:rows]
    unit_image, image_norm = normalize(image[...].astype(jnp.float32))
    grad_image[...] = unproject(grad_zi, unit_image, image_norm)
    for copy in copies:
        copy.wait()


def gathered_plan(
    picture_mean_embeddings,
    caption_tower_summary,
    caption_mapping_matrix,
    picture_match_index,
    sharpness_factor,
    score_shift_term,
):
    rows, width = caption_tower_summary.shape
    depth = caption_mapping_matrix.shape[0]
    half = depth // 2
    core = lax.axis_index("dp") % 2
    total = rows * 32
    smem = pl.BlockSpec(memory_space=pltpu.SMEM)
    vmem = pl.BlockSpec(memory_space=pltpu.VMEM)
    anywhere = pl.BlockSpec(memory_space=pl.ANY)
    f32, bf16 = jnp.float32, jnp.bfloat16
    params = pltpu.CompilerParams(vmem_limit_bytes=24 * 2**20)

    def doubled(block, bits):
        return jnp.concatenate([block, across(block, bits)])

    def direct(block, beside, bits):
        return jnp.concatenate([block, beside, across(block, bits), across(block, bits | Y)])

    own, own_images = pl.pallas_call(
        own_kernel,
        out_shape=(
            jax.ShapeDtypeStruct((2, rows, width), bf16),
            jax.ShapeDtypeStruct((rows, width), bf16),
        ),
        compiler_params=params,
        name="own_block",
    )(picture_mean_embeddings, caption_tower_summary)
    beside = across(own, Y)
    texts = direct(caption_tower_summary, beside[1], TEXT_ORDER[1])
    images = direct(own_images, beside[0], IMAGE_ORDER[1])

    quarter = lax.dynamic_slice_in_dim(caption_mapping_matrix, core * half, half, 0)
    quarter, _ = lax.optimization_barrier((quarter, beside))
    near = across(quarter, Y)
    texts = doubled(texts, TEXT_ORDER[2])
    images = doubled(images, IMAGE_ORDER[2])
    texts = [texts, across(texts, CORE), across(texts, TEXT_ORDER[4])]
    near, texts[1] = lax.optimization_barrier((near, texts[1]))
    far = across(near, CORE)
    _, match = lax.optimization_barrier((images, picture_match_index))
    images = [images, across(images, IMAGE_ORDER[3]), across(images, CORE)]
    match = jnp.broadcast_to(match, (16, 2 * rows))
    match = lax.all_to_all(match, "dp", split_axis=0, concat_axis=0, tiled=True)
    match = pl.pallas_call(
        functools.partial(index_kernel, rows),
        out_shape=jax.ShapeDtypeStruct((1, total), jnp.int32),
        compiler_params=params,
        name="pair_indices",
    )(match)

    zt, projected, turned, matrix = pl.pallas_call(
        early_kernel,
        out_shape=(
            jax.ShapeDtypeStruct((total // 2, width), bf16),
            jax.ShapeDtypeStruct((total // 2, width), f32),
            jax.ShapeDtypeStruct((depth, 256), bf16),
            jax.ShapeDtypeStruct((2 * depth, width), bf16),
        ),
        in_specs=[anywhere] * 3 + [vmem] * 2,
        out_specs=(vmem,) * 4,
        scratch_shapes=[pltpu.VMEM((total // 2, width), bf16), pltpu.SemaphoreType.DMA((3,))],
        compiler_params=params,
        name="early_texts",
    )(caption_mapping_matrix, near, far, *texts[:2])
    texts[2], images[1], zt, match = lax.optimization_barrier((texts[2], images[1], zt, match))
    texts.append(across(texts[2], CORE))
    images.append(across(images[1], CORE))
    return pl.pallas_call(
        batch_kernel,
        out_shape=(
            jax.ShapeDtypeStruct((rows, width), f32),
            jax.ShapeDtypeStruct((rows, width), f32),
            jax.ShapeDtypeStruct((depth, width), f32),
        ),
        in_specs=[smem] * 2 + [vmem] * 14,
        out_specs=(vmem, vmem, anywhere),
        scratch_shapes=[
            pltpu.VMEM((total, width), bf16),
            pltpu.VMEM((total, width), bf16),
            pltpu.VMEM((total, width), bf16),
            pltpu.VMEM((total, width), f32),
            pltpu.VMEM((total, total), bf16),
            pltpu.VMEM((total, width), f32),
            pltpu.VMEM((depth, total), bf16),
            pltpu.VMEM((total, width), bf16),
            pltpu.SemaphoreType.DMA((8,)),
        ],
        compiler_params=params,
        name="batch",
    )(
        sharpness_factor,
        score_shift_term,
        picture_mean_embeddings,
        match,
        zt,
        projected,
        turned,
        matrix,
        *texts,
        *images,
    )


def solution(mesh):
    gathered = dict(mesh.shape) == {"dp": 16, "fsdp": 2}
    per_device = gathered_plan if gathered else ring_plan
    return jax.shard_map(
        per_device,
        mesh=mesh,
        in_specs=(
            P(("dp", "fsdp"), None),
            P(("dp", "fsdp"), None),
            P("fsdp", None),
            P("dp"),
            P(),
            P(),
        ),
        out_specs=(P(("dp", "fsdp"), None), P(("dp", "fsdp"), None), P("fsdp", None)),
        check_vma=False,
    )
```

```python
import functools

import jax
import jax.numpy as jnp
from jax import lax
from jax.experimental import pallas as pl
from jax.experimental.pallas import tpu as pltpu
from jax.sharding import PartitionSpec as P

epsilon = 1e-06


def passed_along(block, axis, distance):
    devices = range(lax.axis_size(axis))
    route = [((i - distance) % len(devices), i) for i in devices]
    return lax.ppermute(block, axis, route)


def normalize(values):
    norms = jnp.sqrt(jnp.sum(values * values, axis=1, keepdims=True) + epsilon)
    return (values / norms, norms)


def unproject(grad_unit, unit, norms):
    return (grad_unit - unit * jnp.sum(unit * grad_unit, axis=1, keepdims=True)) / norms


def ring_plan(
    picture_mean_embeddings,
    caption_tower_summary,
    caption_mapping_matrix,
    picture_match_index,
    sharpness_factor,
    score_shift_term,
):
    rows = caption_tower_summary.shape[0]
    width = caption_mapping_matrix.shape[1]
    cycle_size = lax.axis_size("dp")
    column_count = lax.axis_size("fsdp")
    cycle_index = lax.axis_index("dp")
    column_index = lax.axis_index("fsdp")
    score_multiplier = sharpness_factor[0]
    offset = score_shift_term[0]
    feature_column_set = lax.all_to_all(
        caption_tower_summary, "fsdp", split_axis=1, concat_axis=0, tiled=True
    )
    projected = jnp.dot(
        caption_tower_summary,
        lax.all_gather(caption_mapping_matrix, "fsdp", axis=0, tiled=True),
        preferred_element_type=jnp.float32,
    )
    unit_text, text_norm = normalize(projected)
    text_unit = unit_text.astype(jnp.bfloat16)
    unit_image, image_norm = normalize(picture_mean_embeddings.astype(jnp.float32))
    image_unit = lax.all_gather(unit_image.astype(jnp.bfloat16), "fsdp", axis=0, tiled=True)
    group = image_unit.shape[0]

    def tile(block, text_rows):
        scores = lax.dot_general(
            image_unit, block, (((1,), (1,)), ((), ())), preferred_element_type=jnp.float32
        )
        logits = score_multiplier * scores + offset
        sign = jnp.where(picture_match_index[:, None] == text_rows[None, :], 1.0, -1.0).astype(
            jnp.float32
        )
        weights = (score_multiplier * -sign * jax.nn.sigmoid(-sign * logits)).astype(jnp.bfloat16)
        image_part = jnp.dot(weights, block, preferred_element_type=jnp.float32)
        text_part = lax.dot_general(
            weights, image_unit, (((0,), (0,)), ((), ())), preferred_element_type=jnp.float32
        )
        return (image_part, text_part)

    def rows_of(owner, count):
        return (owner * column_count + column_index) * rows + jnp.arange(count, dtype=jnp.int32)

    image_start = jnp.zeros((group, width), jnp.float32)

    def advance(count, state):
        block, carried, image_sum = state
        owner = (cycle_index - count) % cycle_size
        image_part, text_part = tile(block, rows_of(owner, rows))
        block = passed_along(block, "dp", 1)
        carried = passed_along(carried + text_part, "dp", 1)
        return (block, carried, image_sum + image_part)

    state = (text_unit, jnp.zeros((rows, width), jnp.float32), image_start)
    block, grad_zt, image_sum = lax.fori_loop(0, cycle_size, advance, state)
    grad_zi = lax.psum_scatter(image_sum, "fsdp", scatter_dimension=0, tiled=True)
    grad_image = unproject(grad_zi, unit_image, image_norm)
    grad_proj = unproject(grad_zt, unit_text, text_norm).astype(jnp.bfloat16)
    grad_group = lax.all_gather(grad_proj, "fsdp", axis=0, tiled=True)
    head_part = lax.dot_general(
        feature_column_set, grad_group, (((0,), (0,)), ((), ())), preferred_element_type=jnp.float32
    )
    head_grad = lax.psum(head_part, "dp")
    grad_text = lax.dot_general(
        grad_proj,
        lax.all_gather(caption_mapping_matrix, "fsdp", axis=0, tiled=True),
        (((1,), (1,)), ((), ())),
        preferred_element_type=jnp.float32,
    )
    return (grad_image, grad_text, head_grad)


def across(block, bits):
    count = lax.axis_size("dp") * lax.axis_size("fsdp")
    return lax.ppermute(block, ("dp", "fsdp"), [(i, i ^ bits) for i in range(count)])


Y, CORE, X, Z1, Z2 = 1, 2, 4, 8, 16
IMAGE_ORDER = (Y, X, Z2, Z1, CORE)
TEXT_ORDER = (Y, Z2, Z1, CORE, X)
NT = (((1,), (1,)), ((), ()))
TN = (((0,), (0,)), ((), ()))


def dot(a, b, dims=(((1,), (0,)), ((), ()))):
    return lax.dot_general(a, b, dims, preferred_element_type=jnp.float32)


def cuts(size, step):
    return [slice(k, min(k + step, size)) for k in range(0, size, step)]


def owners(order, shape, axis, rows, place):
    row = lax.broadcasted_iota(jnp.int32, shape, axis)
    block = sum((row >= k * rows).astype(jnp.int32) for k in range(1, shape[axis] // rows))
    owner = jnp.zeros_like(row)
    for k, bits in enumerate(order):
        owner += ((block >> k) & 1) * bits
    return owner ^ place, row - block * rows


def weigh(scores, paired, sharpness, shift):
    logits = sharpness[0] * scores + shift[0]
    sign = jnp.where(paired, 1.0, -1.0)
    return (sharpness[0] * -sign * jax.nn.sigmoid(-sign * logits)).astype(jnp.bfloat16)


def own_kernel(image, text, match, both, images, texts, digits):
    rows = image.shape[0]
    unit_image, _ = normalize(image[...].astype(jnp.float32))
    both[0] = unit_image.astype(jnp.bfloat16)
    both[1] = text[...]
    texts[...] = text[...]
    digits[...] = jnp.zeros(digits.shape, jnp.float32)
    digits[0:1, : match.shape[1]] = (match[...] >> 5).astype(jnp.float32)
    digits[1:2, : match.shape[1]] = (match[...] & 31).astype(jnp.float32)
    spare = images.shape[0] - rows
    images[...] = jnp.concatenate([unit_image, digits[:spare]]).astype(jnp.bfloat16)


def pair_indices(rows, total, pieces, side):
    digits = jnp.concatenate([piece[-8:, :128].astype(jnp.float32) for piece in pieces])
    lane = lax.broadcasted_iota(jnp.int32, (1, total), 1)
    group = sum((lane >= k).astype(jnp.int32) for k in range(2 * rows, total, 2 * rows))
    row = lane - group * 2 * rows
    row = jnp.where(side == 0, row, jnp.where(row < rows, row + rows, row - rows))
    chosen = lax.broadcasted_iota(jnp.int32, (128, total), 0) == row
    spread = dot(digits.astype(jnp.bfloat16), chosen.astype(jnp.float32).astype(jnp.bfloat16))
    number = lax.broadcasted_iota(jnp.int32, spread.shape, 0)
    scale = jnp.where(number == 2 * group, 32.0, jnp.where(number == 2 * group + 1, 1.0, 0.0))
    return jnp.sum(scale * spread, axis=0, keepdims=True).astype(jnp.int32)


def project(text, matrix, projected, zt):
    for cut in cuts(matrix.shape[1], 256):
        projected[:, cut] = dot(text[...], matrix[:, cut])
    for block in cuts(text.shape[0], 160):
        value = projected[block]
        inverse = lax.rsqrt(jnp.sum(value * value, axis=1, keepdims=True) + epsilon)
        zt[block] = (value * inverse).astype(jnp.bfloat16)


def early_kernel(matrix_own, matrix_near, matrix_far, *rest):
    texts, rest = rest[:2], rest[2:]
    zt, projected, turned, matrix, text, sems = rest
    depth, near = matrix_own.shape[0], matrix_near.shape[0]
    core, side = lax.rem(lax.axis_index("dp"), 2), lax.axis_index("fsdp")

    other = (1 - side) * depth
    places = (side * depth, other + core * near, other + (1 - core) * near)
    copies = []
    for k, (source, start) in enumerate(zip((matrix_own, matrix_near, matrix_far), places)):
        start = pl.multiple_of(start, 32)
        target = matrix.at[pl.ds(start, source.shape[0])]
        copies.append(pltpu.make_async_copy(source, target, sems.at[k]))
        copies[-1].start()
    count = texts[0].shape[0]
    for k, source in enumerate(texts):
        text[pl.ds(k * count, count)] = source[...]
    for s in (0, 1):

        @pl.when(side == s)
        def _():
            turned[...] = jnp.transpose(text[: turned.shape[1], s * depth : (s + 1) * depth])

    for copy in copies:
        copy.wait()
    project(text, matrix, projected, zt)


def batch_kernel(sharpness, shift, image, zt_early, projected_early, *rest):
    (turned_early, matrix), texts, images, rest = rest[:2], rest[2:6], rest[6:10], rest[10:]
    (grad_image, grad_text, head_grad), rest = rest[:3], rest[3:]
    zi, text, zt, projected, weights, grad, turned, proj, sems = rest
    rows = image.shape[0]
    total, width = zi.shape
    half = total // 2
    depth = head_grad.shape[0]
    group, side = lax.axis_index("dp"), lax.axis_index("fsdp")

    count = total // 4
    for sources, target in ((texts, text), (images, zi)):
        for k, source in enumerate(sources):
            target[pl.ds(k * count, count)] = source[:count]
    match = pair_indices(rows, total, images, side)
    late = pl.ds(half, half)
    project(text.at[late], matrix, projected.at[late], zt.at[late])
    zt[:half] = zt_early[...]
    first = turned_early.shape[1]
    turned[:, :first] = turned_early[...]
    for s in (0, 1):

        @pl.when(side == s)
        def _():
            turned[:, first:] = jnp.transpose(text[first:, s * depth : (s + 1) * depth])

    owner, row = owners(TEXT_ORDER, (total, 1), 0, rows, group * 2 + side)
    ids = owner * rows + row
    for cut in cuts(total, 256):
        scores = dot(zt[...], zi[cut], NT)
        weights[:, cut] = weigh(scores, ids == match[:, cut], sharpness, shift)
    for cut in cuts(width, 256):
        grad[:, cut] = dot(weights[...], zi[:, cut])
    for block in cuts(total, 160):
        value = projected_early[block] if block.stop <= half else projected[block]
        slope = grad[block]
        squares = jnp.sum(value * value, axis=1, keepdims=True) + epsilon
        inner = jnp.sum(value * slope, axis=1, keepdims=True)
        proj[block] = ((slope - value * (inner / squares)) * lax.rsqrt(squares)).astype(
            jnp.bfloat16
        )
    copies = []
    head = grad
    for k, cut in enumerate(cuts(width, 256)):
        head[:depth, cut] = dot(turned[...], proj[:, cut])
        copies.append(
            pltpu.make_async_copy(head.at[:depth, cut], head_grad.at[:, cut], sems.at[k])
        )
        copies[-1].start()
    grad_text[...] = dot(proj[:48], matrix[...], NT)[:rows]
    grad_zi = dot(weights[:, :128], zt[...], TN)[:rows]
    unit_image, image_norm = normalize(image[...].astype(jnp.float32))
    grad_image[...] = unproject(grad_zi, unit_image, image_norm)
    for copy in copies:
        copy.wait()


def gathered_plan(
    picture_mean_embeddings,
    caption_tower_summary,
    caption_mapping_matrix,
    picture_match_index,
    sharpness_factor,
    score_shift_term,
):
    rows, width = caption_tower_summary.shape
    depth = caption_mapping_matrix.shape[0]
    half = depth // 2
    core = lax.axis_index("dp") % 2
    total = rows * 32
    smem = pl.BlockSpec(memory_space=pltpu.SMEM)
    vmem = pl.BlockSpec(memory_space=pltpu.VMEM)
    anywhere = pl.BlockSpec(memory_space=pl.ANY)
    f32, bf16 = jnp.float32, jnp.bfloat16
    params = pltpu.CompilerParams(vmem_limit_bytes=24 * 2**20)

    both, own_images, own_texts = pl.pallas_call(
        own_kernel,
        out_shape=(
            jax.ShapeDtypeStruct((2, rows, width), bf16),
            jax.ShapeDtypeStruct((rows + 4, width), bf16),
            jax.ShapeDtypeStruct((rows, width), bf16),
        ),
        scratch_shapes=[pltpu.VMEM((8, width), f32)],
        compiler_params=params,
        name="own_block",
    )(picture_mean_embeddings, caption_tower_summary, picture_match_index[None, :])
    beside = across(both, Y)
    texts = [own_texts, beside[1]]
    texts += [across(own_texts, TEXT_ORDER[1] | bits) for bits in (0, Y)]
    texts = jnp.concatenate(texts)
    images = [own_images] + [across(own_images, IMAGE_ORDER[1] | bits) for bits in (0, Y)]
    digits = [images[0][rows : rows + 2], images[1][rows : rows + 2]]
    images = [images[0][:rows], beside[0], images[1][:rows], images[2][:rows]]
    images = jnp.concatenate(images + digits + [jnp.zeros((4, width), bf16)])

    quarter = lax.dynamic_slice_in_dim(caption_mapping_matrix, core * half, half, 0)
    quarter, texts, images = lax.optimization_barrier((quarter, texts, images))
    near = across(quarter, Y)
    texts = jnp.concatenate([texts, across(texts, TEXT_ORDER[2])])
    count = 4 * rows
    beside = across(images, IMAGE_ORDER[2])
    digits = [images[count : count + 4], beside[count : count + 4]]
    images = jnp.concatenate([images[:count], beside[:count]] + digits)
    texts, images = lax.optimization_barrier((texts, images))
    texts = [texts, across(texts, CORE), across(texts, TEXT_ORDER[4])]
    images = [images, across(images, IMAGE_ORDER[3]), across(images, CORE)]
    near, texts[1] = lax.optimization_barrier((near, texts[1]))
    far = across(near, CORE)
    zt, projected, turned, matrix = pl.pallas_call(
        early_kernel,
        out_shape=(
            jax.ShapeDtypeStruct((total // 2, width), bf16),
            jax.ShapeDtypeStruct((total // 2, width), f32),
            jax.ShapeDtypeStruct((depth, 256), bf16),
            jax.ShapeDtypeStruct((2 * depth, width), bf16),
        ),
        in_specs=[anywhere] * 3 + [vmem] * 2,
        out_specs=(vmem,) * 4,
        scratch_shapes=[pltpu.VMEM((total // 2, width), bf16), pltpu.SemaphoreType.DMA((3,))],
        compiler_params=params,
        name="early_texts",
    )(caption_mapping_matrix, near, far, *texts[:2])
    texts[2], images[1], zt = lax.optimization_barrier((texts[2], images[1], zt))
    texts.append(across(texts[2], CORE))
    images.append(across(images[1], CORE))
    return pl.pallas_call(
        batch_kernel,
        out_shape=(
            jax.ShapeDtypeStruct((rows, width), f32),
            jax.ShapeDtypeStruct((rows, width), f32),
            jax.ShapeDtypeStruct((depth, width), f32),
        ),
        in_specs=[smem] * 2 + [vmem] * 13,
        out_specs=(vmem, vmem, anywhere),
        scratch_shapes=[
            pltpu.VMEM((total, width), bf16),
            pltpu.VMEM((total, width), bf16),
            pltpu.VMEM((total, width), bf16),
            pltpu.VMEM((total, width), f32),
            pltpu.VMEM((total, total), bf16),
            pltpu.VMEM((total, width), f32),
            pltpu.VMEM((depth, total), bf16),
            pltpu.VMEM((total, width), bf16),
            pltpu.SemaphoreType.DMA((8,)),
        ],
        compiler_params=params,
        name="batch",
    )(
        sharpness_factor,
        score_shift_term,
        picture_mean_embeddings,
        zt,
        projected,
        turned,
        matrix,
        *texts,
        *images,
    )


def solution(mesh):
    gathered = dict(mesh.shape) == {"dp": 16, "fsdp": 2}
    per_device = gathered_plan if gathered else ring_plan
    return jax.shard_map(
        per_device,
        mesh=mesh,
        in_specs=(
            P(("dp", "fsdp"), None),
            P(("dp", "fsdp"), None),
            P("fsdp", None),
            P("dp"),
            P(),
            P(),
        ),
        out_specs=(P(("dp", "fsdp"), None), P(("dp", "fsdp"), None), P("fsdp", None)),
        check_vma=False,
    )
```

```python
import functools

import jax
import jax.numpy as jnp
from jax import lax
from jax.experimental import pallas as pl
from jax.experimental.pallas import tpu as pltpu
from jax.sharding import PartitionSpec as P

epsilon = 1e-06


def passed_along(block, axis, distance):
    devices = range(lax.axis_size(axis))
    route = [((i - distance) % len(devices), i) for i in devices]
    return lax.ppermute(block, axis, route)


def normalize(values):
    norms = jnp.sqrt(jnp.sum(values * values, axis=1, keepdims=True) + epsilon)
    return (values / norms, norms)


def unproject(grad_unit, unit, norms):
    return (grad_unit - unit * jnp.sum(unit * grad_unit, axis=1, keepdims=True)) / norms


def ring_plan(
    picture_mean_embeddings,
    caption_tower_summary,
    caption_mapping_matrix,
    picture_match_index,
    sharpness_factor,
    score_shift_term,
):
    rows = caption_tower_summary.shape[0]
    width = caption_mapping_matrix.shape[1]
    cycle_size = lax.axis_size("dp")
    column_count = lax.axis_size("fsdp")
    cycle_index = lax.axis_index("dp")
    column_index = lax.axis_index("fsdp")
    score_multiplier = sharpness_factor[0]
    offset = score_shift_term[0]
    feature_column_set = lax.all_to_all(
        caption_tower_summary, "fsdp", split_axis=1, concat_axis=0, tiled=True
    )
    projected = jnp.dot(
        caption_tower_summary,
        lax.all_gather(caption_mapping_matrix, "fsdp", axis=0, tiled=True),
        preferred_element_type=jnp.float32,
    )
    unit_text, text_norm = normalize(projected)
    text_unit = unit_text.astype(jnp.bfloat16)
    unit_image, image_norm = normalize(picture_mean_embeddings.astype(jnp.float32))
    image_unit = lax.all_gather(unit_image.astype(jnp.bfloat16), "fsdp", axis=0, tiled=True)
    group = image_unit.shape[0]

    def tile(block, text_rows):
        scores = lax.dot_general(
            image_unit, block, (((1,), (1,)), ((), ())), preferred_element_type=jnp.float32
        )
        logits = score_multiplier * scores + offset
        sign = jnp.where(picture_match_index[:, None] == text_rows[None, :], 1.0, -1.0).astype(
            jnp.float32
        )
        weights = (score_multiplier * -sign * jax.nn.sigmoid(-sign * logits)).astype(jnp.bfloat16)
        image_part = jnp.dot(weights, block, preferred_element_type=jnp.float32)
        text_part = lax.dot_general(
            weights, image_unit, (((0,), (0,)), ((), ())), preferred_element_type=jnp.float32
        )
        return (image_part, text_part)

    def rows_of(owner, count):
        return (owner * column_count + column_index) * rows + jnp.arange(count, dtype=jnp.int32)

    image_start = jnp.zeros((group, width), jnp.float32)

    def advance(count, state):
        block, carried, image_sum = state
        owner = (cycle_index - count) % cycle_size
        image_part, text_part = tile(block, rows_of(owner, rows))
        block = passed_along(block, "dp", 1)
        carried = passed_along(carried + text_part, "dp", 1)
        return (block, carried, image_sum + image_part)

    state = (text_unit, jnp.zeros((rows, width), jnp.float32), image_start)
    block, grad_zt, image_sum = lax.fori_loop(0, cycle_size, advance, state)
    grad_zi = lax.psum_scatter(image_sum, "fsdp", scatter_dimension=0, tiled=True)
    grad_image = unproject(grad_zi, unit_image, image_norm)
    grad_proj = unproject(grad_zt, unit_text, text_norm).astype(jnp.bfloat16)
    grad_group = lax.all_gather(grad_proj, "fsdp", axis=0, tiled=True)
    head_part = lax.dot_general(
        feature_column_set, grad_group, (((0,), (0,)), ((), ())), preferred_element_type=jnp.float32
    )
    head_grad = lax.psum(head_part, "dp")
    grad_text = lax.dot_general(
        grad_proj,
        lax.all_gather(caption_mapping_matrix, "fsdp", axis=0, tiled=True),
        (((1,), (1,)), ((), ())),
        preferred_element_type=jnp.float32,
    )
    return (grad_image, grad_text, head_grad)


def across(block, bits):
    count = lax.axis_size("dp") * lax.axis_size("fsdp")
    return lax.ppermute(block, ("dp", "fsdp"), [(i, i ^ bits) for i in range(count)])


Y, CORE, X, Z1, Z2 = 1, 2, 4, 8, 16
IMAGE_ORDER = (Y, Z2, X, Z1, CORE)
TEXT_ORDER = (Y, Z2, Z1, CORE, X)
NT = (((1,), (1,)), ((), ()))
TN = (((0,), (0,)), ((), ()))


def dot(a, b, dims=(((1,), (0,)), ((), ()))):
    return lax.dot_general(a, b, dims, preferred_element_type=jnp.float32)


def cuts(size, step):
    return [slice(k, min(k + step, size)) for k in range(0, size, step)]


def owners(order, shape, axis, rows, place):
    row = lax.broadcasted_iota(jnp.int32, shape, axis)
    block = sum((row >= k * rows).astype(jnp.int32) for k in range(1, shape[axis] // rows))
    owner = jnp.zeros_like(row)
    for k, bits in enumerate(order):
        owner += ((block >> k) & 1) * bits
    return owner ^ place, row - block * rows


def weigh(scores, paired, sharpness, shift):
    logits = sharpness[0] * scores + shift[0]
    sign = jnp.where(paired, 1.0, -1.0)
    return (sharpness[0] * -sign * jax.nn.sigmoid(-sign * logits)).astype(jnp.bfloat16)


def own_kernel(image, text, matrix, match, own, quarter, images, texts, digits, sems):
    rows = images.shape[0]
    count = quarter.shape[0]
    start = pl.multiple_of(lax.rem(lax.axis_index("dp"), 2) * count, 32)
    pairs = ((image, images), (text, texts), (matrix.at[pl.ds(start, count)], quarter))
    copies = [pltpu.make_async_copy(*pair, sems.at[k]) for k, pair in enumerate(pairs)]
    for copy in copies:
        copy.start()
    digits[...] = jnp.zeros(digits.shape, jnp.float32)
    digits[0:1, : match.shape[1]] = (match[...] >> 5).astype(jnp.float32)
    digits[1:2, : match.shape[1]] = (match[...] & 31).astype(jnp.float32)
    spare = digits[: own.shape[1] - rows]
    for copy in copies:
        copy.wait()
    unit_image, _ = normalize(images[...].astype(jnp.float32))
    own[0] = jnp.concatenate([unit_image, spare]).astype(jnp.bfloat16)
    text_rows = texts[...].astype(jnp.float32)
    own[1] = jnp.concatenate([text_rows, jnp.zeros_like(spare)]).astype(jnp.bfloat16)


def pair_indices(rows, total, pieces, side):
    digits = jnp.concatenate([piece[-8:, :128].astype(jnp.float32) for piece in pieces])
    lane = lax.broadcasted_iota(jnp.int32, (1, total), 1)
    group = sum((lane >= k).astype(jnp.int32) for k in range(2 * rows, total, 2 * rows))
    row = lane - group * 2 * rows
    row = jnp.where(side == 0, row, jnp.where(row < rows, row + rows, row - rows))
    chosen = lax.broadcasted_iota(jnp.int32, (128, total), 0) == row
    spread = dot(digits.astype(jnp.bfloat16), chosen.astype(jnp.float32).astype(jnp.bfloat16))
    number = lax.broadcasted_iota(jnp.int32, spread.shape, 0)
    scale = jnp.where(number == 2 * group, 32.0, jnp.where(number == 2 * group + 1, 1.0, 0.0))
    return jnp.sum(scale * spread, axis=0, keepdims=True).astype(jnp.int32)


def project(text, matrix, projected, zt):
    for cut in cuts(matrix.shape[1], 256):
        projected[:, cut] = dot(text[...], matrix[:, cut])
    for block in cuts(text.shape[0], 160):
        value = projected[block]
        inverse = lax.rsqrt(jnp.sum(value * value, axis=1, keepdims=True) + epsilon)
        zt[block] = (value * inverse).astype(jnp.bfloat16)


def early_kernel(matrix_own, matrix_near, matrix_far, *rest):
    texts, rest = rest[:2], rest[2:]
    zt, projected, turned, matrix, text, sems = rest
    depth, near = matrix_own.shape[0], matrix_near.shape[0]
    core, side = lax.rem(lax.axis_index("dp"), 2), lax.axis_index("fsdp")

    other = (1 - side) * depth
    places = (side * depth, other + core * near, other + (1 - core) * near)
    copies = []
    for k, (source, start) in enumerate(zip((matrix_own, matrix_near, matrix_far), places)):
        start = pl.multiple_of(start, 32)
        target = matrix.at[pl.ds(start, source.shape[0])]
        copies.append(pltpu.make_async_copy(source, target, sems.at[k]))
        copies[-1].start()
    count = texts[0].shape[0]
    for k, source in enumerate(texts):
        text[pl.ds(k * count, count)] = source[...]
    for s in (0, 1):

        @pl.when(side == s)
        def _():
            turned[...] = jnp.transpose(text[: turned.shape[1], s * depth : (s + 1) * depth])

    for copy in copies:
        copy.wait()
    project(text, matrix, projected, zt)


def batch_kernel(sharpness, shift, image, zt_early, projected_early, *rest):
    (turned_early, matrix), texts, images, rest = rest[:2], rest[2:6], rest[6:10], rest[10:]
    (grad_image, grad_text, head_grad), rest = rest[:3], rest[3:]
    zi, text, zt, projected, weights, grad, turned, proj, sems = rest
    rows = image.shape[0]
    total, width = zi.shape
    half = total // 2
    depth = head_grad.shape[0]
    group, side = lax.axis_index("dp"), lax.axis_index("fsdp")

    count = total // 4
    for sources, target in ((texts, text), (images, zi)):
        for k, source in enumerate(sources):
            target[pl.ds(k * count, count)] = source[:count]
    match = pair_indices(rows, total, images, side)
    late = pl.ds(half, half)
    project(text.at[late], matrix, projected.at[late], zt.at[late])
    zt[:half] = zt_early[...]
    first = turned_early.shape[1]
    turned[:, :first] = turned_early[...]
    for s in (0, 1):

        @pl.when(side == s)
        def _():
            turned[:, first:] = jnp.transpose(text[first:, s * depth : (s + 1) * depth])

    owner, row = owners(TEXT_ORDER, (total, 1), 0, rows, group * 2 + side)
    ids = owner * rows + row
    for cut in cuts(total, 256):
        scores = dot(zt[...], zi[cut], NT)
        weights[:, cut] = weigh(scores, ids == match[:, cut], sharpness, shift)
    for cut in cuts(width, 256):
        grad[:, cut] = dot(weights[...], zi[:, cut])
    for block in cuts(total, 160):
        value = projected_early[block] if block.stop <= half else projected[block]
        slope = grad[block]
        squares = jnp.sum(value * value, axis=1, keepdims=True) + epsilon
        inner = jnp.sum(value * slope, axis=1, keepdims=True)
        proj[block] = ((slope - value * (inner / squares)) * lax.rsqrt(squares)).astype(
            jnp.bfloat16
        )
    copies = []
    head = grad
    for k, cut in enumerate(cuts(width, 256)):
        head[:depth, cut] = dot(turned[...], proj[:, cut])
        copies.append(
            pltpu.make_async_copy(head.at[:depth, cut], head_grad.at[:, cut], sems.at[k])
        )
        copies[-1].start()
    grad_text[...] = dot(proj[:48], matrix[...], NT)[:rows]
    grad_zi = dot(weights[:, :128], zt[...], TN)[:rows]
    unit_image, image_norm = normalize(image[...].astype(jnp.float32))
    grad_image[...] = unproject(grad_zi, unit_image, image_norm)
    for copy in copies:
        copy.wait()


def gathered_plan(
    picture_mean_embeddings,
    caption_tower_summary,
    caption_mapping_matrix,
    picture_match_index,
    sharpness_factor,
    score_shift_term,
):
    rows, width = caption_tower_summary.shape
    depth = caption_mapping_matrix.shape[0]
    half = depth // 2
    total = rows * 32
    smem = pl.BlockSpec(memory_space=pltpu.SMEM)
    vmem = pl.BlockSpec(memory_space=pltpu.VMEM)
    anywhere = pl.BlockSpec(memory_space=pl.ANY)
    f32, bf16 = jnp.float32, jnp.bfloat16
    params = pltpu.CompilerParams(vmem_limit_bytes=24 * 2**20)

    hbm = pl.BlockSpec(memory_space=pltpu.HBM)
    own, quarter = pl.pallas_call(
        own_kernel,
        out_shape=(
            jax.ShapeDtypeStruct((2, rows + 4, width), bf16),
            jax.ShapeDtypeStruct((half, width), bf16),
        ),
        in_specs=[hbm] * 3 + [vmem],
        out_specs=(vmem, vmem),
        scratch_shapes=[
            pltpu.VMEM((rows, width), bf16),
            pltpu.VMEM((rows, width), bf16),
            pltpu.VMEM((8, width), f32),
            pltpu.SemaphoreType.DMA((3,)),
        ],
        name="own_block",
    )(
        picture_mean_embeddings,
        caption_tower_summary,
        caption_mapping_matrix,
        picture_match_index[None, :],
    )
    first = IMAGE_ORDER[1]
    blocks = [own, across(own, Y), across(own, first), across(own, first | Y)]
    near = across(quarter, Y)
    digits = [block[0, rows : rows + 2] for block in (blocks[0], blocks[2])]
    digits += [jnp.zeros((4, width), bf16)]
    images = jnp.concatenate([block[0, :rows] for block in blocks] + digits)
    texts = jnp.concatenate([block[1, :rows] for block in blocks])
    texts, images = lax.optimization_barrier((texts, images))
    texts = jnp.concatenate([texts, across(texts, TEXT_ORDER[2])])
    count = 4 * rows
    beside = across(images, IMAGE_ORDER[2])
    digits = [images[count : count + 4], beside[count : count + 4]]
    images = jnp.concatenate([images[:count], beside[:count]] + digits)
    texts, images = lax.optimization_barrier((texts, images))
    texts = [texts, across(texts, CORE), across(texts, TEXT_ORDER[4])]
    images = [images, across(images, IMAGE_ORDER[3]), across(images, CORE)]
    near, texts[1] = lax.optimization_barrier((near, texts[1]))
    far = across(near, CORE)
    zt, projected, turned, matrix = pl.pallas_call(
        early_kernel,
        out_shape=(
            jax.ShapeDtypeStruct((total // 2, width), bf16),
            jax.ShapeDtypeStruct((total // 2, width), f32),
            jax.ShapeDtypeStruct((depth, 256), bf16),
            jax.ShapeDtypeStruct((2 * depth, width), bf16),
        ),
        in_specs=[anywhere] * 3 + [vmem] * 2,
        out_specs=(vmem,) * 4,
        scratch_shapes=[pltpu.VMEM((total // 2, width), bf16), pltpu.SemaphoreType.DMA((3,))],
        compiler_params=params,
        name="early_texts",
    )(caption_mapping_matrix, near, far, *texts[:2])
    texts.append(across(texts[2], CORE))
    images.append(across(images[1], CORE))
    return pl.pallas_call(
        batch_kernel,
        out_shape=(
            jax.ShapeDtypeStruct((rows, width), f32),
            jax.ShapeDtypeStruct((rows, width), f32),
            jax.ShapeDtypeStruct((depth, width), f32),
        ),
        in_specs=[smem] * 2 + [vmem] * 13,
        out_specs=(vmem, vmem, anywhere),
        scratch_shapes=[
            pltpu.VMEM((total, width), bf16),
            pltpu.VMEM((total, width), bf16),
            pltpu.VMEM((total, width), bf16),
            pltpu.VMEM((total, width), f32),
            pltpu.VMEM((total, total), bf16),
            pltpu.VMEM((total, width), f32),
            pltpu.VMEM((depth, total), bf16),
            pltpu.VMEM((total, width), bf16),
            pltpu.SemaphoreType.DMA((8,)),
        ],
        compiler_params=params,
        name="batch",
    )(
        sharpness_factor,
        score_shift_term,
        picture_mean_embeddings,
        zt,
        projected,
        turned,
        matrix,
        *texts,
        *images,
    )


def solution(mesh):
    gathered = dict(mesh.shape) == {"dp": 16, "fsdp": 2}
    per_device = gathered_plan if gathered else ring_plan
    return jax.shard_map(
        per_device,
        mesh=mesh,
        in_specs=(
            P(("dp", "fsdp"), None),
            P(("dp", "fsdp"), None),
            P("fsdp", None),
            P("dp"),
            P(),
            P(),
        ),
        out_specs=(P(("dp", "fsdp"), None), P(("dp", "fsdp"), None), P("fsdp", None)),
        check_vma=False,
    )
```

```python
import functools

import jax
import jax.numpy as jnp
from jax import lax
from jax.experimental import pallas as pl
from jax.experimental.pallas import tpu as pltpu
from jax.sharding import PartitionSpec as P

epsilon = 1e-06


def passed_along(block, axis, distance):
    devices = range(lax.axis_size(axis))
    route = [((i - distance) % len(devices), i) for i in devices]
    return lax.ppermute(block, axis, route)


def normalize(values):
    norms = jnp.sqrt(jnp.sum(values * values, axis=1, keepdims=True) + epsilon)
    return (values / norms, norms)


def unproject(grad_unit, unit, norms):
    return (grad_unit - unit * jnp.sum(unit * grad_unit, axis=1, keepdims=True)) / norms


def ring_plan(
    picture_mean_embeddings,
    caption_tower_summary,
    caption_mapping_matrix,
    picture_match_index,
    sharpness_factor,
    score_shift_term,
):
    rows = caption_tower_summary.shape[0]
    width = caption_mapping_matrix.shape[1]
    cycle_size = lax.axis_size("dp")
    column_count = lax.axis_size("fsdp")
    cycle_index = lax.axis_index("dp")
    column_index = lax.axis_index("fsdp")
    score_multiplier = sharpness_factor[0]
    offset = score_shift_term[0]
    feature_column_set = lax.all_to_all(
        caption_tower_summary, "fsdp", split_axis=1, concat_axis=0, tiled=True
    )
    projected = jnp.dot(
        caption_tower_summary,
        lax.all_gather(caption_mapping_matrix, "fsdp", axis=0, tiled=True),
        preferred_element_type=jnp.float32,
    )
    unit_text, text_norm = normalize(projected)
    text_unit = unit_text.astype(jnp.bfloat16)
    unit_image, image_norm = normalize(picture_mean_embeddings.astype(jnp.float32))
    image_unit = lax.all_gather(unit_image.astype(jnp.bfloat16), "fsdp", axis=0, tiled=True)
    group = image_unit.shape[0]

    def tile(block, text_rows):
        scores = lax.dot_general(
            image_unit, block, (((1,), (1,)), ((), ())), preferred_element_type=jnp.float32
        )
        logits = score_multiplier * scores + offset
        sign = jnp.where(picture_match_index[:, None] == text_rows[None, :], 1.0, -1.0).astype(
            jnp.float32
        )
        weights = (score_multiplier * -sign * jax.nn.sigmoid(-sign * logits)).astype(jnp.bfloat16)
        image_part = jnp.dot(weights, block, preferred_element_type=jnp.float32)
        text_part = lax.dot_general(
            weights, image_unit, (((0,), (0,)), ((), ())), preferred_element_type=jnp.float32
        )
        return (image_part, text_part)

    def rows_of(owner, count):
        return (owner * column_count + column_index) * rows + jnp.arange(count, dtype=jnp.int32)

    image_start = jnp.zeros((group, width), jnp.float32)

    def advance(count, state):
        block, carried, image_sum = state
        owner = (cycle_index - count) % cycle_size
        image_part, text_part = tile(block, rows_of(owner, rows))
        block = passed_along(block, "dp", 1)
        carried = passed_along(carried + text_part, "dp", 1)
        return (block, carried, image_sum + image_part)

    state = (text_unit, jnp.zeros((rows, width), jnp.float32), image_start)
    block, grad_zt, image_sum = lax.fori_loop(0, cycle_size, advance, state)
    grad_zi = lax.psum_scatter(image_sum, "fsdp", scatter_dimension=0, tiled=True)
    grad_image = unproject(grad_zi, unit_image, image_norm)
    grad_proj = unproject(grad_zt, unit_text, text_norm).astype(jnp.bfloat16)
    grad_group = lax.all_gather(grad_proj, "fsdp", axis=0, tiled=True)
    head_part = lax.dot_general(
        feature_column_set, grad_group, (((0,), (0,)), ((), ())), preferred_element_type=jnp.float32
    )
    head_grad = lax.psum(head_part, "dp")
    grad_text = lax.dot_general(
        grad_proj,
        lax.all_gather(caption_mapping_matrix, "fsdp", axis=0, tiled=True),
        (((1,), (1,)), ((), ())),
        preferred_element_type=jnp.float32,
    )
    return (grad_image, grad_text, head_grad)


def across(block, bits):
    count = lax.axis_size("dp") * lax.axis_size("fsdp")
    return lax.ppermute(block, ("dp", "fsdp"), [(i, i ^ bits) for i in range(count)])


Y, CORE, X, Z1, Z2 = 1, 2, 4, 8, 16
IMAGE_ORDER = (Y, Z2, X, Z1, CORE)
TEXT_ORDER = (Y, Z2, Z1, CORE, X)
NT = (((1,), (1,)), ((), ()))
TN = (((0,), (0,)), ((), ()))


def dot(a, b, dims=(((1,), (0,)), ((), ()))):
    return lax.dot_general(a, b, dims, preferred_element_type=jnp.float32)


def cuts(size, step):
    return [slice(k, min(k + step, size)) for k in range(0, size, step)]


def owners(order, shape, axis, rows, place):
    row = lax.broadcasted_iota(jnp.int32, shape, axis)
    block = sum((row >= k * rows).astype(jnp.int32) for k in range(1, shape[axis] // rows))
    owner = jnp.zeros_like(row)
    for k, bits in enumerate(order):
        owner += ((block >> k) & 1) * bits
    return owner ^ place, row - block * rows


def weigh(scores, paired, sharpness, shift):
    logits = sharpness[...] * scores + shift[...]
    share = 1.0 / (1.0 + jnp.exp(jnp.where(paired, logits, -logits)))
    return (jnp.where(paired, -sharpness[...], sharpness[...]) * share).astype(jnp.bfloat16)


def own_kernel(image, text, matrix, match, own, quarter, images, texts, indices, digits, sems):
    rows = images.shape[0]
    count = quarter.shape[0]
    start = pl.multiple_of(lax.rem(lax.axis_index("dp"), 2) * count, 32)
    pairs = ((image, images), (text, texts), (match, indices))
    pairs += ((matrix.at[pl.ds(start, count)], quarter),)
    copies = [pltpu.make_async_copy(*pair, sems.at[k]) for k, pair in enumerate(pairs)]
    for copy in copies:
        copy.start()
    for copy in copies[:3]:
        copy.wait()
    width = indices.shape[1]
    digits[...] = jnp.zeros(digits.shape, jnp.float32)
    digits[0:1, :width] = (indices[...] >> 5).astype(jnp.float32)
    digits[1:2, :width] = (indices[...] & 31).astype(jnp.float32)
    spare = digits[: own.shape[1] - rows]
    unit_image, _ = normalize(images[...].astype(jnp.float32))
    own[0] = jnp.concatenate([unit_image, spare]).astype(jnp.bfloat16)
    text_rows = texts[...].astype(jnp.float32)
    own[1] = jnp.concatenate([text_rows, jnp.zeros_like(spare)]).astype(jnp.bfloat16)
    copies[3].wait()


def pair_indices(rows, total, pieces, side):
    digits = jnp.concatenate([piece[-8:, :128].astype(jnp.float32) for piece in pieces])
    lane = lax.broadcasted_iota(jnp.int32, (1, total), 1)
    group = sum((lane >= k).astype(jnp.int32) for k in range(2 * rows, total, 2 * rows))
    row = lane - group * 2 * rows
    row = jnp.where(side == 0, row, jnp.where(row < rows, row + rows, row - rows))
    chosen = lax.broadcasted_iota(jnp.int32, (128, total), 0) == row
    spread = dot(digits.astype(jnp.bfloat16), chosen.astype(jnp.float32).astype(jnp.bfloat16))
    number = lax.broadcasted_iota(jnp.int32, spread.shape, 0)
    scale = jnp.where(number == 2 * group, 32.0, jnp.where(number == 2 * group + 1, 1.0, 0.0))
    return jnp.sum(scale * spread, axis=0, keepdims=True).astype(jnp.int32)


def project(text, matrix, projected, zt):
    projected[...] = dot(text[...], matrix[...])
    for block in cuts(text.shape[0], 160):
        value = projected[block]
        inverse = lax.rsqrt(jnp.sum(value * value, axis=1, keepdims=True) + epsilon)
        zt[block] = (value * inverse).astype(jnp.bfloat16)


def early_kernel(matrix_own, matrix_near, matrix_far, *rest):
    texts, rest = rest[:2], rest[2:]
    zt, projected, turned, matrix, text, sems = rest
    depth, near = matrix_own.shape[0], matrix_near.shape[0]
    core, side = lax.rem(lax.axis_index("dp"), 2), lax.axis_index("fsdp")

    other = (1 - side) * depth
    places = (side * depth, other + core * near, other + (1 - core) * near)
    copies = []
    for k, (source, start) in enumerate(zip((matrix_own, matrix_near, matrix_far), places)):
        start = pl.multiple_of(start, 32)
        target = matrix.at[pl.ds(start, source.shape[0])]
        copies.append(pltpu.make_async_copy(source, target, sems.at[k]))
        copies[-1].start()
    count = texts[0].shape[0]
    for k, source in enumerate(texts):
        text[pl.ds(k * count, count)] = source[...]
    for s in (0, 1):

        @pl.when(side == s)
        def _():
            turned[...] = jnp.transpose(text[: turned.shape[1], s * depth : (s + 1) * depth])

    for copy in copies:
        copy.wait()
    project(text, matrix, projected, zt)


def batch_kernel(sharpness, shift, image, zt_early, projected_early, *rest):
    (turned_early, matrix), texts, images, rest = rest[:2], rest[2:6], rest[6:10], rest[10:]
    (grad_image, grad_text, head_grad), rest = rest[:3], rest[3:]
    zi, text, zt, projected, weights, grad, turned, proj, sems = rest
    rows = image.shape[0]
    total, width = zi.shape
    half = total // 2
    depth = head_grad.shape[0]
    group, side = lax.axis_index("dp"), lax.axis_index("fsdp")

    count = total // 4
    for sources, target in ((texts, text), (images, zi)):
        for k, source in enumerate(sources):
            target[pl.ds(k * count, count)] = source[:count]
    match = pair_indices(rows, total, images, side)
    late = pl.ds(half, half)
    project(text.at[late], matrix, projected.at[late], zt.at[late])
    zt[:half] = zt_early[...]
    first = turned_early.shape[1]
    turned[:, :first] = turned_early[...]
    for s in (0, 1):

        @pl.when(side == s)
        def _():
            turned[:, first:] = jnp.transpose(text[first:, s * depth : (s + 1) * depth])

    owner, row = owners(TEXT_ORDER, (total, 1), 0, rows, group * 2 + side)
    ids = owner * rows + row
    scores = dot(zt[...], zi[...], NT)
    weights[...] = weigh(scores, ids == match, sharpness, shift)
    grad[...] = dot(weights[...], zi[...])
    for block in cuts(total, 160):
        value = projected_early[block] if block.stop <= half else projected[block]
        slope = grad[block]
        squares = jnp.sum(value * value, axis=1, keepdims=True) + epsilon
        inner = jnp.sum(value * slope, axis=1, keepdims=True)
        proj[block] = ((slope - value * (inner / squares)) * lax.rsqrt(squares)).astype(
            jnp.bfloat16
        )
    copies = []
    head = grad
    for k, cut in enumerate(cuts(width, 384)):
        head[:depth, cut] = dot(turned[...], proj[:, cut])
        copies.append(
            pltpu.make_async_copy(head.at[:depth, cut], head_grad.at[:, cut], sems.at[k])
        )
        copies[-1].start()
    grad_text[...] = dot(proj[:48], matrix[...], NT)[:rows]
    grad_zi = dot(weights[:, :128], zt[...], TN)[:rows]
    unit_image, image_norm = normalize(image[...].astype(jnp.float32))
    grad_image[...] = unproject(grad_zi, unit_image, image_norm)
    for copy in copies:
        copy.wait()


def gathered_plan(
    picture_mean_embeddings,
    caption_tower_summary,
    caption_mapping_matrix,
    picture_match_index,
    sharpness_factor,
    score_shift_term,
):
    rows, width = caption_tower_summary.shape
    depth = caption_mapping_matrix.shape[0]
    half = depth // 2
    total = rows * 32
    vmem = pl.BlockSpec(memory_space=pltpu.VMEM)
    anywhere = pl.BlockSpec(memory_space=pl.ANY)
    f32, bf16 = jnp.float32, jnp.bfloat16
    params = pltpu.CompilerParams(vmem_limit_bytes=24 * 2**20)

    hbm = pl.BlockSpec(memory_space=pltpu.HBM)
    own, quarter = pl.pallas_call(
        own_kernel,
        out_shape=(
            jax.ShapeDtypeStruct((2, rows + 4, width), bf16),
            jax.ShapeDtypeStruct((half, width), bf16),
        ),
        in_specs=[hbm] * 4,
        out_specs=(vmem, vmem),
        scratch_shapes=[
            pltpu.VMEM((rows, width), bf16),
            pltpu.VMEM((rows, width), bf16),
            pltpu.VMEM((1, 2 * rows), jnp.int32),
            pltpu.VMEM((8, width), f32),
            pltpu.SemaphoreType.DMA((4,)),
        ],
        name="own_block",
    )(
        picture_mean_embeddings,
        caption_tower_summary,
        caption_mapping_matrix,
        picture_match_index[None, :],
    )
    first = IMAGE_ORDER[1]
    blocks = [own, across(own, Y), across(own, first), across(own, first | Y)]
    near = across(quarter, Y)
    digits = [block[0, rows : rows + 2] for block in (blocks[0], blocks[2])]
    digits += [jnp.zeros((4, width), bf16)]
    images = jnp.concatenate([block[0, :rows] for block in blocks] + digits)
    texts = jnp.concatenate([block[1, :rows] for block in blocks])
    texts, images = lax.optimization_barrier((texts, images))
    texts = jnp.concatenate([texts, across(texts, TEXT_ORDER[2])])
    count = 4 * rows
    beside = across(images, IMAGE_ORDER[2])
    digits = [images[count : count + 4], beside[count : count + 4]]
    images = jnp.concatenate([images[:count], beside[:count]] + digits)
    texts, images = lax.optimization_barrier((texts, images))
    texts = [texts, across(texts, CORE), across(texts, TEXT_ORDER[4])]
    images = [images, across(images, IMAGE_ORDER[3]), across(images, CORE)]
    near, texts[1] = lax.optimization_barrier((near, texts[1]))
    far = across(near, CORE)
    zt, projected, turned, matrix = pl.pallas_call(
        early_kernel,
        out_shape=(
            jax.ShapeDtypeStruct((total // 2, width), bf16),
            jax.ShapeDtypeStruct((total // 2, width), f32),
            jax.ShapeDtypeStruct((depth, 256), bf16),
            jax.ShapeDtypeStruct((2 * depth, width), bf16),
        ),
        in_specs=[anywhere] * 3 + [vmem] * 2,
        out_specs=(vmem,) * 4,
        scratch_shapes=[pltpu.VMEM((total // 2, width), bf16), pltpu.SemaphoreType.DMA((3,))],
        compiler_params=params,
        name="early_texts",
    )(caption_mapping_matrix, near, far, *texts[:2])
    texts.append(across(texts[2], CORE))
    images.append(across(images[1], CORE))
    return pl.pallas_call(
        batch_kernel,
        out_shape=(
            jax.ShapeDtypeStruct((rows, width), f32),
            jax.ShapeDtypeStruct((rows, width), f32),
            jax.ShapeDtypeStruct((depth, width), f32),
        ),
        in_specs=[vmem] * 15,
        out_specs=(vmem, vmem, anywhere),
        scratch_shapes=[
            pltpu.VMEM((total, width), bf16),
            pltpu.VMEM((total, width), bf16),
            pltpu.VMEM((total, width), bf16),
            pltpu.VMEM((total, width), f32),
            pltpu.VMEM((total, total), bf16),
            pltpu.VMEM((total, width), f32),
            pltpu.VMEM((depth, total), bf16),
            pltpu.VMEM((total, width), bf16),
            pltpu.SemaphoreType.DMA((8,)),
        ],
        compiler_params=params,
        name="batch",
    )(
        sharpness_factor[None],
        score_shift_term[None],
        picture_mean_embeddings,
        zt,
        projected,
        turned,
        matrix,
        *texts,
        *images,
    )


def solution(mesh):
    gathered = dict(mesh.shape) == {"dp": 16, "fsdp": 2}
    per_device = gathered_plan if gathered else ring_plan
    return jax.shard_map(
        per_device,
        mesh=mesh,
        in_specs=(
            P(("dp", "fsdp"), None),
            P(("dp", "fsdp"), None),
            P("fsdp", None),
            P("dp"),
            P(),
            P(),
        ),
        out_specs=(P(("dp", "fsdp"), None), P(("dp", "fsdp"), None), P("fsdp", None)),
        check_vma=False,
    )
```

```python
import functools

import jax
import jax.numpy as jnp
from jax import lax
from jax.experimental import pallas as pl
from jax.experimental.pallas import tpu as pltpu
from jax.sharding import PartitionSpec as P

epsilon = 1e-06


def passed_along(block, axis, distance):
    devices = range(lax.axis_size(axis))
    route = [((i - distance) % len(devices), i) for i in devices]
    return lax.ppermute(block, axis, route)


def normalize(values):
    norms = jnp.sqrt(jnp.sum(values * values, axis=1, keepdims=True) + epsilon)
    return (values / norms, norms)


def unproject(grad_unit, unit, norms):
    return (grad_unit - unit * jnp.sum(unit * grad_unit, axis=1, keepdims=True)) / norms


def ring_plan(
    picture_mean_embeddings,
    caption_tower_summary,
    caption_mapping_matrix,
    picture_match_index,
    sharpness_factor,
    score_shift_term,
):
    rows = caption_tower_summary.shape[0]
    width = caption_mapping_matrix.shape[1]
    cycle_size = lax.axis_size("dp")
    column_count = lax.axis_size("fsdp")
    cycle_index = lax.axis_index("dp")
    column_index = lax.axis_index("fsdp")
    score_multiplier = sharpness_factor[0]
    offset = score_shift_term[0]
    feature_column_set = lax.all_to_all(
        caption_tower_summary, "fsdp", split_axis=1, concat_axis=0, tiled=True
    )
    projected = jnp.dot(
        caption_tower_summary,
        lax.all_gather(caption_mapping_matrix, "fsdp", axis=0, tiled=True),
        preferred_element_type=jnp.float32,
    )
    unit_text, text_norm = normalize(projected)
    text_unit = unit_text.astype(jnp.bfloat16)
    unit_image, image_norm = normalize(picture_mean_embeddings.astype(jnp.float32))
    image_unit = lax.all_gather(unit_image.astype(jnp.bfloat16), "fsdp", axis=0, tiled=True)
    group = image_unit.shape[0]

    def tile(block, text_rows):
        scores = lax.dot_general(
            image_unit, block, (((1,), (1,)), ((), ())), preferred_element_type=jnp.float32
        )
        logits = score_multiplier * scores + offset
        sign = jnp.where(picture_match_index[:, None] == text_rows[None, :], 1.0, -1.0).astype(
            jnp.float32
        )
        weights = (score_multiplier * -sign * jax.nn.sigmoid(-sign * logits)).astype(jnp.bfloat16)
        image_part = jnp.dot(weights, block, preferred_element_type=jnp.float32)
        text_part = lax.dot_general(
            weights, image_unit, (((0,), (0,)), ((), ())), preferred_element_type=jnp.float32
        )
        return (image_part, text_part)

    def rows_of(owner, count):
        return (owner * column_count + column_index) * rows + jnp.arange(count, dtype=jnp.int32)

    image_start = jnp.zeros((group, width), jnp.float32)

    def advance(count, state):
        block, carried, image_sum = state
        owner = (cycle_index - count) % cycle_size
        image_part, text_part = tile(block, rows_of(owner, rows))
        block = passed_along(block, "dp", 1)
        carried = passed_along(carried + text_part, "dp", 1)
        return (block, carried, image_sum + image_part)

    state = (text_unit, jnp.zeros((rows, width), jnp.float32), image_start)
    block, grad_zt, image_sum = lax.fori_loop(0, cycle_size, advance, state)
    grad_zi = lax.psum_scatter(image_sum, "fsdp", scatter_dimension=0, tiled=True)
    grad_image = unproject(grad_zi, unit_image, image_norm)
    grad_proj = unproject(grad_zt, unit_text, text_norm).astype(jnp.bfloat16)
    grad_group = lax.all_gather(grad_proj, "fsdp", axis=0, tiled=True)
    head_part = lax.dot_general(
        feature_column_set, grad_group, (((0,), (0,)), ((), ())), preferred_element_type=jnp.float32
    )
    head_grad = lax.psum(head_part, "dp")
    grad_text = lax.dot_general(
        grad_proj,
        lax.all_gather(caption_mapping_matrix, "fsdp", axis=0, tiled=True),
        (((1,), (1,)), ((), ())),
        preferred_element_type=jnp.float32,
    )
    return (grad_image, grad_text, head_grad)


def across(block, bits):
    count = lax.axis_size("dp") * lax.axis_size("fsdp")
    return lax.ppermute(block, ("dp", "fsdp"), [(i, i ^ bits) for i in range(count)])


Y, CORE, X, Z1, Z2 = 1, 2, 4, 8, 16
IMAGE_ORDER = (Y, Z2, X, Z1, CORE)
TEXT_ORDER = (Y, Z2, Z1, CORE, X)
NT = (((1,), (1,)), ((), ()))
TN = (((0,), (0,)), ((), ()))


def dot(a, b, dims=(((1,), (0,)), ((), ()))):
    return lax.dot_general(a, b, dims, preferred_element_type=jnp.float32)


def cuts(size, step):
    return [slice(k, min(k + step, size)) for k in range(0, size, step)]


def owners(order, shape, axis, rows, place):
    row = lax.broadcasted_iota(jnp.int32, shape, axis)
    block = sum((row >= k * rows).astype(jnp.int32) for k in range(1, shape[axis] // rows))
    owner = jnp.zeros_like(row)
    for k, bits in enumerate(order):
        owner += ((block >> k) & 1) * bits
    return owner ^ place, row - block * rows


def weigh(scores, paired, sharpness, shift):
    logits = sharpness[0] * scores + shift[0]
    share = 1.0 / (1.0 + jnp.exp(jnp.where(paired, logits, -logits)))
    return (jnp.where(paired, -sharpness[0], sharpness[0]) * share).astype(jnp.bfloat16)


def own_kernel(image, text, matrix, match, own, quarter, images, texts, indices, digits, sems):
    rows = images.shape[0]
    count = quarter.shape[0]
    start = pl.multiple_of(lax.rem(lax.axis_index("dp"), 2) * count, 32)
    pairs = ((image, images), (text, texts), (match, indices))
    pairs += ((matrix.at[pl.ds(start, count)], quarter),)
    copies = [pltpu.make_async_copy(*pair, sems.at[k]) for k, pair in enumerate(pairs)]
    for copy in copies:
        copy.start()
    for copy in copies[:3]:
        copy.wait()
    width = indices.shape[1]
    digits[...] = jnp.zeros(digits.shape, jnp.float32)
    digits[0:1, :width] = (indices[...] >> 5).astype(jnp.float32)
    digits[1:2, :width] = (indices[...] & 31).astype(jnp.float32)
    spare = digits[: own.shape[1] - rows]
    unit_image, _ = normalize(images[...].astype(jnp.float32))
    own[0] = jnp.concatenate([unit_image, spare]).astype(jnp.bfloat16)
    text_rows = texts[...].astype(jnp.float32)
    own[1] = jnp.concatenate([text_rows, jnp.zeros_like(spare)]).astype(jnp.bfloat16)
    copies[3].wait()


def pair_indices(rows, total, pieces, side):
    digits = jnp.concatenate([piece[-8:, :128].astype(jnp.float32) for piece in pieces])
    lane = lax.broadcasted_iota(jnp.int32, (1, total), 1)
    group = sum((lane >= k).astype(jnp.int32) for k in range(2 * rows, total, 2 * rows))
    row = lane - group * 2 * rows
    row = jnp.where(side == 0, row, jnp.where(row < rows, row + rows, row - rows))
    chosen = lax.broadcasted_iota(jnp.int32, (128, total), 0) == row
    spread = dot(digits.astype(jnp.bfloat16), chosen.astype(jnp.float32).astype(jnp.bfloat16))
    number = lax.broadcasted_iota(jnp.int32, spread.shape, 0)
    scale = jnp.where(number == 2 * group, 32.0, jnp.where(number == 2 * group + 1, 1.0, 0.0))
    return jnp.sum(scale * spread, axis=0, keepdims=True).astype(jnp.int32)


def project(text, matrix, projected, zt):
    projected[...] = dot(text[...], matrix[...])
    for block in cuts(text.shape[0], 160):
        value = projected[block]
        inverse = lax.rsqrt(jnp.sum(value * value, axis=1, keepdims=True) + epsilon)
        zt[block] = (value * inverse).astype(jnp.bfloat16)


def early_kernel(matrix_own, matrix_near, matrix_far, *rest):
    texts, rest = rest[:2], rest[2:]
    zt, projected, turned, matrix, text, sems = rest
    depth, near = matrix_own.shape[0], matrix_near.shape[0]
    core, side = lax.rem(lax.axis_index("dp"), 2), lax.axis_index("fsdp")

    other = (1 - side) * depth
    places = (side * depth, other + core * near, other + (1 - core) * near)
    copies = []
    for k, (source, start) in enumerate(zip((matrix_own, matrix_near, matrix_far), places)):
        start = pl.multiple_of(start, 32)
        target = matrix.at[pl.ds(start, source.shape[0])]
        copies.append(pltpu.make_async_copy(source, target, sems.at[k]))
        copies[-1].start()
    count = texts[0].shape[0]
    for k, source in enumerate(texts):
        text[pl.ds(k * count, count)] = source[...]
    for s in (0, 1):

        @pl.when(side == s)
        def _():
            turned[...] = jnp.transpose(text[: turned.shape[1], s * depth : (s + 1) * depth])

    for copy in copies:
        copy.wait()
    project(text, matrix, projected, zt)


def batch_kernel(sharpness_hbm, shift_hbm, image, zt_early, projected_early, *rest):
    (turned_early, matrix), texts, images, rest = rest[:2], rest[2:6], rest[6:10], rest[10:]
    (grad_image, grad_text, head_grad), rest = rest[:3], rest[3:]
    zi, text, zt, projected, weights, grad, turned, proj, sharpness, shift, sems = rest
    rows = image.shape[0]
    total, width = zi.shape
    half = total // 2
    depth = head_grad.shape[0]
    group, side = lax.axis_index("dp"), lax.axis_index("fsdp")
    copies = [
        pltpu.make_async_copy(sharpness_hbm, sharpness, sems.at[0]),
        pltpu.make_async_copy(shift_hbm, shift, sems.at[1]),
    ]
    for copy in copies:
        copy.start()

    count = total // 4
    for k, source in enumerate(images):
        zi[pl.ds(k * count, count)] = source[:count]
    zt[:half] = zt_early[...]
    early_scores = dot(zt_early[...], zi[...], NT)
    for k, source in enumerate(texts):
        text[pl.ds(k * count, count)] = source[...]
    first = turned_early.shape[1]
    turned[:, :first] = turned_early[...]
    for s in (0, 1):

        @pl.when(side == s)
        def _():
            turned[:, first:] = jnp.transpose(text[first:, s * depth : (s + 1) * depth])

    match = pair_indices(rows, total, images, side)
    owner, row = owners(TEXT_ORDER, (total, 1), 0, rows, group * 2 + side)
    paired = owner * rows + row == match
    for copy in copies:
        copy.wait()

    def unprojected(value, slope):
        squares = jnp.sum(value * value, axis=1, keepdims=True) + epsilon
        inner = jnp.sum(value * slope, axis=1, keepdims=True)
        return ((slope - value * (inner / squares)) * lax.rsqrt(squares)).astype(jnp.bfloat16)

    projected[...] = dot(text[half:], matrix[...])
    weights[:half] = weigh(early_scores, paired[:half], sharpness, shift)
    value = projected[...]
    inverse = lax.rsqrt(jnp.sum(value * value, axis=1, keepdims=True) + epsilon)
    zt[half:] = (value * inverse).astype(jnp.bfloat16)
    grad[:half] = dot(weights[:half], zi[...])
    late_scores = dot(zt[half:], zi[...], NT)
    proj[:half] = unprojected(projected_early[...], grad[:half])
    weights[half:] = weigh(late_scores, paired[half:], sharpness, shift)
    grad_text[...] = dot(proj[:48], matrix[...], NT)[:rows]
    grad[half:] = dot(weights[half:], zi[...])
    grad_zi = dot(weights[:, :128], zt[...], TN)[:rows]
    proj[half:] = unprojected(projected[...], grad[half:])
    copies = []
    head = grad
    for k, cut in enumerate(cuts(width, 384)):
        head[:depth, cut] = dot(turned[...], proj[:, cut])
        copies.append(
            pltpu.make_async_copy(head.at[:depth, cut], head_grad.at[:, cut], sems.at[k])
        )
        copies[-1].start()
    unit_image, image_norm = normalize(image[...].astype(jnp.float32))
    grad_image[...] = unproject(grad_zi, unit_image, image_norm)
    for copy in copies:
        copy.wait()


def gathered_plan(
    picture_mean_embeddings,
    caption_tower_summary,
    caption_mapping_matrix,
    picture_match_index,
    sharpness_factor,
    score_shift_term,
):
    rows, width = caption_tower_summary.shape
    depth = caption_mapping_matrix.shape[0]
    half = depth // 2
    total = rows * 32
    vmem = pl.BlockSpec(memory_space=pltpu.VMEM)
    anywhere = pl.BlockSpec(memory_space=pl.ANY)
    f32, bf16 = jnp.float32, jnp.bfloat16
    params = pltpu.CompilerParams(vmem_limit_bytes=24 * 2**20)

    hbm = pl.BlockSpec(memory_space=pltpu.HBM)
    own, quarter = pl.pallas_call(
        own_kernel,
        out_shape=(
            jax.ShapeDtypeStruct((2, rows + 4, width), bf16),
            jax.ShapeDtypeStruct((half, width), bf16),
        ),
        in_specs=[hbm] * 4,
        out_specs=(vmem, vmem),
        scratch_shapes=[
            pltpu.VMEM((rows, width), bf16),
            pltpu.VMEM((rows, width), bf16),
            pltpu.VMEM((1, 2 * rows), jnp.int32),
            pltpu.VMEM((8, width), f32),
            pltpu.SemaphoreType.DMA((4,)),
        ],
        name="own_block",
    )(
        picture_mean_embeddings,
        caption_tower_summary,
        caption_mapping_matrix,
        picture_match_index[None, :],
    )
    first = IMAGE_ORDER[1]
    blocks = [own, across(own, Y), across(own, first), across(own, first | Y)]
    near = across(quarter, Y)
    digits = [block[0, rows : rows + 2] for block in (blocks[0], blocks[2])]
    digits += [jnp.zeros((4, width), bf16)]
    images = jnp.concatenate([block[0, :rows] for block in blocks] + digits)
    texts = jnp.concatenate([block[1, :rows] for block in blocks])
    texts, images = lax.optimization_barrier((texts, images))
    texts = jnp.concatenate([texts, across(texts, TEXT_ORDER[2])])
    count = 4 * rows
    beside = across(images, IMAGE_ORDER[2])
    digits = [images[count : count + 4], beside[count : count + 4]]
    images = jnp.concatenate([images[:count], beside[:count]] + digits)
    texts, images = lax.optimization_barrier((texts, images))
    texts = [texts, across(texts, CORE), across(texts, TEXT_ORDER[4])]
    images = [images, across(images, IMAGE_ORDER[3]), across(images, CORE)]
    near, texts[1] = lax.optimization_barrier((near, texts[1]))
    far = across(near, CORE)
    zt, projected, turned, matrix = pl.pallas_call(
        early_kernel,
        out_shape=(
            jax.ShapeDtypeStruct((total // 2, width), bf16),
            jax.ShapeDtypeStruct((total // 2, width), f32),
            jax.ShapeDtypeStruct((depth, 256), bf16),
            jax.ShapeDtypeStruct((2 * depth, width), bf16),
        ),
        in_specs=[anywhere] * 3 + [vmem] * 2,
        out_specs=(vmem,) * 4,
        scratch_shapes=[pltpu.VMEM((total // 2, width), bf16), pltpu.SemaphoreType.DMA((3,))],
        compiler_params=params,
        name="early_texts",
    )(caption_mapping_matrix, near, far, *texts[:2])
    texts.append(across(texts[2], CORE))
    images.append(across(images[1], CORE))
    return pl.pallas_call(
        batch_kernel,
        out_shape=(
            jax.ShapeDtypeStruct((rows, width), f32),
            jax.ShapeDtypeStruct((rows, width), f32),
            jax.ShapeDtypeStruct((depth, width), f32),
        ),
        in_specs=[hbm] * 2 + [vmem] * 13,
        out_specs=(vmem, vmem, anywhere),
        scratch_shapes=[
            pltpu.VMEM((total, width), bf16),
            pltpu.VMEM((total, width), bf16),
            pltpu.VMEM((total, width), bf16),
            pltpu.VMEM((total // 2, width), f32),
            pltpu.VMEM((total, total), bf16),
            pltpu.VMEM((total, width), f32),
            pltpu.VMEM((depth, total), bf16),
            pltpu.VMEM((total, width), bf16),
            pltpu.SMEM((1,), f32),
            pltpu.SMEM((1,), f32),
            pltpu.SemaphoreType.DMA((4,)),
        ],
        compiler_params=params,
        name="batch",
    )(
        sharpness_factor,
        score_shift_term,
        picture_mean_embeddings,
        zt,
        projected,
        turned,
        matrix,
        *texts,
        *images,
    )


def solution(mesh):
    gathered = dict(mesh.shape) == {"dp": 16, "fsdp": 2}
    per_device = gathered_plan if gathered else ring_plan
    return jax.shard_map(
        per_device,
        mesh=mesh,
        in_specs=(
            P(("dp", "fsdp"), None),
            P(("dp", "fsdp"), None),
            P("fsdp", None),
            P("dp"),
            P(),
            P(),
        ),
        out_specs=(P(("dp", "fsdp"), None), P(("dp", "fsdp"), None), P("fsdp", None)),
        check_vma=False,
    )
```

```python
import functools

import jax
import jax.numpy as jnp
from jax import lax
from jax.experimental import pallas as pl
from jax.experimental.pallas import tpu as pltpu
from jax.sharding import PartitionSpec as P

epsilon = 1e-06


def passed_along(block, axis, distance):
    devices = range(lax.axis_size(axis))
    route = [((i - distance) % len(devices), i) for i in devices]
    return lax.ppermute(block, axis, route)


def normalize(values):
    norms = jnp.sqrt(jnp.sum(values * values, axis=1, keepdims=True) + epsilon)
    return (values / norms, norms)


def unproject(grad_unit, unit, norms):
    return (grad_unit - unit * jnp.sum(unit * grad_unit, axis=1, keepdims=True)) / norms


def ring_plan(
    picture_mean_embeddings,
    caption_tower_summary,
    caption_mapping_matrix,
    picture_match_index,
    sharpness_factor,
    score_shift_term,
):
    rows = caption_tower_summary.shape[0]
    width = caption_mapping_matrix.shape[1]
    cycle_size = lax.axis_size("dp")
    column_count = lax.axis_size("fsdp")
    cycle_index = lax.axis_index("dp")
    column_index = lax.axis_index("fsdp")
    score_multiplier = sharpness_factor[0]
    offset = score_shift_term[0]
    feature_column_set = lax.all_to_all(
        caption_tower_summary, "fsdp", split_axis=1, concat_axis=0, tiled=True
    )
    projected = jnp.dot(
        caption_tower_summary,
        lax.all_gather(caption_mapping_matrix, "fsdp", axis=0, tiled=True),
        preferred_element_type=jnp.float32,
    )
    unit_text, text_norm = normalize(projected)
    text_unit = unit_text.astype(jnp.bfloat16)
    unit_image, image_norm = normalize(picture_mean_embeddings.astype(jnp.float32))
    image_unit = lax.all_gather(unit_image.astype(jnp.bfloat16), "fsdp", axis=0, tiled=True)
    group = image_unit.shape[0]

    def tile(block, text_rows):
        scores = lax.dot_general(
            image_unit, block, (((1,), (1,)), ((), ())), preferred_element_type=jnp.float32
        )
        logits = score_multiplier * scores + offset
        sign = jnp.where(picture_match_index[:, None] == text_rows[None, :], 1.0, -1.0).astype(
            jnp.float32
        )
        weights = (score_multiplier * -sign * jax.nn.sigmoid(-sign * logits)).astype(jnp.bfloat16)
        image_part = jnp.dot(weights, block, preferred_element_type=jnp.float32)
        text_part = lax.dot_general(
            weights, image_unit, (((0,), (0,)), ((), ())), preferred_element_type=jnp.float32
        )
        return (image_part, text_part)

    def rows_of(owner, count):
        return (owner * column_count + column_index) * rows + jnp.arange(count, dtype=jnp.int32)

    image_start = jnp.zeros((group, width), jnp.float32)

    def advance(count, state):
        block, carried, image_sum = state
        owner = (cycle_index - count) % cycle_size
        image_part, text_part = tile(block, rows_of(owner, rows))
        block = passed_along(block, "dp", 1)
        carried = passed_along(carried + text_part, "dp", 1)
        return (block, carried, image_sum + image_part)

    state = (text_unit, jnp.zeros((rows, width), jnp.float32), image_start)
    block, grad_zt, image_sum = lax.fori_loop(0, cycle_size, advance, state)
    grad_zi = lax.psum_scatter(image_sum, "fsdp", scatter_dimension=0, tiled=True)
    grad_image = unproject(grad_zi, unit_image, image_norm)
    grad_proj = unproject(grad_zt, unit_text, text_norm).astype(jnp.bfloat16)
    grad_group = lax.all_gather(grad_proj, "fsdp", axis=0, tiled=True)
    head_part = lax.dot_general(
        feature_column_set, grad_group, (((0,), (0,)), ((), ())), preferred_element_type=jnp.float32
    )
    head_grad = lax.psum(head_part, "dp")
    grad_text = lax.dot_general(
        grad_proj,
        lax.all_gather(caption_mapping_matrix, "fsdp", axis=0, tiled=True),
        (((1,), (1,)), ((), ())),
        preferred_element_type=jnp.float32,
    )
    return (grad_image, grad_text, head_grad)


def across(block, bits):
    count = lax.axis_size("dp") * lax.axis_size("fsdp")
    return lax.ppermute(block, ("dp", "fsdp"), [(i, i ^ bits) for i in range(count)])


Y, CORE, X, Z1, Z2 = 1, 2, 4, 8, 16
IMAGE_ORDER = (Y, Z2, X, Z1, CORE)
TEXT_ORDER = (Y, Z2, Z1, CORE, X)
NT = (((1,), (1,)), ((), ()))
TN = (((0,), (0,)), ((), ()))


def dot(a, b, dims=(((1,), (0,)), ((), ()))):
    return lax.dot_general(a, b, dims, preferred_element_type=jnp.float32)


def cuts(size, step):
    return [slice(k, min(k + step, size)) for k in range(0, size, step)]


def owners(order, shape, axis, rows, place):
    row = lax.broadcasted_iota(jnp.int32, shape, axis)
    block = sum((row >= k * rows).astype(jnp.int32) for k in range(1, shape[axis] // rows))
    owner = jnp.zeros_like(row)
    for k, bits in enumerate(order):
        owner += ((block >> k) & 1) * bits
    return owner ^ place, row - block * rows


def weigh(scores, paired, scalars):
    sharpness, shift = scalars[:, 0:1], scalars[:, 1:2]
    logits = sharpness * scores + shift
    share = 1.0 / (1.0 + jnp.exp(jnp.where(paired, logits, -logits)))
    return (jnp.where(paired, -sharpness, sharpness) * share).astype(jnp.bfloat16)


def own_kernel(image, text, matrix, match, own, quarter, images, texts, indices, digits, sems):
    rows = images.shape[0]
    count = quarter.shape[0]
    start = pl.multiple_of(lax.rem(lax.axis_index("dp"), 2) * count, 32)
    pairs = ((image, images), (text, texts), (match, indices))
    pairs += ((matrix.at[pl.ds(start, count)], quarter),)
    copies = [pltpu.make_async_copy(*pair, sems.at[k]) for k, pair in enumerate(pairs)]
    for copy in copies:
        copy.start()
    for copy in copies[:3]:
        copy.wait()
    width = indices.shape[1]
    digits[...] = jnp.zeros(digits.shape, jnp.float32)
    digits[0:1, :width] = (indices[...] >> 5).astype(jnp.float32)
    digits[1:2, :width] = (indices[...] & 31).astype(jnp.float32)
    spare = digits[: own.shape[1] - rows]
    unit_image, _ = normalize(images[...].astype(jnp.float32))
    own[0] = jnp.concatenate([unit_image, spare]).astype(jnp.bfloat16)
    text_rows = texts[...].astype(jnp.float32)
    own[1] = jnp.concatenate([text_rows, jnp.zeros_like(spare)]).astype(jnp.bfloat16)
    copies[3].wait()


def pair_indices(rows, total, pieces, side):
    digits = jnp.concatenate([piece[-8:, :128].astype(jnp.float32) for piece in pieces])
    lane = lax.broadcasted_iota(jnp.int32, (1, total), 1)
    group = sum((lane >= k).astype(jnp.int32) for k in range(2 * rows, total, 2 * rows))
    row = lane - group * 2 * rows
    row = jnp.where(side == 0, row, jnp.where(row < rows, row + rows, row - rows))
    chosen = lax.broadcasted_iota(jnp.int32, (128, total), 0) == row
    spread = dot(digits.astype(jnp.bfloat16), chosen.astype(jnp.float32).astype(jnp.bfloat16))
    number = lax.broadcasted_iota(jnp.int32, spread.shape, 0)
    scale = jnp.where(number == 2 * group, 32.0, jnp.where(number == 2 * group + 1, 1.0, 0.0))
    return jnp.sum(scale * spread, axis=0, keepdims=True).astype(jnp.int32)


def project(text, matrix, projected, zt):
    for cut in cuts(matrix.shape[1], 256):
        projected[:, cut] = dot(text[...], matrix[:, cut])
    for block in cuts(text.shape[0], 160):
        value = projected[block]
        inverse = lax.rsqrt(jnp.sum(value * value, axis=1, keepdims=True) + epsilon)
        zt[block] = (value * inverse).astype(jnp.bfloat16)


def early_kernel(matrix_own, matrix_near, matrix_far, *rest):
    texts, rest = rest[:2], rest[2:]
    zt, projected, turned, matrix, text, sems = rest
    depth, near = matrix_own.shape[0], matrix_near.shape[0]
    core, side = lax.rem(lax.axis_index("dp"), 2), lax.axis_index("fsdp")

    other = (1 - side) * depth
    places = (side * depth, other + core * near, other + (1 - core) * near)
    copies = []
    for k, (source, start) in enumerate(zip((matrix_own, matrix_near, matrix_far), places)):
        start = pl.multiple_of(start, 32)
        target = matrix.at[pl.ds(start, source.shape[0])]
        copies.append(pltpu.make_async_copy(source, target, sems.at[k]))
        copies[-1].start()
    count = texts[0].shape[0]
    for k, source in enumerate(texts):
        text[pl.ds(k * count, count)] = source[...]
    for s in (0, 1):

        @pl.when(side == s)
        def _():
            turned[...] = jnp.transpose(text[: turned.shape[1], s * depth : (s + 1) * depth])

    for copy in copies:
        copy.wait()
    project(text, matrix, projected, zt)


def batch_kernel(scalars, image, zt_early, projected_early, *rest):
    (turned_early, matrix), texts, images, rest = rest[:2], rest[2:6], rest[6:10], rest[10:]
    (grad_image, grad_text, head_grad), rest = rest[:3], rest[3:]
    zi, text, zt, projected, weights, grad, turned, proj, sems = rest
    rows = image.shape[0]
    total, width = zi.shape
    half = total // 2
    depth = head_grad.shape[0]
    group, side = lax.axis_index("dp"), lax.axis_index("fsdp")

    count = total // 4
    for sources, target in ((texts, text), (images, zi)):
        for k, source in enumerate(sources):
            target[pl.ds(k * count, count)] = source[:count]
    match = pair_indices(rows, total, images, side)
    late = pl.ds(half, half)
    project(text.at[late], matrix, projected.at[late], zt.at[late])
    zt[:half] = zt_early[...]
    first = turned_early.shape[1]
    turned[:, :first] = turned_early[...]
    for s in (0, 1):

        @pl.when(side == s)
        def _():
            turned[:, first:] = jnp.transpose(text[first:, s * depth : (s + 1) * depth])

    owner, row = owners(TEXT_ORDER, (total, 1), 0, rows, group * 2 + side)
    ids = owner * rows + row
    for cut in cuts(total, 256):
        scores = dot(zt[...], zi[cut], NT)
        weights[:, cut] = weigh(scores, ids == match[:, cut], scalars)
    for cut in cuts(width, 256):
        grad[:, cut] = dot(weights[...], zi[:, cut])
    for block in cuts(total, 160):
        value = projected_early[block] if block.stop <= half else projected[block]
        slope = grad[block]
        squares = jnp.sum(value * value, axis=1, keepdims=True) + epsilon
        inner = jnp.sum(value * slope, axis=1, keepdims=True)
        proj[block] = ((slope - value * (inner / squares)) * lax.rsqrt(squares)).astype(
            jnp.bfloat16
        )
    copies = []
    head = grad
    for k, cut in enumerate(cuts(width, 384)):
        head[:depth, cut] = dot(turned[...], proj[:, cut])
        copies.append(
            pltpu.make_async_copy(head.at[:depth, cut], head_grad.at[:, cut], sems.at[k])
        )
        copies[-1].start()
    grad_text[...] = dot(proj[:48], matrix[...], NT)[:rows]
    grad_zi = dot(weights[:, :128], zt[...], TN)[:rows]
    unit_image, image_norm = normalize(image[...].astype(jnp.float32))
    grad_image[...] = unproject(grad_zi, unit_image, image_norm)
    for copy in copies:
        copy.wait()


def gathered_plan(
    picture_mean_embeddings,
    caption_tower_summary,
    caption_mapping_matrix,
    picture_match_index,
    sharpness_factor,
    score_shift_term,
):
    rows, width = caption_tower_summary.shape
    depth = caption_mapping_matrix.shape[0]
    half = depth // 2
    total = rows * 32
    vmem = pl.BlockSpec(memory_space=pltpu.VMEM)
    anywhere = pl.BlockSpec(memory_space=pl.ANY)
    f32, bf16 = jnp.float32, jnp.bfloat16
    params = pltpu.CompilerParams(vmem_limit_bytes=24 * 2**20)

    hbm = pl.BlockSpec(memory_space=pltpu.HBM)
    own, quarter = pl.pallas_call(
        own_kernel,
        out_shape=(
            jax.ShapeDtypeStruct((2, rows + 4, width), bf16),
            jax.ShapeDtypeStruct((half, width), bf16),
        ),
        in_specs=[hbm] * 4,
        out_specs=(vmem, vmem),
        scratch_shapes=[
            pltpu.VMEM((rows, width), bf16),
            pltpu.VMEM((rows, width), bf16),
            pltpu.VMEM((1, 2 * rows), jnp.int32),
            pltpu.VMEM((8, width), f32),
            pltpu.SemaphoreType.DMA((4,)),
        ],
        name="own_block",
    )(
        picture_mean_embeddings,
        caption_tower_summary,
        caption_mapping_matrix,
        picture_match_index[None, :],
    )
    first = IMAGE_ORDER[1]
    blocks = [own, across(own, Y), across(own, first), across(own, first | Y)]
    near = across(quarter, Y)
    digits = [block[0, rows : rows + 2] for block in (blocks[0], blocks[2])]
    digits += [jnp.zeros((4, width), bf16)]
    images = jnp.concatenate([block[0, :rows] for block in blocks] + digits)
    texts = jnp.concatenate([block[1, :rows] for block in blocks])
    scalars = jnp.concatenate([sharpness_factor, score_shift_term])[None]
    texts, images, scalars = lax.optimization_barrier((texts, images, scalars))
    texts = jnp.concatenate([texts, across(texts, TEXT_ORDER[2])])
    count = 4 * rows
    beside = across(images, IMAGE_ORDER[2])
    digits = [images[count : count + 4], beside[count : count + 4]]
    images = jnp.concatenate([images[:count], beside[:count]] + digits)
    texts, images = lax.optimization_barrier((texts, images))
    texts = [texts, across(texts, CORE), across(texts, TEXT_ORDER[4])]
    images = [images, across(images, IMAGE_ORDER[3]), across(images, CORE)]
    near, texts[1] = lax.optimization_barrier((near, texts[1]))
    far = across(near, CORE)
    zt, projected, turned, matrix = pl.pallas_call(
        early_kernel,
        out_shape=(
            jax.ShapeDtypeStruct((total // 2, width), bf16),
            jax.ShapeDtypeStruct((total // 2, width), f32),
            jax.ShapeDtypeStruct((depth, 256), bf16),
            jax.ShapeDtypeStruct((2 * depth, width), bf16),
        ),
        in_specs=[anywhere] * 3 + [vmem] * 2,
        out_specs=(vmem,) * 4,
        scratch_shapes=[pltpu.VMEM((total // 2, width), bf16), pltpu.SemaphoreType.DMA((3,))],
        compiler_params=params,
        name="early_texts",
    )(caption_mapping_matrix, near, far, *texts[:2])
    texts.append(across(texts[2], CORE))
    images.append(across(images[1], CORE))
    return pl.pallas_call(
        batch_kernel,
        out_shape=(
            jax.ShapeDtypeStruct((rows, width), f32),
            jax.ShapeDtypeStruct((rows, width), f32),
            jax.ShapeDtypeStruct((depth, width), f32),
        ),
        in_specs=[vmem] * 14,
        out_specs=(vmem, vmem, anywhere),
        scratch_shapes=[
            pltpu.VMEM((total, width), bf16),
            pltpu.VMEM((total, width), bf16),
            pltpu.VMEM((total, width), bf16),
            pltpu.VMEM((total, width), f32),
            pltpu.VMEM((total, total), bf16),
            pltpu.VMEM((total, width), f32),
            pltpu.VMEM((depth, total), bf16),
            pltpu.VMEM((total, width), bf16),
            pltpu.SemaphoreType.DMA((8,)),
        ],
        compiler_params=params,
        name="batch",
    )(
        scalars,
        picture_mean_embeddings,
        zt,
        projected,
        turned,
        matrix,
        *texts,
        *images,
    )


def solution(mesh):
    gathered = dict(mesh.shape) == {"dp": 16, "fsdp": 2}
    per_device = gathered_plan if gathered else ring_plan
    return jax.shard_map(
        per_device,
        mesh=mesh,
        in_specs=(
            P(("dp", "fsdp"), None),
            P(("dp", "fsdp"), None),
            P("fsdp", None),
            P("dp"),
            P(),
            P(),
        ),
        out_specs=(P(("dp", "fsdp"), None), P(("dp", "fsdp"), None), P("fsdp", None)),
        check_vma=False,
    )
```

```python
import functools

import jax
import jax.numpy as jnp
from jax import lax
from jax.experimental import pallas as pl
from jax.experimental.pallas import tpu as pltpu
from jax.sharding import PartitionSpec as P

epsilon = 1e-06


def passed_along(block, axis, distance):
    devices = range(lax.axis_size(axis))
    route = [((i - distance) % len(devices), i) for i in devices]
    return lax.ppermute(block, axis, route)


def normalize(values):
    norms = jnp.sqrt(jnp.sum(values * values, axis=1, keepdims=True) + epsilon)
    return (values / norms, norms)


def unproject(grad_unit, unit, norms):
    return (grad_unit - unit * jnp.sum(unit * grad_unit, axis=1, keepdims=True)) / norms


def ring_plan(
    picture_mean_embeddings,
    caption_tower_summary,
    caption_mapping_matrix,
    picture_match_index,
    sharpness_factor,
    score_shift_term,
):
    rows = caption_tower_summary.shape[0]
    width = caption_mapping_matrix.shape[1]
    cycle_size = lax.axis_size("dp")
    column_count = lax.axis_size("fsdp")
    cycle_index = lax.axis_index("dp")
    column_index = lax.axis_index("fsdp")
    score_multiplier = sharpness_factor[0]
    offset = score_shift_term[0]
    feature_column_set = lax.all_to_all(
        caption_tower_summary, "fsdp", split_axis=1, concat_axis=0, tiled=True
    )
    projected = jnp.dot(
        caption_tower_summary,
        lax.all_gather(caption_mapping_matrix, "fsdp", axis=0, tiled=True),
        preferred_element_type=jnp.float32,
    )
    unit_text, text_norm = normalize(projected)
    text_unit = unit_text.astype(jnp.bfloat16)
    unit_image, image_norm = normalize(picture_mean_embeddings.astype(jnp.float32))
    image_unit = lax.all_gather(unit_image.astype(jnp.bfloat16), "fsdp", axis=0, tiled=True)
    group = image_unit.shape[0]

    def tile(block, text_rows):
        scores = lax.dot_general(
            image_unit, block, (((1,), (1,)), ((), ())), preferred_element_type=jnp.float32
        )
        logits = score_multiplier * scores + offset
        sign = jnp.where(picture_match_index[:, None] == text_rows[None, :], 1.0, -1.0).astype(
            jnp.float32
        )
        weights = (score_multiplier * -sign * jax.nn.sigmoid(-sign * logits)).astype(jnp.bfloat16)
        image_part = jnp.dot(weights, block, preferred_element_type=jnp.float32)
        text_part = lax.dot_general(
            weights, image_unit, (((0,), (0,)), ((), ())), preferred_element_type=jnp.float32
        )
        return (image_part, text_part)

    def rows_of(owner, count):
        return (owner * column_count + column_index) * rows + jnp.arange(count, dtype=jnp.int32)

    image_start = jnp.zeros((group, width), jnp.float32)

    def advance(count, state):
        block, carried, image_sum = state
        owner = (cycle_index - count) % cycle_size
        image_part, text_part = tile(block, rows_of(owner, rows))
        block = passed_along(block, "dp", 1)
        carried = passed_along(carried + text_part, "dp", 1)
        return (block, carried, image_sum + image_part)

    state = (text_unit, jnp.zeros((rows, width), jnp.float32), image_start)
    block, grad_zt, image_sum = lax.fori_loop(0, cycle_size, advance, state)
    grad_zi = lax.psum_scatter(image_sum, "fsdp", scatter_dimension=0, tiled=True)
    grad_image = unproject(grad_zi, unit_image, image_norm)
    grad_proj = unproject(grad_zt, unit_text, text_norm).astype(jnp.bfloat16)
    grad_group = lax.all_gather(grad_proj, "fsdp", axis=0, tiled=True)
    head_part = lax.dot_general(
        feature_column_set, grad_group, (((0,), (0,)), ((), ())), preferred_element_type=jnp.float32
    )
    head_grad = lax.psum(head_part, "dp")
    grad_text = lax.dot_general(
        grad_proj,
        lax.all_gather(caption_mapping_matrix, "fsdp", axis=0, tiled=True),
        (((1,), (1,)), ((), ())),
        preferred_element_type=jnp.float32,
    )
    return (grad_image, grad_text, head_grad)


def across(block, bits):
    count = lax.axis_size("dp") * lax.axis_size("fsdp")
    return lax.ppermute(block, ("dp", "fsdp"), [(i, i ^ bits) for i in range(count)])


Y, CORE, X, Z1, Z2 = 1, 2, 4, 8, 16
IMAGE_ORDER = (Y, Z2, X, Z1, CORE)
TEXT_ORDER = (Y, Z2, Z1, CORE, X)
NT = (((1,), (1,)), ((), ()))
TN = (((0,), (0,)), ((), ()))


def dot(a, b, dims=(((1,), (0,)), ((), ()))):
    return lax.dot_general(a, b, dims, preferred_element_type=jnp.float32)


def cuts(size, step):
    return [slice(k, min(k + step, size)) for k in range(0, size, step)]


def owners(order, shape, axis, rows, place):
    row = lax.broadcasted_iota(jnp.int32, shape, axis)
    block = sum((row >= k * rows).astype(jnp.int32) for k in range(1, shape[axis] // rows))
    owner = jnp.zeros_like(row)
    for k, bits in enumerate(order):
        owner += ((block >> k) & 1) * bits
    return owner ^ place, row - block * rows


def weigh(scores, paired, scalars):
    sharpness, shift = scalars[:, 0:1], scalars[:, 1:2]
    logits = sharpness * scores + shift
    share = 1.0 / (1.0 + jnp.exp(jnp.where(paired, logits, -logits)))
    return (jnp.where(paired, -sharpness, sharpness) * share).astype(jnp.bfloat16)


def own_kernel(image, text, matrix, match, own, plain, quarter, *rest):
    images, texts, indices, digits, sems = rest
    rows = images.shape[0]
    count = quarter.shape[0]
    start = pl.multiple_of(lax.rem(lax.axis_index("dp"), 2) * count, 32)
    pairs = ((image, images), (text, texts), (match, indices))
    pairs += ((matrix.at[pl.ds(start, count)], quarter),)
    copies = [pltpu.make_async_copy(*pair, sems.at[k]) for k, pair in enumerate(pairs)]
    for copy in copies:
        copy.start()
    for copy in copies[:3]:
        copy.wait()
    width = indices.shape[1]
    digits[...] = jnp.zeros(digits.shape, jnp.float32)
    digits[0:1, :width] = (indices[...] >> 5).astype(jnp.float32)
    digits[1:2, :width] = (indices[...] & 31).astype(jnp.float32)
    spare = digits[: own.shape[1] - rows]
    unit_image, _ = normalize(images[...].astype(jnp.float32))
    own[0] = jnp.concatenate([unit_image, spare]).astype(jnp.bfloat16)
    text_rows = texts[...].astype(jnp.float32)
    own[1] = jnp.concatenate([text_rows, jnp.zeros_like(spare)]).astype(jnp.bfloat16)
    plain[...] = jnp.concatenate([unit_image, text_rows]).astype(jnp.bfloat16)
    copies[3].wait()


def pair_indices(rows, total, pieces, side):
    digits = jnp.concatenate([piece[-8:, :128].astype(jnp.float32) for piece in pieces])
    lane = lax.broadcasted_iota(jnp.int32, (1, total), 1)
    group = sum((lane >= k).astype(jnp.int32) for k in range(2 * rows, total, 2 * rows))
    row = lane - group * 2 * rows
    row = jnp.where(side == 0, row, jnp.where(row < rows, row + rows, row - rows))
    chosen = lax.broadcasted_iota(jnp.int32, (128, total), 0) == row
    spread = dot(digits.astype(jnp.bfloat16), chosen.astype(jnp.float32).astype(jnp.bfloat16))
    number = lax.broadcasted_iota(jnp.int32, spread.shape, 0)
    scale = jnp.where(number == 2 * group, 32.0, jnp.where(number == 2 * group + 1, 1.0, 0.0))
    return jnp.sum(scale * spread, axis=0, keepdims=True).astype(jnp.int32)


def project(text, matrix, projected, zt):
    for cut in cuts(matrix.shape[1], 256):
        projected[:, cut] = dot(text[...], matrix[:, cut])
    for block in cuts(text.shape[0], 160):
        value = projected[block]
        inverse = lax.rsqrt(jnp.sum(value * value, axis=1, keepdims=True) + epsilon)
        zt[block] = (value * inverse).astype(jnp.bfloat16)


def early_kernel(matrix_own, matrix_near, matrix_far, *rest):
    texts, rest = rest[:2], rest[2:]
    zt, projected, turned, matrix, text, sems = rest
    depth, near = matrix_own.shape[0], matrix_near.shape[0]
    core, side = lax.rem(lax.axis_index("dp"), 2), lax.axis_index("fsdp")

    other = (1 - side) * depth
    places = (side * depth, other + core * near, other + (1 - core) * near)
    copies = []
    for k, (source, start) in enumerate(zip((matrix_own, matrix_near, matrix_far), places)):
        start = pl.multiple_of(start, 32)
        target = matrix.at[pl.ds(start, source.shape[0])]
        copies.append(pltpu.make_async_copy(source, target, sems.at[k]))
        copies[-1].start()
    count = texts[0].shape[0]
    for k, source in enumerate(texts):
        text[pl.ds(k * count, count)] = source[...]
    for s in (0, 1):

        @pl.when(side == s)
        def _():
            turned[...] = jnp.transpose(text[: turned.shape[1], s * depth : (s + 1) * depth])

    for copy in copies:
        copy.wait()
    project(text, matrix, projected, zt)


def batch_kernel(scalars, image, zt_early, projected_early, *rest):
    (turned_early, matrix), texts, images, rest = rest[:2], rest[2:6], rest[6:10], rest[10:]
    (grad_image, grad_text, head_grad), rest = rest[:3], rest[3:]
    zi, text, zt, projected, weights, grad, turned, proj, sems = rest
    rows = image.shape[0]
    total, width = zi.shape
    half = total // 2
    depth = head_grad.shape[0]
    group, side = lax.axis_index("dp"), lax.axis_index("fsdp")

    count = total // 4
    for sources, target in ((texts, text), (images, zi)):
        for k, source in enumerate(sources):
            target[pl.ds(k * count, count)] = source[:count]
    match = pair_indices(rows, total, images, side)
    late = pl.ds(half, half)
    project(text.at[late], matrix, projected.at[late], zt.at[late])
    zt[:half] = zt_early[...]
    first = turned_early.shape[1]
    turned[:, :first] = turned_early[...]
    for s in (0, 1):

        @pl.when(side == s)
        def _():
            turned[:, first:] = jnp.transpose(text[first:, s * depth : (s + 1) * depth])

    owner, row = owners(TEXT_ORDER, (total, 1), 0, rows, group * 2 + side)
    ids = owner * rows + row
    for cut in cuts(total, 256):
        scores = dot(zt[...], zi[cut], NT)
        weights[:, cut] = weigh(scores, ids == match[:, cut], scalars)
    for cut in cuts(width, 256):
        grad[:, cut] = dot(weights[...], zi[:, cut])
    for block in cuts(total, 160):
        value = projected_early[block] if block.stop <= half else projected[block]
        slope = grad[block]
        squares = jnp.sum(value * value, axis=1, keepdims=True) + epsilon
        inner = jnp.sum(value * slope, axis=1, keepdims=True)
        proj[block] = ((slope - value * (inner / squares)) * lax.rsqrt(squares)).astype(
            jnp.bfloat16
        )
    copies = []
    head = grad
    for k, cut in enumerate(cuts(width, 384)):
        head[:depth, cut] = dot(turned[...], proj[:, cut])
        copies.append(
            pltpu.make_async_copy(head.at[:depth, cut], head_grad.at[:, cut], sems.at[k])
        )
        copies[-1].start()
    grad_text[...] = dot(proj[:48], matrix[...], NT)[:rows]
    grad_zi = dot(weights[:, :128], zt[...], TN)[:rows]
    unit_image, image_norm = normalize(image[...].astype(jnp.float32))
    grad_image[...] = unproject(grad_zi, unit_image, image_norm)
    for copy in copies:
        copy.wait()


def gathered_plan(
    picture_mean_embeddings,
    caption_tower_summary,
    caption_mapping_matrix,
    picture_match_index,
    sharpness_factor,
    score_shift_term,
):
    rows, width = caption_tower_summary.shape
    depth = caption_mapping_matrix.shape[0]
    half = depth // 2
    total = rows * 32
    vmem = pl.BlockSpec(memory_space=pltpu.VMEM)
    anywhere = pl.BlockSpec(memory_space=pl.ANY)
    f32, bf16 = jnp.float32, jnp.bfloat16
    params = pltpu.CompilerParams(vmem_limit_bytes=24 * 2**20)

    hbm = pl.BlockSpec(memory_space=pltpu.HBM)
    own, plain, quarter = pl.pallas_call(
        own_kernel,
        out_shape=(
            jax.ShapeDtypeStruct((2, rows + 4, width), bf16),
            jax.ShapeDtypeStruct((2 * rows, width), bf16),
            jax.ShapeDtypeStruct((half, width), bf16),
        ),
        in_specs=[hbm] * 4,
        out_specs=(vmem, vmem, vmem),
        scratch_shapes=[
            pltpu.VMEM((rows, width), bf16),
            pltpu.VMEM((rows, width), bf16),
            pltpu.VMEM((1, 2 * rows), jnp.int32),
            pltpu.VMEM((8, width), f32),
            pltpu.SemaphoreType.DMA((4,)),
        ],
        name="own_block",
    )(
        picture_mean_embeddings,
        caption_tower_summary,
        caption_mapping_matrix,
        picture_match_index[None, :],
    )
    first = IMAGE_ORDER[1]
    beside = across(own, first)
    blocks = [plain, across(plain, Y), beside, across(plain, first | Y)]
    near = across(quarter, Y)
    digits = [block[0, rows : rows + 2] for block in (own, beside)]
    digits += [jnp.zeros((4, width), bf16)]
    images = [block[0, :rows] if block is beside else block[:rows] for block in blocks]
    images = jnp.concatenate(images + digits)
    texts = [block[1, :rows] if block is beside else block[rows:] for block in blocks]
    texts = jnp.concatenate(texts)
    scalars = jnp.concatenate([sharpness_factor, score_shift_term])[None]
    texts, images, scalars = lax.optimization_barrier((texts, images, scalars))
    texts = jnp.concatenate([texts, across(texts, TEXT_ORDER[2])])
    count = 4 * rows
    beside = across(images, IMAGE_ORDER[2])
    digits = [images[count : count + 4], beside[count : count + 4]]
    images = jnp.concatenate([images[:count], beside[:count]] + digits)
    texts, images = lax.optimization_barrier((texts, images))
    texts = [texts, across(texts, CORE), across(texts, TEXT_ORDER[4])]
    images = [images, across(images, IMAGE_ORDER[3]), across(images, CORE)]
    near, texts[1] = lax.optimization_barrier((near, texts[1]))
    far = across(near, CORE)
    zt, projected, turned, matrix = pl.pallas_call(
        early_kernel,
        out_shape=(
            jax.ShapeDtypeStruct((total // 2, width), bf16),
            jax.ShapeDtypeStruct((total // 2, width), f32),
            jax.ShapeDtypeStruct((depth, 256), bf16),
            jax.ShapeDtypeStruct((2 * depth, width), bf16),
        ),
        in_specs=[anywhere] * 3 + [vmem] * 2,
        out_specs=(vmem,) * 4,
        scratch_shapes=[pltpu.VMEM((total // 2, width), bf16), pltpu.SemaphoreType.DMA((3,))],
        compiler_params=params,
        name="early_texts",
    )(caption_mapping_matrix, near, far, *texts[:2])
    texts.append(across(texts[2], CORE))
    images.append(across(images[1], CORE))
    return pl.pallas_call(
        batch_kernel,
        out_shape=(
            jax.ShapeDtypeStruct((rows, width), f32),
            jax.ShapeDtypeStruct((rows, width), f32),
            jax.ShapeDtypeStruct((depth, width), f32),
        ),
        in_specs=[vmem] * 14,
        out_specs=(vmem, vmem, anywhere),
        scratch_shapes=[
            pltpu.VMEM((total, width), bf16),
            pltpu.VMEM((total, width), bf16),
            pltpu.VMEM((total, width), bf16),
            pltpu.VMEM((total, width), f32),
            pltpu.VMEM((total, total), bf16),
            pltpu.VMEM((total, width), f32),
            pltpu.VMEM((depth, total), bf16),
            pltpu.VMEM((total, width), bf16),
            pltpu.SemaphoreType.DMA((8,)),
        ],
        compiler_params=params,
        name="batch",
    )(
        scalars,
        picture_mean_embeddings,
        zt,
        projected,
        turned,
        matrix,
        *texts,
        *images,
    )


def solution(mesh):
    gathered = dict(mesh.shape) == {"dp": 16, "fsdp": 2}
    per_device = gathered_plan if gathered else ring_plan
    return jax.shard_map(
        per_device,
        mesh=mesh,
        in_specs=(
            P(("dp", "fsdp"), None),
            P(("dp", "fsdp"), None),
            P("fsdp", None),
            P("dp"),
            P(),
            P(),
        ),
        out_specs=(P(("dp", "fsdp"), None), P(("dp", "fsdp"), None), P("fsdp", None)),
        check_vma=False,
    )
```

```python
import functools

import jax
import jax.numpy as jnp
from jax import lax
from jax.experimental import pallas as pl
from jax.experimental.pallas import tpu as pltpu
from jax.sharding import PartitionSpec as P

epsilon = 1e-06


def passed_along(block, axis, distance):
    devices = range(lax.axis_size(axis))
    route = [((i - distance) % len(devices), i) for i in devices]
    return lax.ppermute(block, axis, route)


def normalize(values):
    norms = jnp.sqrt(jnp.sum(values * values, axis=1, keepdims=True) + epsilon)
    return (values / norms, norms)


def unproject(grad_unit, unit, norms):
    return (grad_unit - unit * jnp.sum(unit * grad_unit, axis=1, keepdims=True)) / norms


def ring_plan(
    picture_mean_embeddings,
    caption_tower_summary,
    caption_mapping_matrix,
    picture_match_index,
    sharpness_factor,
    score_shift_term,
):
    rows = caption_tower_summary.shape[0]
    width = caption_mapping_matrix.shape[1]
    cycle_size = lax.axis_size("dp")
    column_count = lax.axis_size("fsdp")
    cycle_index = lax.axis_index("dp")
    column_index = lax.axis_index("fsdp")
    score_multiplier = sharpness_factor[0]
    offset = score_shift_term[0]
    feature_column_set = lax.all_to_all(
        caption_tower_summary, "fsdp", split_axis=1, concat_axis=0, tiled=True
    )
    projected = jnp.dot(
        caption_tower_summary,
        lax.all_gather(caption_mapping_matrix, "fsdp", axis=0, tiled=True),
        preferred_element_type=jnp.float32,
    )
    unit_text, text_norm = normalize(projected)
    text_unit = unit_text.astype(jnp.bfloat16)
    unit_image, image_norm = normalize(picture_mean_embeddings.astype(jnp.float32))
    image_unit = lax.all_gather(unit_image.astype(jnp.bfloat16), "fsdp", axis=0, tiled=True)
    group = image_unit.shape[0]

    def tile(block, text_rows):
        scores = lax.dot_general(
            image_unit, block, (((1,), (1,)), ((), ())), preferred_element_type=jnp.float32
        )
        logits = score_multiplier * scores + offset
        sign = jnp.where(picture_match_index[:, None] == text_rows[None, :], 1.0, -1.0).astype(
            jnp.float32
        )
        weights = (score_multiplier * -sign * jax.nn.sigmoid(-sign * logits)).astype(jnp.bfloat16)
        image_part = jnp.dot(weights, block, preferred_element_type=jnp.float32)
        text_part = lax.dot_general(
            weights, image_unit, (((0,), (0,)), ((), ())), preferred_element_type=jnp.float32
        )
        return (image_part, text_part)

    def rows_of(owner, count):
        return (owner * column_count + column_index) * rows + jnp.arange(count, dtype=jnp.int32)

    image_start = jnp.zeros((group, width), jnp.float32)

    def advance(count, state):
        block, carried, image_sum = state
        owner = (cycle_index - count) % cycle_size
        image_part, text_part = tile(block, rows_of(owner, rows))
        block = passed_along(block, "dp", 1)
        carried = passed_along(carried + text_part, "dp", 1)
        return (block, carried, image_sum + image_part)

    state = (text_unit, jnp.zeros((rows, width), jnp.float32), image_start)
    block, grad_zt, image_sum = lax.fori_loop(0, cycle_size, advance, state)
    grad_zi = lax.psum_scatter(image_sum, "fsdp", scatter_dimension=0, tiled=True)
    grad_image = unproject(grad_zi, unit_image, image_norm)
    grad_proj = unproject(grad_zt, unit_text, text_norm).astype(jnp.bfloat16)
    grad_group = lax.all_gather(grad_proj, "fsdp", axis=0, tiled=True)
    head_part = lax.dot_general(
        feature_column_set, grad_group, (((0,), (0,)), ((), ())), preferred_element_type=jnp.float32
    )
    head_grad = lax.psum(head_part, "dp")
    grad_text = lax.dot_general(
        grad_proj,
        lax.all_gather(caption_mapping_matrix, "fsdp", axis=0, tiled=True),
        (((1,), (1,)), ((), ())),
        preferred_element_type=jnp.float32,
    )
    return (grad_image, grad_text, head_grad)


def across(block, bits):
    count = lax.axis_size("dp") * lax.axis_size("fsdp")
    return lax.ppermute(block, ("dp", "fsdp"), [(i, i ^ bits) for i in range(count)])


Y, CORE, X, Z1, Z2 = 1, 2, 4, 8, 16
IMAGE_ORDER = (Y, Z2, X, Z1, CORE)
TEXT_ORDER = (Y, Z2, Z1, CORE, X)
NT = (((1,), (1,)), ((), ()))
TN = (((0,), (0,)), ((), ()))


def dot(a, b, dims=(((1,), (0,)), ((), ()))):
    return lax.dot_general(a, b, dims, preferred_element_type=jnp.float32)


def cuts(size, step):
    return [slice(k, min(k + step, size)) for k in range(0, size, step)]


def owners(order, shape, axis, rows, place):
    row = lax.broadcasted_iota(jnp.int32, shape, axis)
    block = sum((row >= k * rows).astype(jnp.int32) for k in range(1, shape[axis] // rows))
    owner = jnp.zeros_like(row)
    for k, bits in enumerate(order):
        owner += ((block >> k) & 1) * bits
    return owner ^ place, row - block * rows


def weigh(scores, paired, scalars):
    sharpness, shift = scalars[:, 0:1], scalars[:, 1:2]
    logits = sharpness * scores + shift
    share = 1.0 / (1.0 + jnp.exp(jnp.where(paired, logits, -logits)))
    return (jnp.where(paired, -sharpness, sharpness) * share).astype(jnp.bfloat16)


def own_kernel(image, text, match, own, plain, images, texts, indices, digits, sems):
    rows = images.shape[0]
    pairs = ((image, images), (text, texts), (match, indices))
    copies = [pltpu.make_async_copy(*pair, sems.at[k]) for k, pair in enumerate(pairs)]
    for copy in copies:
        copy.start()
    for copy in copies:
        copy.wait()
    width = indices.shape[1]
    digits[...] = jnp.zeros(digits.shape, jnp.float32)
    digits[0:1, :width] = (indices[...] >> 5).astype(jnp.float32)
    digits[1:2, :width] = (indices[...] & 31).astype(jnp.float32)
    spare = digits[: own.shape[1] - rows]
    unit_image, _ = normalize(images[...].astype(jnp.float32))
    own[0] = jnp.concatenate([unit_image, spare]).astype(jnp.bfloat16)
    text_rows = texts[...].astype(jnp.float32)
    own[1] = jnp.concatenate([text_rows, jnp.zeros_like(spare)]).astype(jnp.bfloat16)
    plain[...] = jnp.concatenate([unit_image, text_rows]).astype(jnp.bfloat16)


def pair_indices(rows, total, pieces, side):
    digits = jnp.concatenate([piece[-8:, :128].astype(jnp.float32) for piece in pieces])
    lane = lax.broadcasted_iota(jnp.int32, (1, total), 1)
    group = sum((lane >= k).astype(jnp.int32) for k in range(2 * rows, total, 2 * rows))
    row = lane - group * 2 * rows
    row = jnp.where(side == 0, row, jnp.where(row < rows, row + rows, row - rows))
    chosen = lax.broadcasted_iota(jnp.int32, (128, total), 0) == row
    spread = dot(digits.astype(jnp.bfloat16), chosen.astype(jnp.float32).astype(jnp.bfloat16))
    number = lax.broadcasted_iota(jnp.int32, spread.shape, 0)
    scale = jnp.where(number == 2 * group, 32.0, jnp.where(number == 2 * group + 1, 1.0, 0.0))
    return jnp.sum(scale * spread, axis=0, keepdims=True).astype(jnp.int32)


def project(text, matrix, projected, zt):
    for cut in cuts(matrix.shape[1], 256):
        projected[:, cut] = dot(text[...], matrix[:, cut])
    for block in cuts(text.shape[0], 160):
        value = projected[block]
        inverse = lax.rsqrt(jnp.sum(value * value, axis=1, keepdims=True) + epsilon)
        zt[block] = (value * inverse).astype(jnp.bfloat16)


def early_kernel(matrix_own, matrix_near, matrix_far, *rest):
    texts, rest = rest[:2], rest[2:]
    zt, projected, turned, matrix, text, sems = rest
    depth, near = matrix_own.shape[0], matrix_near.shape[0]
    core, side = lax.rem(lax.axis_index("dp"), 2), lax.axis_index("fsdp")

    other = (1 - side) * depth
    places = (side * depth, other + core * near, other + (1 - core) * near)
    copies = []
    for k, (source, start) in enumerate(zip((matrix_own, matrix_near, matrix_far), places)):
        start = pl.multiple_of(start, 32)
        target = matrix.at[pl.ds(start, source.shape[0])]
        copies.append(pltpu.make_async_copy(source, target, sems.at[k]))
        copies[-1].start()
    count = texts[0].shape[0]
    for k, source in enumerate(texts):
        text[pl.ds(k * count, count)] = source[...]
    for s in (0, 1):

        @pl.when(side == s)
        def _():
            turned[...] = jnp.transpose(text[: turned.shape[1], s * depth : (s + 1) * depth])

    for copy in copies:
        copy.wait()
    project(text, matrix, projected, zt)


def batch_kernel(scalars, image, zt_early, projected_early, *rest):
    (turned_early, matrix), texts, images, rest = rest[:2], rest[2:6], rest[6:10], rest[10:]
    (grad_image, grad_text, head_grad), rest = rest[:3], rest[3:]
    zi, text, zt, projected, weights, grad, turned, proj, sems = rest
    rows = image.shape[0]
    total, width = zi.shape
    half = total // 2
    depth = head_grad.shape[0]
    group, side = lax.axis_index("dp"), lax.axis_index("fsdp")

    count = total // 4
    for sources, target in ((texts, text), (images, zi)):
        for k, source in enumerate(sources):
            target[pl.ds(k * count, count)] = source[:count]
    match = pair_indices(rows, total, images, side)
    late = pl.ds(half, half)
    project(text.at[late], matrix, projected.at[late], zt.at[late])
    zt[:half] = zt_early[...]
    first = turned_early.shape[1]
    turned[:, :first] = turned_early[...]
    for s in (0, 1):

        @pl.when(side == s)
        def _():
            turned[:, first:] = jnp.transpose(text[first:, s * depth : (s + 1) * depth])

    owner, row = owners(TEXT_ORDER, (total, 1), 0, rows, group * 2 + side)
    ids = owner * rows + row
    for cut in cuts(total, 256):
        scores = dot(zt[...], zi[cut], NT)
        weights[:, cut] = weigh(scores, ids == match[:, cut], scalars)
    for cut in cuts(width, 256):
        grad[:, cut] = dot(weights[...], zi[:, cut])
    for block in cuts(total, 160):
        value = projected_early[block] if block.stop <= half else projected[block]
        slope = grad[block]
        squares = jnp.sum(value * value, axis=1, keepdims=True) + epsilon
        inner = jnp.sum(value * slope, axis=1, keepdims=True)
        proj[block] = ((slope - value * (inner / squares)) * lax.rsqrt(squares)).astype(
            jnp.bfloat16
        )
    copies = []
    head = grad
    for k, cut in enumerate(cuts(width, 256)):
        head[:depth, cut] = dot(turned[...], proj[:, cut])
        copies.append(
            pltpu.make_async_copy(head.at[:depth, cut], head_grad.at[:, cut], sems.at[k])
        )
        copies[-1].start()
    grad_text[...] = dot(proj[:48], matrix[...], NT)[:rows]
    grad_zi = dot(weights[:, :128], zt[...], TN)[:rows]
    unit_image, image_norm = normalize(image[...].astype(jnp.float32))
    grad_image[...] = unproject(grad_zi, unit_image, image_norm)
    for copy in copies:
        copy.wait()


def gathered_plan(
    picture_mean_embeddings,
    caption_tower_summary,
    caption_mapping_matrix,
    picture_match_index,
    sharpness_factor,
    score_shift_term,
):
    rows, width = caption_tower_summary.shape
    depth = caption_mapping_matrix.shape[0]
    half = depth // 2
    total = rows * 32
    vmem = pl.BlockSpec(memory_space=pltpu.VMEM)
    anywhere = pl.BlockSpec(memory_space=pl.ANY)
    f32, bf16 = jnp.float32, jnp.bfloat16
    params = pltpu.CompilerParams(vmem_limit_bytes=24 * 2**20)

    hbm = pl.BlockSpec(memory_space=pltpu.HBM)
    own, plain = pl.pallas_call(
        own_kernel,
        out_shape=(
            jax.ShapeDtypeStruct((2, rows + 4, width), bf16),
            jax.ShapeDtypeStruct((2 * rows, width), bf16),
        ),
        in_specs=[hbm] * 3,
        out_specs=(vmem, vmem),
        scratch_shapes=[
            pltpu.VMEM((rows, width), bf16),
            pltpu.VMEM((rows, width), bf16),
            pltpu.VMEM((1, 2 * rows), jnp.int32),
            pltpu.VMEM((8, width), f32),
            pltpu.SemaphoreType.DMA((3,)),
        ],
        name="own_block",
    )(
        picture_mean_embeddings,
        caption_tower_summary,
        picture_match_index[None, :],
    )
    first = IMAGE_ORDER[1]
    beside = across(own, first)
    blocks = [plain, across(plain, Y), beside, across(plain, first | Y)]
    matrix, plain = lax.optimization_barrier((caption_mapping_matrix, plain))
    core = lax.axis_index("dp") % 2
    quarter = lax.dynamic_slice_in_dim(matrix, core * half, half, 0)
    digits = [block[0, rows : rows + 2] for block in (own, beside)]
    digits += [jnp.zeros((4, width), bf16)]
    images = [block[0, :rows] if block is beside else block[:rows] for block in blocks]
    images = jnp.concatenate(images + digits)
    texts = [block[1, :rows] if block is beside else block[rows:] for block in blocks]
    texts = jnp.concatenate(texts)
    scalars = jnp.concatenate([sharpness_factor, score_shift_term])[None]
    tied = lax.optimization_barrier((texts, images, scalars, quarter))
    texts, images, scalars, quarter = tied
    near = across(quarter, Y)
    texts = jnp.concatenate([texts, across(texts, TEXT_ORDER[2])])
    count = 4 * rows
    beside = across(images, IMAGE_ORDER[2])
    digits = [images[count : count + 4], beside[count : count + 4]]
    images = jnp.concatenate([images[:count], beside[:count]] + digits)
    texts, images = lax.optimization_barrier((texts, images))
    texts = [texts, across(texts, CORE), across(texts, TEXT_ORDER[4])]
    images = [images, across(images, IMAGE_ORDER[3]), across(images, CORE)]
    near, texts[1] = lax.optimization_barrier((near, texts[1]))
    far = across(near, CORE)
    zt, projected, turned, matrix = pl.pallas_call(
        early_kernel,
        out_shape=(
            jax.ShapeDtypeStruct((total // 2, width), bf16),
            jax.ShapeDtypeStruct((total // 2, width), f32),
            jax.ShapeDtypeStruct((depth, 256), bf16),
            jax.ShapeDtypeStruct((2 * depth, width), bf16),
        ),
        in_specs=[anywhere] * 3 + [vmem] * 2,
        out_specs=(vmem,) * 4,
        scratch_shapes=[pltpu.VMEM((total // 2, width), bf16), pltpu.SemaphoreType.DMA((3,))],
        compiler_params=params,
        name="early_texts",
    )(caption_mapping_matrix, near, far, *texts[:2])
    texts.append(across(texts[2], CORE))
    images.append(across(images[1], CORE))
    return pl.pallas_call(
        batch_kernel,
        out_shape=(
            jax.ShapeDtypeStruct((rows, width), f32),
            jax.ShapeDtypeStruct((rows, width), f32),
            jax.ShapeDtypeStruct((depth, width), f32),
        ),
        in_specs=[vmem] * 14,
        out_specs=(vmem, vmem, anywhere),
        scratch_shapes=[
            pltpu.VMEM((total, width), bf16),
            pltpu.VMEM((total, width), bf16),
            pltpu.VMEM((total, width), bf16),
            pltpu.VMEM((total, width), f32),
            pltpu.VMEM((total, total), bf16),
            pltpu.VMEM((total, width), f32),
            pltpu.VMEM((depth, total), bf16),
            pltpu.VMEM((total, width), bf16),
            pltpu.SemaphoreType.DMA((8,)),
        ],
        compiler_params=params,
        name="batch",
    )(
        scalars,
        picture_mean_embeddings,
        zt,
        projected,
        turned,
        matrix,
        *texts,
        *images,
    )


def solution(mesh):
    gathered = dict(mesh.shape) == {"dp": 16, "fsdp": 2}
    per_device = gathered_plan if gathered else ring_plan
    return jax.shard_map(
        per_device,
        mesh=mesh,
        in_specs=(
            P(("dp", "fsdp"), None),
            P(("dp", "fsdp"), None),
            P("fsdp", None),
            P("dp"),
            P(),
            P(),
        ),
        out_specs=(P(("dp", "fsdp"), None), P(("dp", "fsdp"), None), P("fsdp", None)),
        check_vma=False,
    )
```

```python
import functools

import jax
import jax.numpy as jnp
from jax import lax
from jax.experimental import pallas as pl
from jax.experimental.pallas import tpu as pltpu
from jax.sharding import PartitionSpec as P

epsilon = 1e-06


def passed_along(block, axis, distance):
    devices = range(lax.axis_size(axis))
    route = [((i - distance) % len(devices), i) for i in devices]
    return lax.ppermute(block, axis, route)


def normalize(values):
    norms = jnp.sqrt(jnp.sum(values * values, axis=1, keepdims=True) + epsilon)
    return (values / norms, norms)


def unproject(grad_unit, unit, norms):
    return (grad_unit - unit * jnp.sum(unit * grad_unit, axis=1, keepdims=True)) / norms


def ring_plan(
    picture_mean_embeddings,
    caption_tower_summary,
    caption_mapping_matrix,
    picture_match_index,
    sharpness_factor,
    score_shift_term,
):
    rows = caption_tower_summary.shape[0]
    width = caption_mapping_matrix.shape[1]
    cycle_size = lax.axis_size("dp")
    column_count = lax.axis_size("fsdp")
    cycle_index = lax.axis_index("dp")
    column_index = lax.axis_index("fsdp")
    score_multiplier = sharpness_factor[0]
    offset = score_shift_term[0]
    feature_column_set = lax.all_to_all(
        caption_tower_summary, "fsdp", split_axis=1, concat_axis=0, tiled=True
    )
    projected = jnp.dot(
        caption_tower_summary,
        lax.all_gather(caption_mapping_matrix, "fsdp", axis=0, tiled=True),
        preferred_element_type=jnp.float32,
    )
    unit_text, text_norm = normalize(projected)
    text_unit = unit_text.astype(jnp.bfloat16)
    unit_image, image_norm = normalize(picture_mean_embeddings.astype(jnp.float32))
    image_unit = lax.all_gather(unit_image.astype(jnp.bfloat16), "fsdp", axis=0, tiled=True)
    group = image_unit.shape[0]

    def tile(block, text_rows):
        scores = lax.dot_general(
            image_unit, block, (((1,), (1,)), ((), ())), preferred_element_type=jnp.float32
        )
        logits = score_multiplier * scores + offset
        sign = jnp.where(picture_match_index[:, None] == text_rows[None, :], 1.0, -1.0).astype(
            jnp.float32
        )
        weights = (score_multiplier * -sign * jax.nn.sigmoid(-sign * logits)).astype(jnp.bfloat16)
        image_part = jnp.dot(weights, block, preferred_element_type=jnp.float32)
        text_part = lax.dot_general(
            weights, image_unit, (((0,), (0,)), ((), ())), preferred_element_type=jnp.float32
        )
        return (image_part, text_part)

    def rows_of(owner, count):
        return (owner * column_count + column_index) * rows + jnp.arange(count, dtype=jnp.int32)

    image_start = jnp.zeros((group, width), jnp.float32)

    def advance(count, state):
        block, carried, image_sum = state
        owner = (cycle_index - count) % cycle_size
        image_part, text_part = tile(block, rows_of(owner, rows))
        block = passed_along(block, "dp", 1)
        carried = passed_along(carried + text_part, "dp", 1)
        return (block, carried, image_sum + image_part)

    state = (text_unit, jnp.zeros((rows, width), jnp.float32), image_start)
    block, grad_zt, image_sum = lax.fori_loop(0, cycle_size, advance, state)
    grad_zi = lax.psum_scatter(image_sum, "fsdp", scatter_dimension=0, tiled=True)
    grad_image = unproject(grad_zi, unit_image, image_norm)
    grad_proj = unproject(grad_zt, unit_text, text_norm).astype(jnp.bfloat16)
    grad_group = lax.all_gather(grad_proj, "fsdp", axis=0, tiled=True)
    head_part = lax.dot_general(
        feature_column_set, grad_group, (((0,), (0,)), ((), ())), preferred_element_type=jnp.float32
    )
    head_grad = lax.psum(head_part, "dp")
    grad_text = lax.dot_general(
        grad_proj,
        lax.all_gather(caption_mapping_matrix, "fsdp", axis=0, tiled=True),
        (((1,), (1,)), ((), ())),
        preferred_element_type=jnp.float32,
    )
    return (grad_image, grad_text, head_grad)


def across(block, bits):
    count = lax.axis_size("dp") * lax.axis_size("fsdp")
    return lax.ppermute(block, ("dp", "fsdp"), [(i, i ^ bits) for i in range(count)])


Y, CORE, X, Z1, Z2 = 1, 2, 4, 8, 16
IMAGE_ORDER = (Y, Z2, X, Z1, CORE)
TEXT_ORDER = (Y, Z2, Z1, CORE, X)
NT = (((1,), (1,)), ((), ()))
TN = (((0,), (0,)), ((), ()))


def dot(a, b, dims=(((1,), (0,)), ((), ()))):
    return lax.dot_general(a, b, dims, preferred_element_type=jnp.float32)


def cuts(size, step):
    return [slice(k, min(k + step, size)) for k in range(0, size, step)]


def owners(order, shape, axis, rows, place):
    row = lax.broadcasted_iota(jnp.int32, shape, axis)
    block = sum((row >= k * rows).astype(jnp.int32) for k in range(1, shape[axis] // rows))
    owner = jnp.zeros_like(row)
    for k, bits in enumerate(order):
        owner += ((block >> k) & 1) * bits
    return owner ^ place, row - block * rows


def weigh(scores, paired, scalars):
    sharpness, shift = scalars[:, 0:1], scalars[:, 1:2]
    logits = sharpness * scores + shift
    share = 1.0 / (1.0 + jnp.exp(jnp.where(paired, logits, -logits)))
    return (jnp.where(paired, -sharpness, sharpness) * share).astype(jnp.bfloat16)


def own_kernel(image, text, match, own, plain, digits):
    rows, width = image.shape[0], match.shape[1]
    digits[...] = jnp.zeros(digits.shape, jnp.float32)
    digits[0:1, :width] = (match[...] >> 5).astype(jnp.float32)
    digits[1:2, :width] = (match[...] & 31).astype(jnp.float32)
    spare = digits[: own.shape[1] - rows]
    unit_image, _ = normalize(image[...].astype(jnp.float32))
    own[0] = jnp.concatenate([unit_image, spare]).astype(jnp.bfloat16)
    text_rows = text[...].astype(jnp.float32)
    own[1] = jnp.concatenate([text_rows, jnp.zeros_like(spare)]).astype(jnp.bfloat16)
    plain[...] = jnp.concatenate([unit_image, text_rows]).astype(jnp.bfloat16)


def pair_indices(rows, total, pieces, side):
    digits = jnp.concatenate([piece[...].astype(jnp.float32)[-8:, :128] for piece in pieces])
    lane = lax.broadcasted_iota(jnp.int32, (1, total), 1)
    group = sum((lane >= k).astype(jnp.int32) for k in range(2 * rows, total, 2 * rows))
    row = lane - group * 2 * rows
    row = jnp.where(side == 0, row, jnp.where(row < rows, row + rows, row - rows))
    chosen = lax.broadcasted_iota(jnp.int32, (128, total), 0) == row
    spread = dot(digits.astype(jnp.bfloat16), chosen.astype(jnp.float32).astype(jnp.bfloat16))
    number = lax.broadcasted_iota(jnp.int32, spread.shape, 0)
    scale = jnp.where(number == 2 * group, 32.0, jnp.where(number == 2 * group + 1, 1.0, 0.0))
    return jnp.sum(scale * spread, axis=0, keepdims=True).astype(jnp.int32)


def project(text, matrix, projected, zt):
    for cut in cuts(matrix.shape[1], 256):
        projected[:, cut] = dot(text[...], matrix[:, cut])
    for block in cuts(text.shape[0], 160):
        value = projected[block]
        inverse = lax.rsqrt(jnp.sum(value * value, axis=1, keepdims=True) + epsilon)
        zt[block] = (value * inverse).astype(jnp.bfloat16)


def early_kernel(matrix_own, matrix_near, matrix_far, *rest):
    texts, rest = rest[:2], rest[2:]
    zt, projected, turned, matrix, text, sems = rest
    depth, near = matrix_own.shape[0], matrix_near.shape[0]
    core, side = lax.rem(lax.axis_index("dp"), 2), lax.axis_index("fsdp")

    other = (1 - side) * depth
    places = (side * depth, other + core * near, other + (1 - core) * near)
    copies = []
    for k, (source, start) in enumerate(zip((matrix_own, matrix_near, matrix_far), places)):
        start = pl.multiple_of(start, 32)
        target = matrix.at[pl.ds(start, source.shape[0])]
        copies.append(pltpu.make_async_copy(source, target, sems.at[k]))
        copies[-1].start()
    count = texts[0].shape[0]
    for k, source in enumerate(texts):
        text[pl.ds(k * count, count)] = source[...]
    for s in (0, 1):

        @pl.when(side == s)
        def _():
            turned[...] = jnp.transpose(text[: turned.shape[1], s * depth : (s + 1) * depth])

    for copy in copies:
        copy.wait()
    project(text, matrix, projected, zt)


def batch_kernel(scalars, image, zt_early, projected_early, *rest):
    (turned_early, matrix), texts, images, rest = rest[:2], rest[2:6], rest[6:10], rest[10:]
    (grad_image, grad_text, head_grad), rest = rest[:3], rest[3:]
    zi, text, zt, projected, weights, grad, turned, proj, sems = rest
    rows = image.shape[0]
    total, width = zi.shape
    half = total // 2
    depth = head_grad.shape[0]
    group, side = lax.axis_index("dp"), lax.axis_index("fsdp")

    count = total // 4
    for sources, target in ((texts, text), (images, zi)):
        for k, source in enumerate(sources):
            target[pl.ds(k * count, count)] = source[:count]
    match = pair_indices(rows, total, images, side)
    late = pl.ds(half, half)
    project(text.at[late], matrix, projected.at[late], zt.at[late])
    zt[:half] = zt_early[...]
    first = turned_early.shape[1]
    turned[:, :first] = turned_early[...]
    for s in (0, 1):

        @pl.when(side == s)
        def _():
            turned[:, first:] = jnp.transpose(text[first:, s * depth : (s + 1) * depth])

    owner, row = owners(TEXT_ORDER, (total, 1), 0, rows, group * 2 + side)
    ids = owner * rows + row
    for cut in cuts(total, 256):
        scores = dot(zt[...], zi[cut], NT)
        weights[:, cut] = weigh(scores, ids == match[:, cut], scalars)
    for cut in cuts(width, 256):
        grad[:, cut] = dot(weights[...], zi[:, cut])
    for block in cuts(total, 160):
        value = projected_early[block] if block.stop <= half else projected[block]
        slope = grad[block]
        squares = jnp.sum(value * value, axis=1, keepdims=True) + epsilon
        inner = jnp.sum(value * slope, axis=1, keepdims=True)
        proj[block] = ((slope - value * (inner / squares)) * lax.rsqrt(squares)).astype(
            jnp.bfloat16
        )
    copies = []
    head = grad
    for k, cut in enumerate(cuts(width, 256)):
        head[:depth, cut] = dot(turned[...], proj[:, cut])
        copies.append(
            pltpu.make_async_copy(head.at[:depth, cut], head_grad.at[:, cut], sems.at[k])
        )
        copies[-1].start()
    grad_text[...] = dot(proj[:48], matrix[...], NT)[:rows]
    grad_zi = dot(weights[:, :128], zt[...], TN)[:rows]
    unit_image, image_norm = normalize(image[...].astype(jnp.float32))
    grad_image[...] = unproject(grad_zi, unit_image, image_norm)
    for copy in copies:
        copy.wait()


def gathered_plan(
    picture_mean_embeddings,
    caption_tower_summary,
    caption_mapping_matrix,
    picture_match_index,
    sharpness_factor,
    score_shift_term,
):
    rows, width = caption_tower_summary.shape
    depth = caption_mapping_matrix.shape[0]
    half = depth // 2
    total = rows * 32
    vmem = pl.BlockSpec(memory_space=pltpu.VMEM)
    anywhere = pl.BlockSpec(memory_space=pl.ANY)
    f32, bf16 = jnp.float32, jnp.bfloat16
    params = pltpu.CompilerParams(vmem_limit_bytes=24 * 2**20)

    own, plain = pl.pallas_call(
        own_kernel,
        out_shape=(
            jax.ShapeDtypeStruct((2, rows + 4, width), bf16),
            jax.ShapeDtypeStruct((2 * rows, width), bf16),
        ),
        in_specs=[vmem] * 3,
        out_specs=(vmem, vmem),
        scratch_shapes=[pltpu.VMEM((8, width), f32)],
        name="own_block",
    )(
        picture_mean_embeddings,
        caption_tower_summary,
        picture_match_index[None, :],
    )
    first = IMAGE_ORDER[1]
    beside = across(own, first)
    blocks = [plain, across(plain, Y), beside, across(plain, first | Y)]
    matrix, plain = lax.optimization_barrier((caption_mapping_matrix, plain))
    core = lax.axis_index("dp") % 2
    quarter = lax.dynamic_slice_in_dim(matrix, core * half, half, 0)
    digits = [block[0, rows : rows + 2] for block in (own, beside)]
    digits += [jnp.zeros((4, width), bf16)]
    images = [block[0, :rows] if block is beside else block[:rows] for block in blocks]
    images = jnp.concatenate(images + digits)
    texts = [block[1, :rows] if block is beside else block[rows:] for block in blocks]
    texts = jnp.concatenate(texts)
    scalars = jnp.concatenate([sharpness_factor, score_shift_term])[None]
    tied = lax.optimization_barrier((texts, images, scalars, quarter))
    texts, images, scalars, quarter = tied
    near = across(quarter, Y)
    texts = jnp.concatenate([texts, across(texts, TEXT_ORDER[2])])
    count = 4 * rows
    beside = across(images, IMAGE_ORDER[2])
    digits = [images[count : count + 4], beside[count : count + 4]]
    images = jnp.concatenate([images[:count], beside[:count]] + digits)
    texts, images = lax.optimization_barrier((texts, images))
    texts = [texts, across(texts, CORE), across(texts, TEXT_ORDER[4])]
    images = [images, across(images, IMAGE_ORDER[3]), across(images, CORE)]
    near, texts[1] = lax.optimization_barrier((near, texts[1]))
    far = across(near, CORE)
    zt, projected, turned, matrix = pl.pallas_call(
        early_kernel,
        out_shape=(
            jax.ShapeDtypeStruct((total // 2, width), bf16),
            jax.ShapeDtypeStruct((total // 2, width), f32),
            jax.ShapeDtypeStruct((depth, 256), bf16),
            jax.ShapeDtypeStruct((2 * depth, width), bf16),
        ),
        in_specs=[anywhere] * 3 + [vmem] * 2,
        out_specs=(vmem,) * 4,
        scratch_shapes=[pltpu.VMEM((total // 2, width), bf16), pltpu.SemaphoreType.DMA((3,))],
        compiler_params=params,
        name="early_texts",
    )(caption_mapping_matrix, near, far, *texts[:2])
    texts.append(across(texts[2], CORE))
    images.append(across(images[1], CORE))
    return pl.pallas_call(
        batch_kernel,
        out_shape=(
            jax.ShapeDtypeStruct((rows, width), f32),
            jax.ShapeDtypeStruct((rows, width), f32),
            jax.ShapeDtypeStruct((depth, width), f32),
        ),
        in_specs=[vmem] * 14,
        out_specs=(vmem, vmem, anywhere),
        scratch_shapes=[
            pltpu.VMEM((total, width), bf16),
            pltpu.VMEM((total, width), bf16),
            pltpu.VMEM((total, width), bf16),
            pltpu.VMEM((total, width), f32),
            pltpu.VMEM((total, total), bf16),
            pltpu.VMEM((total, width), f32),
            pltpu.VMEM((depth, total), bf16),
            pltpu.VMEM((total, width), bf16),
            pltpu.SemaphoreType.DMA((8,)),
        ],
        compiler_params=params,
        name="batch",
    )(
        scalars,
        picture_mean_embeddings,
        zt,
        projected,
        turned,
        matrix,
        *texts,
        *images,
    )


def solution(mesh):
    gathered = dict(mesh.shape) == {"dp": 16, "fsdp": 2}
    per_device = gathered_plan if gathered else ring_plan
    return jax.shard_map(
        per_device,
        mesh=mesh,
        in_specs=(
            P(("dp", "fsdp"), None),
            P(("dp", "fsdp"), None),
            P("fsdp", None),
            P("dp"),
            P(),
            P(),
        ),
        out_specs=(P(("dp", "fsdp"), None), P(("dp", "fsdp"), None), P("fsdp", None)),
        check_vma=False,
    )
```

```python
import functools

import jax
import jax.numpy as jnp
from jax import lax
from jax.experimental import pallas as pl
from jax.experimental.pallas import tpu as pltpu
from jax.sharding import PartitionSpec as P

epsilon = 1e-06


def passed_along(block, axis, distance):
    devices = range(lax.axis_size(axis))
    route = [((i - distance) % len(devices), i) for i in devices]
    return lax.ppermute(block, axis, route)


def normalize(values):
    norms = jnp.sqrt(jnp.sum(values * values, axis=1, keepdims=True) + epsilon)
    return (values / norms, norms)


def unproject(grad_unit, unit, norms):
    return (grad_unit - unit * jnp.sum(unit * grad_unit, axis=1, keepdims=True)) / norms


def ring_plan(
    picture_mean_embeddings,
    caption_tower_summary,
    caption_mapping_matrix,
    picture_match_index,
    sharpness_factor,
    score_shift_term,
):
    rows = caption_tower_summary.shape[0]
    width = caption_mapping_matrix.shape[1]
    cycle_size = lax.axis_size("dp")
    column_count = lax.axis_size("fsdp")
    cycle_index = lax.axis_index("dp")
    column_index = lax.axis_index("fsdp")
    score_multiplier = sharpness_factor[0]
    offset = score_shift_term[0]
    feature_column_set = lax.all_to_all(
        caption_tower_summary, "fsdp", split_axis=1, concat_axis=0, tiled=True
    )
    projected = jnp.dot(
        caption_tower_summary,
        lax.all_gather(caption_mapping_matrix, "fsdp", axis=0, tiled=True),
        preferred_element_type=jnp.float32,
    )
    unit_text, text_norm = normalize(projected)
    text_unit = unit_text.astype(jnp.bfloat16)
    unit_image, image_norm = normalize(picture_mean_embeddings.astype(jnp.float32))
    image_unit = lax.all_gather(unit_image.astype(jnp.bfloat16), "fsdp", axis=0, tiled=True)
    group = image_unit.shape[0]

    def tile(block, text_rows):
        scores = lax.dot_general(
            image_unit, block, (((1,), (1,)), ((), ())), preferred_element_type=jnp.float32
        )
        logits = score_multiplier * scores + offset
        sign = jnp.where(picture_match_index[:, None] == text_rows[None, :], 1.0, -1.0).astype(
            jnp.float32
        )
        weights = (score_multiplier * -sign * jax.nn.sigmoid(-sign * logits)).astype(jnp.bfloat16)
        image_part = jnp.dot(weights, block, preferred_element_type=jnp.float32)
        text_part = lax.dot_general(
            weights, image_unit, (((0,), (0,)), ((), ())), preferred_element_type=jnp.float32
        )
        return (image_part, text_part)

    def rows_of(owner, count):
        return (owner * column_count + column_index) * rows + jnp.arange(count, dtype=jnp.int32)

    image_start = jnp.zeros((group, width), jnp.float32)

    def advance(count, state):
        block, carried, image_sum = state
        owner = (cycle_index - count) % cycle_size
        image_part, text_part = tile(block, rows_of(owner, rows))
        block = passed_along(block, "dp", 1)
        carried = passed_along(carried + text_part, "dp", 1)
        return (block, carried, image_sum + image_part)

    state = (text_unit, jnp.zeros((rows, width), jnp.float32), image_start)
    block, grad_zt, image_sum = lax.fori_loop(0, cycle_size, advance, state)
    grad_zi = lax.psum_scatter(image_sum, "fsdp", scatter_dimension=0, tiled=True)
    grad_image = unproject(grad_zi, unit_image, image_norm)
    grad_proj = unproject(grad_zt, unit_text, text_norm).astype(jnp.bfloat16)
    grad_group = lax.all_gather(grad_proj, "fsdp", axis=0, tiled=True)
    head_part = lax.dot_general(
        feature_column_set, grad_group, (((0,), (0,)), ((), ())), preferred_element_type=jnp.float32
    )
    head_grad = lax.psum(head_part, "dp")
    grad_text = lax.dot_general(
        grad_proj,
        lax.all_gather(caption_mapping_matrix, "fsdp", axis=0, tiled=True),
        (((1,), (1,)), ((), ())),
        preferred_element_type=jnp.float32,
    )
    return (grad_image, grad_text, head_grad)


def across(block, bits):
    count = lax.axis_size("dp") * lax.axis_size("fsdp")
    return lax.ppermute(block, ("dp", "fsdp"), [(i, i ^ bits) for i in range(count)])


Y, CORE, X, Z1, Z2 = 1, 2, 4, 8, 16
IMAGE_ORDER = (Y, Z2, X, Z1, CORE)
TEXT_ORDER = (Y, Z2, Z1, CORE, X)
NT = (((1,), (1,)), ((), ()))
TN = (((0,), (0,)), ((), ()))


def dot(a, b, dims=(((1,), (0,)), ((), ()))):
    return lax.dot_general(a, b, dims, preferred_element_type=jnp.float32)


def cuts(size, step):
    return [slice(k, min(k + step, size)) for k in range(0, size, step)]


def owners(order, shape, axis, rows, place):
    row = lax.broadcasted_iota(jnp.int32, shape, axis)
    block = sum((row >= k * rows).astype(jnp.int32) for k in range(1, shape[axis] // rows))
    owner = jnp.zeros_like(row)
    for k, bits in enumerate(order):
        owner += ((block >> k) & 1) * bits
    return owner ^ place, row - block * rows


def weigh(scores, paired, scalars):
    sharpness, shift = scalars[:, 0:1], scalars[:, 1:2]
    logits = sharpness * scores + shift
    share = 1.0 / (1.0 + jnp.exp(jnp.where(paired, logits, -logits)))
    return (jnp.where(paired, -sharpness, sharpness) * share).astype(jnp.bfloat16)


def own_kernel(image, text, match, own, plain, digits):
    rows, width = image.shape[0], match.shape[1]
    digits[...] = jnp.zeros(digits.shape, jnp.float32)
    digits[0:1, :width] = (match[...] >> 5).astype(jnp.float32)
    digits[1:2, :width] = (match[...] & 31).astype(jnp.float32)
    spare = digits[: own.shape[1] - rows]
    unit_image, _ = normalize(image[...].astype(jnp.float32))
    own[0] = jnp.concatenate([unit_image, spare]).astype(jnp.bfloat16)
    text_rows = text[...].astype(jnp.float32)
    own[1] = jnp.concatenate([text_rows, jnp.zeros_like(spare)]).astype(jnp.bfloat16)
    plain[...] = jnp.concatenate([unit_image, text_rows]).astype(jnp.bfloat16)


def pair_indices(rows, total, pieces, side):
    digits = jnp.concatenate([piece[...].astype(jnp.float32)[-8:, :128] for piece in pieces])
    lane = lax.broadcasted_iota(jnp.int32, (1, total), 1)
    group = sum((lane >= k).astype(jnp.int32) for k in range(2 * rows, total, 2 * rows))
    row = lane - group * 2 * rows
    row = jnp.where(side == 0, row, jnp.where(row < rows, row + rows, row - rows))
    chosen = lax.broadcasted_iota(jnp.int32, (128, total), 0) == row
    spread = dot(digits.astype(jnp.bfloat16), chosen.astype(jnp.float32).astype(jnp.bfloat16))
    number = lax.broadcasted_iota(jnp.int32, spread.shape, 0)
    scale = jnp.where(number == 2 * group, 32.0, jnp.where(number == 2 * group + 1, 1.0, 0.0))
    return jnp.sum(scale * spread, axis=0, keepdims=True).astype(jnp.int32)


def project(text, matrix, projected, zt):
    for cut in cuts(matrix.shape[1], 256):
        projected[:, cut] = dot(text[...], matrix[:, cut])
    for block in cuts(text.shape[0], 160):
        value = projected[block]
        inverse = lax.rsqrt(jnp.sum(value * value, axis=1, keepdims=True) + epsilon)
        zt[block] = (value * inverse).astype(jnp.bfloat16)


def early_kernel(matrix_own, matrix_near, matrix_far, *rest):
    texts, rest = rest[:2], rest[2:]
    zt, projected, turned, matrix, text, sems = rest
    depth, near = matrix_own.shape[0], matrix_near.shape[0]
    core, side = lax.rem(lax.axis_index("dp"), 2), lax.axis_index("fsdp")

    other = (1 - side) * depth
    places = (side * depth, other + core * near, other + (1 - core) * near)
    copies = []
    for k, (source, start) in enumerate(zip((matrix_own, matrix_near, matrix_far), places)):
        start = pl.multiple_of(start, 32)
        target = matrix.at[pl.ds(start, source.shape[0])]
        copies.append(pltpu.make_async_copy(source, target, sems.at[k]))
        copies[-1].start()
    count = texts[0].shape[0]
    for k, source in enumerate(texts):
        text[pl.ds(k * count, count)] = source[...]
    for s in (0, 1):

        @pl.when(side == s)
        def _():
            turned[...] = jnp.transpose(text[: turned.shape[1], s * depth : (s + 1) * depth])

    for copy in copies:
        copy.wait()
    project(text, matrix, projected, zt)


def batch_kernel(scalars, image, zt_early, projected_early, *rest):
    (turned_early, matrix), texts, images, rest = rest[:2], rest[2:6], rest[6:10], rest[10:]
    (grad_image, grad_text, head_grad), rest = rest[:3], rest[3:]
    zi, text, zt, projected, weights, grad, turned, proj, sems = rest
    rows = image.shape[0]
    total, width = zi.shape
    half = total // 2
    depth = head_grad.shape[0]
    group, side = lax.axis_index("dp"), lax.axis_index("fsdp")

    count = total // 4
    for sources, target, skip in ((texts, text, 1), (images, zi, 0)):
        for k, source in enumerate(sources[skip:], skip):
            target[pl.ds(k * count, count)] = source[:count]
    match = pair_indices(rows, total, images, side)
    late = pl.ds(half, half)
    project(text.at[late], matrix, projected.at[late], zt.at[late])
    zt[:half] = zt_early[...]
    first = turned_early.shape[1]
    turned[:, :first] = turned_early[...]
    for s in (0, 1):

        @pl.when(side == s)
        def _():
            turned[:, first:] = jnp.transpose(text[first:, s * depth : (s + 1) * depth])

    owner, row = owners(TEXT_ORDER, (total, 1), 0, rows, group * 2 + side)
    ids = owner * rows + row
    for cut in cuts(total, 256):
        scores = dot(zt[...], zi[cut], NT)
        weights[:, cut] = weigh(scores, ids == match[:, cut], scalars)
    for cut in cuts(width, 256):
        grad[:, cut] = dot(weights[...], zi[:, cut])
    for block in cuts(total, 160):
        value = projected_early[block] if block.stop <= half else projected[block]
        slope = grad[block]
        squares = jnp.sum(value * value, axis=1, keepdims=True) + epsilon
        inner = jnp.sum(value * slope, axis=1, keepdims=True)
        proj[block] = ((slope - value * (inner / squares)) * lax.rsqrt(squares)).astype(
            jnp.bfloat16
        )
    copies = []
    head = grad
    for k, cut in enumerate(cuts(width, 256)):
        head[:depth, cut] = dot(turned[...], proj[:, cut])
        copies.append(
            pltpu.make_async_copy(head.at[:depth, cut], head_grad.at[:, cut], sems.at[k])
        )
        copies[-1].start()
    grad_text[...] = dot(proj[:48], matrix[...], NT)[:rows]
    grad_zi = dot(weights[:, :128], zt[...], TN)[:rows]
    unit_image, image_norm = normalize(image[...].astype(jnp.float32))
    grad_image[...] = unproject(grad_zi, unit_image, image_norm)
    for copy in copies:
        copy.wait()


def gathered_plan(
    picture_mean_embeddings,
    caption_tower_summary,
    caption_mapping_matrix,
    picture_match_index,
    sharpness_factor,
    score_shift_term,
):
    rows, width = caption_tower_summary.shape
    depth = caption_mapping_matrix.shape[0]
    half = depth // 2
    total = rows * 32
    vmem = pl.BlockSpec(memory_space=pltpu.VMEM)
    anywhere = pl.BlockSpec(memory_space=pl.ANY)
    f32, bf16 = jnp.float32, jnp.bfloat16
    params = pltpu.CompilerParams(vmem_limit_bytes=24 * 2**20)

    own, plain = pl.pallas_call(
        own_kernel,
        out_shape=(
            jax.ShapeDtypeStruct((2, rows + 4, width), bf16),
            jax.ShapeDtypeStruct((2 * rows, width), bf16),
        ),
        in_specs=[vmem] * 3,
        out_specs=(vmem, vmem),
        scratch_shapes=[pltpu.VMEM((8, width), f32)],
        name="own_block",
    )(
        picture_mean_embeddings,
        caption_tower_summary,
        picture_match_index[None, :],
    )
    first = IMAGE_ORDER[1]
    beside = across(own, first)
    blocks = [plain, across(plain, Y), beside, across(plain, first | Y)]
    matrix, plain = lax.optimization_barrier((caption_mapping_matrix, plain))
    core = lax.axis_index("dp") % 2
    quarter = lax.dynamic_slice_in_dim(matrix, core * half, half, 0)
    digits = [block[0, rows : rows + 2] for block in (own, beside)]
    digits += [jnp.zeros((4, width), bf16)]
    images = [block[0, :rows] if block is beside else block[:rows] for block in blocks]
    images = jnp.concatenate(images + digits)
    texts = [block[1, :rows] if block is beside else block[rows:] for block in blocks]
    texts = jnp.concatenate(texts)
    scalars = jnp.concatenate([sharpness_factor, score_shift_term])[None]
    tied = lax.optimization_barrier((texts, images, scalars, quarter))
    texts, images, scalars, quarter = tied
    near = across(quarter, Y)
    texts = jnp.concatenate([texts, across(texts, TEXT_ORDER[2])])
    count = 4 * rows
    beside = across(images, IMAGE_ORDER[2])
    digits = [images[count : count + 4], beside[count : count + 4]]
    images = jnp.concatenate([images[:count], beside[:count]] + digits)
    texts, images = lax.optimization_barrier((texts, images))
    texts = [texts, across(texts, CORE), across(texts, TEXT_ORDER[4])]
    images = [images, across(images, IMAGE_ORDER[3]), across(images, CORE)]
    near, texts[1] = lax.optimization_barrier((near, texts[1]))
    far = across(near, CORE)
    zt, projected, turned, matrix = pl.pallas_call(
        early_kernel,
        out_shape=(
            jax.ShapeDtypeStruct((total // 2, width), bf16),
            jax.ShapeDtypeStruct((total // 2, width), f32),
            jax.ShapeDtypeStruct((depth, 256), bf16),
            jax.ShapeDtypeStruct((2 * depth, width), bf16),
        ),
        in_specs=[anywhere] * 3 + [vmem] * 2,
        out_specs=(vmem,) * 4,
        scratch_shapes=[pltpu.VMEM((total // 2, width), bf16), pltpu.SemaphoreType.DMA((3,))],
        compiler_params=params,
        name="early_texts",
    )(caption_mapping_matrix, near, far, *texts[:2])
    texts.append(across(texts[2], CORE))
    images.append(across(images[1], CORE))
    return pl.pallas_call(
        batch_kernel,
        out_shape=(
            jax.ShapeDtypeStruct((rows, width), f32),
            jax.ShapeDtypeStruct((rows, width), f32),
            jax.ShapeDtypeStruct((depth, width), f32),
        ),
        in_specs=[vmem] * 14,
        out_specs=(vmem, vmem, anywhere),
        scratch_shapes=[
            pltpu.VMEM((total, width), bf16),
            pltpu.VMEM((total, width), bf16),
            pltpu.VMEM((total, width), bf16),
            pltpu.VMEM((total, width), f32),
            pltpu.VMEM((total, total), bf16),
            pltpu.VMEM((total, width), f32),
            pltpu.VMEM((depth, total), bf16),
            pltpu.VMEM((total, width), bf16),
            pltpu.SemaphoreType.DMA((8,)),
        ],
        compiler_params=params,
        name="batch",
    )(
        scalars,
        picture_mean_embeddings,
        zt,
        projected,
        turned,
        matrix,
        *texts,
        *images,
    )


def solution(mesh):
    gathered = dict(mesh.shape) == {"dp": 16, "fsdp": 2}
    per_device = gathered_plan if gathered else ring_plan
    return jax.shard_map(
        per_device,
        mesh=mesh,
        in_specs=(
            P(("dp", "fsdp"), None),
            P(("dp", "fsdp"), None),
            P("fsdp", None),
            P("dp"),
            P(),
            P(),
        ),
        out_specs=(P(("dp", "fsdp"), None), P(("dp", "fsdp"), None), P("fsdp", None)),
        check_vma=False,
    )
```
